32 devices in a mesh: ctx: 8 (over z, x), wa: 4 (over y, core).
Axes of the slice: x: 2, y: 2, z: 4, core: 2. Of those that a mesh axis runs over, the one named last changes fastest.
Arguments:
- tokens: bfloat16 [4, 1024, 1536], P('wa', 'ctx'), may hold values from -6 to 6
- teacher: float32 [4, 1024, 1536], P('wa', 'ctx'), may hold values from -6 to 6
- lengths: int32 [4], replicated, may hold values from 897 to 1024, as said below
- routes: int32 [4, 1024, 6], P('wa', 'ctx'), may hold values from 0 to 15, all different within a row; in each aligned block of 128 rows (0 to 127, 128 to 255, ..., all dimensions but the last counted through in order) at most 96 rows name the same one
- query_weight: bfloat16 [1536, 1536], P('wa'), may hold values from -0.15625 to 0.15625
- key_projection_matrix: bfloat16 [1536, 512], P('wa'), may hold values from -0.15625 to 0.15625
- value_projection_matrix: bfloat16 [1536, 512], P('wa'), may hold values from -0.15625 to 0.15625
- output_weight: bfloat16 [1536, 1536], P('wa'), may hold values from -0.4375 to 0.4375
- attn_gain: bfloat16 [1536], P('wa'), may hold values from 0.5 to 1.5
- moe_gain: bfloat16 [1536], P('wa'), may hold values from 0.5 to 1.5
- router_weight: bfloat16 [1536, 16], P('wa'), may hold values from -0.078125 to 0.078125
- shared_gate: bfloat16 [1536, 1024], P('wa'), may hold values from -0.15625 to 0.15625
- shared_up: bfloat16 [1536, 1024], P('wa'), may hold values from -0.15625 to 0.15625
- shared_down: bfloat16 [1536, 1024], P('wa'), may hold values from -0.1875 to 0.1875
- expert_gate: bfloat16 [16, 1536, 512], P('wa'), may hold values from -0.15625 to 0.15625
- expert_up: bfloat16 [16, 1536, 512], P('wa'), may hold values from -0.15625 to 0.15625
- expert_down: bfloat16 [16, 1536, 512], P('wa'), may hold values from -0.25 to 0.25
Outputs:
- block_out: bfloat16 [4, 1024, 1536], P('wa', 'ctx')
- grad_tokens: float32 [4, 1024, 1536], P('wa', 'ctx')
- grad_query: float32 [1536, 1536], P(('ctx', 'wa'))
- grad_key: float32 [1536, 512], P(('ctx', 'wa'))
- grad_value: float32 [1536, 512], P(('ctx', 'wa'))
- grad_output: float32 [1536, 1536], P(('ctx', 'wa'))
- grad_attn_gain: float32 [1536], P(('ctx', 'wa'))
- grad_moe_gain: float32 [1536], P(('ctx', 'wa'))
- grad_router: float32 [1536, 16], P(('ctx', 'wa'))
- grad_shared_gate: float32 [1536, 1024], P(('ctx', 'wa'))
- grad_shared_up: float32 [1536, 1024], P(('ctx', 'wa'))
- grad_shared_down: float32 [1536, 1024], P(('ctx', 'wa'))
- grad_expert_gate: float32 [16, 1536, 512], P('wa', 'ctx')
- grad_expert_up: float32 [16, 1536, 512], P('wa', 'ctx')
- grad_expert_down: float32 [16, 1536, 512], P('wa', 'ctx')
- loss: float32 [], replicated
The draws below stay inside these ranges and needn't reach their ends.
Inputs may be any that keep to these rules, and one draw needn't show every extreme that they name: `lengths`: every sequence reaches into the last block of 128 positions; one is exactly 1024 long. `routes`: a position names 6 different experts; within the 128 positions of one device no expert is named more than 96 times, a bound that some block reaches.
All inputs are finite; a program needn't handle non-finite values.
Results may differ from the reference program's by a relative error of at most 0.029.
Values may be sent and summed in bfloat16 or wider, within the bound.
No kernel may reach another device: no remote copies, remote signals or barrier semaphores. Data moves between devices by JAX's collectives and lax.ppermute only.
A program may use at most 320 MiB of HBM per device.

```python
import math
import jax
import jax.numpy as jnp
import numpy as np
from jax import lax

MODEL_WIDTH = 1536
QUERY_HEADS = 12
KEY_VALUE_HEADS = 4
HEAD_SIZE = 128
FFE = 512
FFS = 1024
TOP = 6
TOK_DEV = 128
PADDED_LENGTH = 1024
SEQS = 4
TOKENS = 4096
EXPERTS = 16
CAP = 96


def draw_lengths(key, part):
    key = jax.random.fold_in(key, 11)
    first_key, second_key = jax.random.split(key)
    drawn = jax.random.randint(first_key, (SEQS,), PADDED_LENGTH - TOK_DEV + 1, PADDED_LENGTH + 1)
    longest = jax.random.randint(second_key, (), 0, SEQS)
    return jnp.where(jnp.arange(SEQS) == longest, PADDED_LENGTH, drawn).astype(jnp.int32)


def level_of(own_key, dims, cuts, least, largest):
    factor_of, own = 1.0, jax.random.fold_in(own_key, 6)
    for axis_at, parts in cuts:
        steps = jnp.exp(jax.random.uniform(jax.random.fold_in(own, axis_at), (parts,), jnp.float32, least / len(cuts), largest / len(cuts)))
        factor_of = factor_of * jnp.repeat(steps, dims[axis_at] // parts).reshape([-1 if axis == axis_at else 1 for axis in range(len(dims))])
    return factor_of


def assign_block(rng, own, number, rows, amount, top, bound, skew):
    ranking = jax.random.permutation(rng, amount)
    crowded, common = portions_of(amount, rows * top, bound, skew, True), portions_of(amount, rows * top, bound, skew, False)
    places = jnp.arange(amount)

    def named(tallies, offset_by):
        used = int((tallies > 0).sum())
        fixed = max(1, used // 4)
        moved = fixed + (places - fixed + offset_by * (used - fixed)) % max(1, amount - fixed)
        return jnp.zeros((amount,), jnp.int32).at[ranking[jnp.where(places < fixed, places, moved)]].set(jnp.asarray(tallies, jnp.int32))

    tallies = jnp.where(number % 4 == 0, named(crowded, number // 4), named(common, number - number // 4 - 1))
    mixed = jax.random.permutation(jax.random.fold_in(own, 3), amount)
    giver, receiver = mixed[0:amount // 2 * 2:2], mixed[1:amount // 2 * 2:2]
    margin = jnp.minimum(tallies[giver] - 1, bound - tallies[receiver]) // 2
    margin = jnp.where((giver == ranking[0]) | (receiver == ranking[0]) | (tallies[receiver] == 0), 0, jnp.maximum(margin, 0))
    moved = jax.random.randint(jax.random.fold_in(own, 4), (amount // 2,), 0, 1 << 20) % (margin + 1)
    tallies = tallies.at[giver].add(-moved).at[receiver].add(moved)
    labels = jnp.searchsorted(jnp.cumsum(tallies), jnp.arange(rows * top), side="right").astype(jnp.int32)
    table = labels.reshape(top, rows).T
    table = table[jax.random.permutation(jax.random.fold_in(own, 1), rows)]
    offset_by = jax.random.randint(jax.random.fold_in(own, 2), (rows, 1), 0, top)
    return jnp.take_along_axis(table, (jnp.arange(top)[None, :] + offset_by) % top, axis=1)


def portions_of(number_of, total, limit, slope, full):
    portions = [(1 << 20) // math.isqrt(standing ** slope) + 1 for standing in range(1, number_of + 1)]
    largest = limit if full else min(limit, max(-(-total // number_of), total * portions[0] // sum(portions)))
    least = 1 if total - largest >= number_of - 1 else 0
    given, spare = [largest] + [least] * (number_of - 1), total - largest - least * (number_of - 1)
    while spare > 0:
        movable = [i for i in range(1, number_of) if given[i] < largest] or [i for i in range(1, number_of) if given[i] < limit]
        pool, remaining = sum([portions[i] for i in movable]), spare
        for i in movable:
            extra = min(limit - given[i], max(1, remaining * portions[i] // pool), spare)
            given[i] = given[i] + extra
            spare = spare - extra
    return np.array(given)


def scatter_about(rng, dims, deviation, limit, pieces=(), held_as=jnp.bfloat16):
    gain = level_of(rng, dims, pieces, -0.22, 0.18) if pieces else 1.0
    entries = jax.random.normal(rng, dims, jnp.float32) * deviation * gain
    return jnp.minimum(jnp.maximum(entries, -limit), limit).astype(held_as)


def setup_inputs(seed: int = 0) -> dict:
    splits = jax.random.split(jax.random.key(seed), 18)
    tokens = scatter_about(splits[0], (SEQS, PADDED_LENGTH, MODEL_WIDTH), 1.0, 6.0, ((0, 4), (1, 8)))
    teacher = scatter_about(splits[1], (SEQS, PADDED_LENGTH, MODEL_WIDTH), 1.0, 6.0, ((0, 4), (1, 8)), jnp.float32)
    lengths = draw_lengths(jax.random.fold_in(splits[17], 71), 0)
    routes_keys = jax.random.split(jax.random.fold_in(splits[3], 1), SEQS * PADDED_LENGTH // TOK_DEV)
    routes_turns = jax.random.permutation(jax.random.fold_in(splits[3], 3), SEQS * PADDED_LENGTH // TOK_DEV)
    routes = jax.vmap(lambda own, number: assign_block(jax.random.fold_in(splits[3], 2), own, number, TOK_DEV, EXPERTS, TOP, CAP, 1))(routes_keys, routes_turns).reshape((SEQS, PADDED_LENGTH, TOP))
    query_weight = scatter_about(splits[4], (MODEL_WIDTH, QUERY_HEADS * HEAD_SIZE), MODEL_WIDTH ** -0.5, 0.15625, ((0, 4),))
    key_projection_matrix = scatter_about(splits[5], (MODEL_WIDTH, KEY_VALUE_HEADS * HEAD_SIZE), MODEL_WIDTH ** -0.5, 0.15625, ((0, 4),))
    value_projection_matrix = scatter_about(splits[6], (MODEL_WIDTH, KEY_VALUE_HEADS * HEAD_SIZE), MODEL_WIDTH ** -0.5, 0.15625, ((0, 4),))
    output_weight = scatter_about(splits[7], (MODEL_WIDTH, QUERY_HEADS * HEAD_SIZE), (QUERY_HEADS * HEAD_SIZE * 128 // PADDED_LENGTH) ** -0.5, 0.4375, ((0, 4),))
    attn_gain = jnp.clip(1.0 + 0.1 * jax.random.normal(splits[8], (MODEL_WIDTH,), jnp.float32), 0.5, 1.5).astype(jnp.bfloat16)
    moe_gain = jnp.clip(1.0 + 0.1 * jax.random.normal(splits[9], (MODEL_WIDTH,), jnp.float32), 0.5, 1.5).astype(jnp.bfloat16)
    router_weight = scatter_about(splits[10], (MODEL_WIDTH, EXPERTS), (4 * MODEL_WIDTH) ** -0.5, 0.078125, ((0, 4),))
    shared_gate = scatter_about(splits[11], (MODEL_WIDTH, FFS), MODEL_WIDTH ** -0.5, 0.15625, ((0, 4),))
    shared_up = scatter_about(splits[12], (MODEL_WIDTH, FFS), MODEL_WIDTH ** -0.5, 0.15625, ((0, 4),))
    shared_down = scatter_about(splits[13], (MODEL_WIDTH, FFS), FFS ** -0.5, 0.1875, ((0, 4),))
    expert_gate = scatter_about(splits[14], (EXPERTS, MODEL_WIDTH, FFE), MODEL_WIDTH ** -0.5, 0.15625, ((0, 4),))
    expert_up = scatter_about(splits[15], (EXPERTS, MODEL_WIDTH, FFE), MODEL_WIDTH ** -0.5, 0.15625, ((0, 4),))
    expert_down = scatter_about(splits[16], (EXPERTS, MODEL_WIDTH, FFE), FFE ** -0.5, 0.25, ((0, 4),))
    return dict(tokens=tokens, teacher=teacher, lengths=lengths, routes=routes, query_weight=query_weight, key_projection_matrix=key_projection_matrix, value_projection_matrix=value_projection_matrix, output_weight=output_weight, attn_gain=attn_gain, moe_gain=moe_gain, router_weight=router_weight, shared_gate=shared_gate, shared_up=shared_up, shared_down=shared_down, expert_gate=expert_gate, expert_up=expert_up, expert_down=expert_down)


@jax.custom_vjp
def low(v):
    return lax.optimization_barrier(v.astype(jnp.bfloat16)).astype(jnp.float32)

@jax.custom_vjp
def low_back(v):
    return v

def low_keep(v):
    return (low(v), None)

def low_pass(kept, grad):
    return (grad,)

def back_keep(v):
    return (v, None)

def back_low(kept, grad):
    return (low(grad),)
low.defvjp(low_keep, low_pass)
low_back.defvjp(back_keep, back_low)
epsilon = 1e-06
highest = lax.Precision.HIGHEST

def matmul(left, right):
    return jnp.dot(left, right, precision=highest)

def rms_scale(value_rows):
    return lax.rsqrt(lax.optimization_barrier(jnp.mean(value_rows * value_rows, axis=-1, keepdims=True)) + epsilon)

def silu(value_rows):
    return value_rows * jax.nn.sigmoid(value_rows)

def attention(query_rows, key_rows, value_rows, length):
    query_group_width = QUERY_HEADS // KEY_VALUE_HEADS
    query_head_rows = query_rows.reshape(PADDED_LENGTH, KEY_VALUE_HEADS, query_group_width, HEAD_SIZE)
    key_head_rows = key_rows.reshape(PADDED_LENGTH, KEY_VALUE_HEADS, HEAD_SIZE)
    value_head_rows = value_rows.reshape(PADDED_LENGTH, KEY_VALUE_HEADS, HEAD_SIZE)
    block_rows = min(PADDED_LENGTH, 512)
    key_pos = jnp.arange(PADDED_LENGTH)

    def one_block(first_row):
        query_block = lax.dynamic_slice_in_dim(query_head_rows, first_row, block_rows, 0)
        scores = jnp.einsum('tkgd,nkd->kgtn', query_block, key_head_rows, precision=highest) * HEAD_SIZE ** (-0.5)
        scores = low_back(scores)
        query_pos = first_row + jnp.arange(block_rows)
        allowed = (key_pos[None, :] <= query_pos[:, None]) & (key_pos[None, :] < length)
        scores = jnp.where(allowed, scores, -1e+30)
        probs = low(jax.nn.softmax(scores, axis=-1))
        mixed = jnp.einsum('kgtn,nkd->tkgd', probs, value_head_rows, precision=highest)
        return mixed.reshape(block_rows, QUERY_HEADS * HEAD_SIZE)
    starts = jnp.arange(0, PADDED_LENGTH, block_rows)
    blocks = lax.map(jax.checkpoint(one_block), starts)
    return blocks.reshape(PADDED_LENGTH, QUERY_HEADS * HEAD_SIZE)

def reference(tokens, teacher, lengths, routes, query_weight, key_projection_matrix, value_projection_matrix, output_weight, attn_gain, moe_gain, router_weight, shared_gate, shared_up, shared_down, expert_gate, expert_up, expert_down):
    blocks = TOKENS // TOK_DEV
    pairs = TOK_DEV * TOP
    route_ids = routes.reshape(blocks, pairs).astype(jnp.int32)
    hot_ids = (route_ids[:, :, None] == jnp.arange(EXPERTS)[None, None, :]).astype(jnp.int32)
    ranks = lax.optimization_barrier(jnp.sum((jnp.cumsum(hot_ids, axis=1) - hot_ids) * hot_ids, axis=-1))
    dest = route_ids * CAP + ranks
    pair_global = (jnp.arange(blocks)[:, None] * pairs + jnp.arange(pairs)[None, :]).astype(jnp.int32)
    block_rows = jnp.broadcast_to(jnp.arange(blocks)[:, None], (blocks, pairs))
    lookup_table = jnp.zeros((blocks, EXPERTS * CAP), jnp.int32).at[block_rows, dest].set(pair_global)
    valid_mask = jnp.zeros((blocks, EXPERTS * CAP), jnp.float32).at[block_rows, dest].set(1.0)
    lookup_table = jnp.transpose(lookup_table.reshape(blocks, EXPERTS, CAP), (1, 0, 2)).reshape(EXPERTS, blocks * CAP)
    valid_mask = jnp.transpose(valid_mask.reshape(blocks, EXPERTS, CAP), (1, 0, 2)).reshape(EXPERTS, blocks * CAP)
    location = (route_ids * (blocks * CAP) + block_rows * CAP + ranks).reshape(-1)
    route_hot = (routes.reshape(TOKENS, TOP)[:, :, None] == jnp.arange(EXPERTS)[None, None, :]).astype(jnp.float32)
    valid = (jnp.arange(PADDED_LENGTH)[None, :] < lengths[:, None]).astype(jnp.float32)
    count = jnp.sum(lengths).astype(jnp.float32)
    teacher_f = teacher.astype(jnp.float32)

    def compute_loss(input_rows, query_projection_weight, key_projection_weight, value_projection_weight, output_projection_weight, first_norm_scale, second_norm_scale, router_projection_weight, shared_gate_weight, shared_up_weight, shared_down_weight, expert_gate_weight, expert_up_weight, expert_down_weight):

        def per_sequence(carry, item):
            sequence, length = item
            attn_in = low(sequence * rms_scale(sequence) * first_norm_scale)
            query_rows = low(low_back(matmul(attn_in, query_projection_weight)))
            key_rows = low(low_back(matmul(attn_in, key_projection_weight)))
            value_rows = low(low_back(matmul(attn_in, value_projection_weight)))
            mixed = attention(query_rows, key_rows, value_rows, length)
            mixed = low(low_back(mixed))
            branch = low_back(matmul(mixed, output_projection_weight.T))
            return (carry, sequence + branch)
        _, resid = lax.scan(jax.checkpoint(per_sequence), jnp.zeros((), jnp.float32), (input_rows, lengths))
        resid = resid.reshape(TOKENS, MODEL_WIDTH)
        moe_in = low(resid * rms_scale(resid) * second_norm_scale)
        logits = matmul(moe_in, router_projection_weight)
        chosen = lax.optimization_barrier(jnp.sum(route_hot * logits[:, None, :], axis=-1))
        gates = jax.nn.softmax(chosen, axis=-1)
        pair_rows = low_back(jnp.repeat(moe_in, TOP, axis=0))

        def single_expert_apply(item):
            gate_w, up_w, down_w, rows_index, rows_live = item
            rows = pair_rows[rows_index] * rows_live[:, None]
            gate_pre = low_back(matmul(rows, gate_w))
            up_pre = low_back(matmul(rows, up_w))
            hidden = low(silu(gate_pre) * up_pre)
            return low(low_back(matmul(hidden, down_w.T)))
        expert_output_rows = lax.map(jax.checkpoint(single_expert_apply), (expert_gate_weight, expert_up_weight, expert_down_weight, lookup_table, valid_mask))
        pair_out = expert_output_rows.reshape(-1, MODEL_WIDTH)[location].reshape(TOKENS, TOP, MODEL_WIDTH)
        moe_out = lax.optimization_barrier(jnp.sum(gates[:, :, None] * pair_out, axis=1))
        shared_pre = low_back(matmul(moe_in, shared_gate_weight))
        shared_lin = low_back(matmul(moe_in, shared_up_weight))
        shared_hidden = low(silu(shared_pre) * shared_lin)
        shared_out = low_back(matmul(shared_hidden, shared_down_weight.T))
        result = (resid + moe_out + shared_out).reshape(SEQS, PADDED_LENGTH, MODEL_WIDTH)
        error = result - teacher_f
        loss = jnp.sum(valid[:, :, None] * error * error) / (2.0 * MODEL_WIDTH * count)
        return (loss, result)
    weights = tuple((item.astype(jnp.float32) for item in (query_weight, key_projection_matrix, value_projection_matrix, output_weight, attn_gain, moe_gain, router_weight, shared_gate, shared_up, shared_down, expert_gate, expert_up, expert_down)))
    loss, pullback, result = jax.vjp(compute_loss, tokens.astype(jnp.float32), *weights, has_aux=True)
    grads = pullback(jnp.ones_like(loss) * (MODEL_WIDTH * TOKENS))
    return (result.astype(jnp.bfloat16), grads[0], grads[1], grads[2], grads[3], grads[4], grads[5], grads[6], grads[7], grads[8], grads[9], grads[10], grads[11], grads[12], grads[13], loss)
```

```python
import jax
import jax.numpy as jnp
from jax import lax
from jax.sharding import PartitionSpec as P

QUERY_HEADS = 12
KEY_VALUE_HEADS = 4
HEAD_SIZE = 128
TOP = 6
GROUP = QUERY_HEADS // KEY_VALUE_HEADS

epsilon = 1e-06
masked = -1e30
bf16 = jnp.bfloat16
f32 = jnp.float32


def dot(a, b, dims):
    return lax.dot_general(a, b, ((dims[0], dims[1]), ((), ())), preferred_element_type=f32)


def mm(a, b):
    return dot(a, b, ((1,), (0,)))


def mm_nt(a, b):
    return dot(a, b, ((1,), (1,)))


def mm_tn(a, b):
    return dot(a, b, ((0,), (0,)))


def swap(value, axis, bit):
    size = lax.axis_size(axis)
    return lax.ppermute(value, axis, [(i, i ^ bit) for i in range(size)])


def perm4(parts, w):
    core, upper = w % 2 == 1, w // 2 == 1
    a, b, c, d = parts
    a, b, c, d = (
        jnp.where(core, b, a),
        jnp.where(core, a, b),
        jnp.where(core, d, c),
        jnp.where(core, c, d),
    )
    return [
        jnp.where(upper, c, a),
        jnp.where(upper, d, b),
        jnp.where(upper, a, c),
        jnp.where(upper, b, d),
    ]


def gather_wa(value):
    near = swap(value, "wa", 1)
    far = swap(value, "wa", 2)
    return [value, near, far, swap(far, "wa", 1)]


def silu_parts(rows):
    sigma = jax.nn.sigmoid(rows)
    return rows * sigma, sigma * (1.0 + rows * (1.0 - sigma))


def rms_factor(rows):
    return lax.rsqrt(jnp.mean(rows * rows, axis=-1, keepdims=True) + epsilon)


def norm_backward(rows, factor, gain, upstream):
    weighted = upstream * gain
    inner = jnp.mean(weighted * rows, axis=-1, keepdims=True)
    grad = factor * weighted - rows * (factor * factor * factor * inner)
    return grad, jnp.sum(upstream * rows * factor, axis=0)


def gather_keys(kv, c, n):
    rows = kv.shape[0]
    if n > 8:
        return lax.all_gather(kv, "ctx", axis=0, tiled=True), jnp.arange(n * rows)
    levels = [kv]
    for s in range(1, n // 2):
        levels.append(lax.ppermute(kv, "ctx", [(i, i + 2 * s) for i in range(n - 2 * s)]))
    blocks, pos = [], []
    for s, level in enumerate(levels):
        blocks += [level, swap(level, "ctx", 1)]
        start = (c - 2 * s) * rows
        pos += [start + jnp.arange(rows), (c - 2 * s + 1 - 2 * (c % 2)) * rows + jnp.arange(rows)]
    return jnp.concatenate(blocks), jnp.concatenate(pos)


def scatter_keys(grads, n):
    rows = grads.shape[0] // n
    if n > 8:
        return lax.psum_scatter(grads, "ctx", scatter_dimension=0, tiled=True).astype(f32)
    blocks = grads.reshape(n, rows, -1)
    total = None
    for s in reversed(range(n // 2)):
        level = blocks[2 * s].astype(f32) + swap(blocks[2 * s + 1], "ctx", 1).astype(f32)
        if s:
            level = lax.ppermute(
                level.astype(bf16), "ctx", [(i + 2 * s, i) for i in range(n - 2 * s)]
            ).astype(f32)
        total = level if total is None else total + level
    return total


def heads(rows, groups):
    return rows.reshape(rows.shape[0], KEY_VALUE_HEADS, groups, HEAD_SIZE)


def attention_scores(q, k, pos, qpos, length):
    scale = HEAD_SIZE**-0.5
    scores = jnp.einsum("tkgd,nkd->kgtn", q, k, preferred_element_type=f32) * scale
    allowed = (pos[None, :] >= 0) & (pos[None, :] <= qpos[:, None]) & (pos[None, :] < length)
    return scores, allowed


def chunked(kv, pos):
    size = 1024
    if kv.shape[0] <= size:
        return None
    return kv.reshape(-1, size, kv.shape[1]), pos.reshape(-1, size)


def attention_forward(q, kv, pos, qpos, length):
    rows = q.shape[0]
    pieces = chunked(kv, pos)
    width = KEY_VALUE_HEADS * HEAD_SIZE
    if pieces is None:
        k, v = heads(kv[:, :width], 1)[:, :, 0], heads(kv[:, width:], 1)[:, :, 0]
        scores, allowed = attention_scores(q, k, pos, qpos, length)
        scores = jnp.where(allowed, scores, masked)
        top = jnp.max(scores, axis=-1, keepdims=True)
        weights = jnp.exp(scores - top)
        probs = (weights / jnp.sum(weights, axis=-1, keepdims=True)).astype(bf16)
        attn = jnp.einsum("kgtn,nkd->tkgd", probs, v, preferred_element_type=f32)
        return attn, probs

    def step(carry, piece):
        top, total, accum = carry
        kv_now, pos_now = piece
        k, v = heads(kv_now[:, :width], 1)[:, :, 0], heads(kv_now[:, width:], 1)[:, :, 0]
        scores, allowed = attention_scores(q, k, pos_now, qpos, length)
        scores = jnp.where(allowed, scores, masked)
        new_top = jnp.maximum(top, jnp.max(scores, axis=-1, keepdims=True))
        weights = jnp.where(allowed, jnp.exp(scores - new_top), 0.0)
        shrink = jnp.exp(top - new_top)
        total = total * shrink + jnp.sum(weights, axis=-1, keepdims=True)
        update = jnp.einsum("kgtn,nkd->kgtd", weights.astype(bf16), v, preferred_element_type=f32)
        return (new_top, total, accum * shrink + update), None

    shape = (KEY_VALUE_HEADS, GROUP, rows)
    start = (
        jnp.full(shape + (1,), masked, f32),
        jnp.zeros(shape + (1,), f32),
        jnp.zeros(shape + (HEAD_SIZE,), f32),
    )
    (top, total, accum), _ = lax.scan(step, start, pieces)
    return jnp.transpose(accum / total, (2, 0, 1, 3)), top + jnp.log(total)


def attention_backward(q, kv, pos, qpos, length, kept, d_attn, delta):
    scale = HEAD_SIZE**-0.5
    width = KEY_VALUE_HEADS * HEAD_SIZE

    def terms(probs, k, v):
        d_probs = jnp.einsum("tkgd,nkd->kgtn", d_attn, v, preferred_element_type=f32)
        d_scores = (probs.astype(f32) * (d_probs - delta)).astype(bf16)
        d_q = jnp.einsum("kgtn,nkd->tkgd", d_scores, k, preferred_element_type=f32) * scale
        d_k = jnp.einsum("kgtn,tkgd->nkd", d_scores, q, preferred_element_type=f32) * scale
        d_v = jnp.einsum(
            "kgtn,tkgd->nkd", probs.astype(bf16), d_attn, preferred_element_type=f32
        )
        keys = k.shape[0]
        return d_q, jnp.concatenate(
            [d_k.reshape(keys, width), d_v.reshape(keys, width)], axis=1
        ).astype(bf16)

    pieces = chunked(kv, pos)
    if pieces is None:
        k, v = heads(kv[:, :width], 1)[:, :, 0], heads(kv[:, width:], 1)[:, :, 0]
        return terms(kept, k, v)

    def step(d_q, piece):
        kv_now, pos_now = piece
        k, v = heads(kv_now[:, :width], 1)[:, :, 0], heads(kv_now[:, width:], 1)[:, :, 0]
        scores, allowed = attention_scores(q, k, pos_now, qpos, length)
        probs = jnp.where(allowed, jnp.exp(scores - kept), 0.0)
        more, d_kv = terms(probs, k, v)
        return d_q + more, d_kv

    d_q, d_kv = lax.scan(step, jnp.zeros(q.shape, f32), pieces)
    return d_q, d_kv.reshape(kv.shape)


def experts_forward(rows, gates, weights):
    e_gate, e_up, e_down, s_gate, s_up, s_down = weights
    out = None
    gate_pres, up_pres, hiddens = [], [], []
    for e in range(e_gate.shape[0]):
        gate_pre, up_pre = mm(rows, e_gate[e]), mm(rows, e_up[e])
        act, _ = silu_parts(gate_pre)
        hidden = (act * up_pre * gates[e]).astype(bf16)
        term = mm_nt(hidden, e_down[e])
        out = term if out is None else out + term
        gate_pres.append(gate_pre.astype(bf16))
        up_pres.append(up_pre.astype(bf16))
        hiddens.append(hidden)
    gate_pre, up_pre = mm(rows, s_gate), mm(rows, s_up)
    act, _ = silu_parts(gate_pre)
    hidden = (act * up_pre).astype(bf16)
    out = out + mm_nt(hidden, s_down)
    kept = (
        jnp.stack(gate_pres),
        jnp.stack(up_pres),
        gate_pre.astype(bf16),
        up_pre.astype(bf16),
    )
    return out, kept, jnp.stack(hiddens), hidden


def experts_backward(grad, gates, weights, kept):
    e_gate, e_up, e_down, s_gate, s_up, s_down = weights
    e_gate_pre, e_up_pre, s_gate_pre, s_up_pre = kept
    d_gates, d_gate_pres, d_up_pres = [], [], []
    d_rows = None
    for e in range(e_gate.shape[0]):
        gate_pre, up_pre = e_gate_pre[e].astype(f32), e_up_pre[e].astype(f32)
        act, slope = silu_parts(gate_pre)
        d_hidden = mm(grad, e_down[e])
        d_gates.append(jnp.sum(d_hidden * act * up_pre, axis=-1))
        d_hidden = d_hidden * gates[e]
        d_gate_pre = (d_hidden * up_pre * slope).astype(bf16)
        d_up_pre = (d_hidden * act).astype(bf16)
        term = mm_nt(d_gate_pre, e_gate[e]) + mm_nt(d_up_pre, e_up[e])
        d_rows = term if d_rows is None else d_rows + term
        d_gate_pres.append(d_gate_pre)
        d_up_pres.append(d_up_pre)
    gate_pre, up_pre = s_gate_pre.astype(f32), s_up_pre.astype(f32)
    act, slope = silu_parts(gate_pre)
    d_hidden = mm(grad, s_down)
    s_d_gate = (d_hidden * up_pre * slope).astype(bf16)
    s_d_up = (d_hidden * act).astype(bf16)
    d_rows = d_rows + mm_nt(s_d_gate, s_gate) + mm_nt(s_d_up, s_up)
    return (
        d_rows,
        jnp.stack(d_gates),
        jnp.stack(d_gate_pres),
        jnp.stack(d_up_pres),
        s_d_gate,
        s_d_up,
    )


def sum_wa(parts):
    own = parts[0] + swap(parts[1].astype(bf16), "wa", 1).astype(f32)
    far = parts[2] + swap(parts[3].astype(bf16), "wa", 1).astype(f32)
    return own + swap(far.astype(bf16), "wa", 2).astype(f32)


def exchange_wa(pick):
    return [pick(0)] + [swap(pick(i), "wa", i) for i in (1, 2, 3)]


def line_scatter(parts, z, n):
    m = n // 2
    if m > 4:
        groups = [[2 * i + x for i in range(m)] for x in range(2)]
        flat = parts.reshape(m, -1)
        done = lax.psum_scatter(
            flat, "ctx", scatter_dimension=0, tiled=True, axis_index_groups=groups
        )
        return done.reshape(parts.shape[1:]).astype(f32)

    def part(index):
        return lax.dynamic_index_in_dim(parts, jnp.clip(index, 0, m - 1), 0, keepdims=False)

    up = down = None
    for t in range(m - 1):
        send_up, send_down = part(z + m - 1 - t), part(z - (m - 1) + t)
        if t:
            send_up = (send_up.astype(f32) + up.astype(f32)).astype(bf16)
            send_down = (send_down.astype(f32) + down.astype(f32)).astype(bf16)
        rising = [(2 * k + x, 2 * k + 2 + x) for k in range(m - 1) if k <= t for x in range(2)]
        falling = [(n - 1 - a, n - 1 - b) for a, b in rising]
        up = lax.ppermute(send_up, "ctx", rising)
        down = lax.ppermute(send_down, "ctx", falling)
    total = part(z).astype(f32)
    if m > 1:
        total = total + up.astype(f32) + down.astype(f32)
    return total


def rows_for(x, value, n):
    m = n // 2
    blocks = value.reshape(m, 2, value.shape[0] // n, value.shape[1])
    return lax.dynamic_index_in_dim(blocks, x, 1, keepdims=False)


def dense_scatter(value, c, n):
    x = c % 2
    value = value.astype(bf16)
    received = swap(rows_for(1 - x, value, n), "ctx", 1)
    mine = (rows_for(x, value, n).astype(f32) + received.astype(f32)).astype(bf16)
    return line_scatter(mine, c // 2, n)


def per_device(
    tokens,
    teacher,
    lengths,
    routes,
    query_weight,
    key_projection_matrix,
    value_projection_matrix,
    output_weight,
    attn_gain,
    moe_gain,
    router_weight,
    shared_gate,
    shared_up,
    shared_down,
    expert_gate,
    expert_up,
    expert_down,
):
    w = lax.axis_index("wa")
    c = lax.axis_index("ctx")
    n = lax.axis_size("ctx")
    groups = lax.axis_size("wa")
    x, z = c % 2, c // 2
    own_tokens = tokens[0]
    rows, features = own_tokens.shape
    slab = features // groups
    length = jnp.sum(jnp.where(jnp.arange(lengths.shape[0]) == w, lengths, 0))
    count = jnp.sum(lengths).astype(f32)
    qpos = c * rows + jnp.arange(rows)

    def columns(value, index):
        return lax.dynamic_slice_in_dim(value, index * slab, slab, 1)

    input_rows = own_tokens.astype(f32)
    factor_a = rms_factor(input_rows)
    far_half = jnp.concatenate([columns(own_tokens, w ^ 2), columns(own_tokens, w ^ 3)], axis=1)
    far_tokens = swap(far_half, "wa", 2)
    far_factor = swap(factor_a, "wa", 2)
    weights_kv = jnp.concatenate([key_projection_matrix, value_projection_matrix], axis=1)
    near_kv = swap(weights_kv, "wa", 1)
    near_q = swap(query_weight, "wa", 1)
    small = jnp.concatenate(
        [router_weight.T, attn_gain[None], moe_gain[None]], axis=0
    )
    near_small = swap(small, "wa", 1)

    gain_own = small[-2:-1].astype(f32)
    gain_near = near_small[-2:-1].astype(f32)
    part_own = jnp.concatenate([columns(own_tokens, w), far_tokens[:, :slab]], axis=0)
    part_near = jnp.concatenate([columns(own_tokens, w ^ 1), far_tokens[:, slab:]], axis=0)
    both_factor = jnp.concatenate([factor_a, far_factor], axis=0)
    normed_own = (part_own.astype(f32) * both_factor * gain_own).astype(bf16)
    normed_near = (part_near.astype(f32) * both_factor * gain_near).astype(bf16)

    def project(weight_own, weight_near):
        partial = mm(normed_own, weight_own) + mm(normed_near, weight_near)
        received = swap(partial[rows:].astype(bf16), "wa", 2)
        return (partial[:rows] + received.astype(f32)).astype(bf16)

    kv = project(weights_kv, near_kv)
    query_rows = project(query_weight, near_q)
    kv_all, pos = gather_keys(kv, c, n)

    far_small = swap(small, "wa", 2)
    smalls = jnp.concatenate(perm4([small, near_small, far_small, swap(far_small, "wa", 1)], w), axis=1)
    router_t = smalls[:-2]
    gain_a, gain_b = smalls[-2].astype(f32), smalls[-1].astype(f32)
    output_parts = gather_wa(output_weight)
    shared_three = jnp.stack([shared_gate, shared_up, shared_down])
    shared_width = shared_three.shape[2] // groups

    def shared_columns(i):
        return lax.dynamic_slice_in_dim(shared_three, (w ^ i) * shared_width, shared_width, 2)

    shared_mine = jnp.concatenate(perm4(exchange_wa(shared_columns), w), axis=1)
    weights = (expert_gate, expert_up, expert_down) + tuple(shared_mine)

    q = heads(query_rows, GROUP)
    attn, kept_attn = attention_forward(q, kv_all, pos, qpos, length)
    attn_out = attn.reshape(rows, -1).astype(bf16)
    branch = jnp.concatenate(perm4([mm_nt(attn_out, part) for part in output_parts], w), axis=1)
    resid = input_rows + branch
    factor_b = rms_factor(resid)
    moe_in = (resid * factor_b * gain_b).astype(bf16)

    experts_all = router_t.shape[0]
    logits = mm_nt(moe_in, router_t)
    chosen = jnp.any(routes[0][:, :, None] == jnp.arange(experts_all), axis=1)
    top = jnp.max(jnp.where(chosen, logits, masked), axis=-1, keepdims=True)
    raised = jnp.where(chosen, jnp.exp(jnp.minimum(logits - top, 0.0)), 0.0)
    gates = raised / jnp.sum(raised, axis=-1, keepdims=True)

    here = expert_gate.shape[0]
    row_parts = gather_wa(moe_in)

    def gates_for(i):
        return lax.dynamic_slice_in_dim(gates.T, (w ^ i) * here, here, 0)

    gate_parts = exchange_wa(gates_for)
    halves = [
        (
            jnp.concatenate(row_parts[2 * h : 2 * h + 2]),
            jnp.concatenate(gate_parts[2 * h : 2 * h + 2], axis=1)[:, :, None],
        )
        for h in range(2)
    ]
    done = [experts_forward(half_rows, half_gates, weights) for half_rows, half_gates in halves]
    out_parts = [done[0][0][:rows], done[0][0][rows:], done[1][0][:rows], done[1][0][rows:]]
    result = resid + sum_wa(out_parts)
    block_out = result.astype(bf16)

    valid = (qpos < length).astype(f32)
    error = (result - teacher[0]) * valid[:, None]
    loss_sum = jnp.sum(error * error)[None]
    grad_result = error * (lengths.shape[0] * n * rows / count)
    grad_low = grad_result.astype(bf16)
    grad_parts = gather_wa(grad_low)

    back = []
    for h in range(2):
        half_grad = jnp.concatenate(grad_parts[2 * h : 2 * h + 2])
        back.append(experts_backward(half_grad, halves[h][1], weights, done[h][1]))
    d_row_parts = [back[0][0][:rows], back[0][0][rows:], back[1][0][:rows], back[1][0][rows:]]
    d_gate_all = jnp.concatenate([back[0][1], back[1][1]], axis=1)
    d_gate_parts = exchange_wa(lambda i: d_gate_all[:, i * rows : (i + 1) * rows])
    grad_moe_in = sum_wa(d_row_parts)
    d_gate = jnp.concatenate(perm4(d_gate_parts, w), axis=0).T
    d_logits = gates * (d_gate - jnp.sum(gates * d_gate, axis=-1, keepdims=True))
    d_logits_low = d_logits.astype(bf16)
    grad_router_t = mm_tn(d_logits_low, moe_in)
    grad_moe_in = grad_moe_in + mm(d_logits_low, router_t)
    grad_norm_b, grad_gain_b = norm_backward(resid, factor_b, gain_b, grad_moe_in)
    grad_resid = grad_result + grad_norm_b
    gz = grad_resid.astype(bf16)

    def fold(expert_value, shared_value):
        half = expert_value.shape[0] // 2
        width = shared_value.shape[1] // 2

        def piece(which):
            return (
                lax.dynamic_slice_in_dim(expert_value, which * half, half, 0),
                lax.dynamic_slice_in_dim(shared_value, which * width, width, 1),
            )

        mine, theirs = piece(x), piece(1 - x)
        got = swap(theirs[0], "ctx", 1), swap(theirs[1], "ctx", 1)
        return (
            jnp.concatenate([mine[0], got[0]], axis=1),
            jnp.concatenate([mine[1], got[1]], axis=0),
        )

    def pair_rows(parts):
        own, far = (
            swap(parts[0], "ctx", 1),
            swap(parts[2], "ctx", 1),
        )
        return jnp.concatenate(parts + [own, swap(own, "wa", 1), far, swap(far, "wa", 1)])

    hidden_all = jnp.concatenate([done[0][2], done[1][2]], axis=1)
    shared_hidden_all = jnp.concatenate([done[0][3], done[1][3]], axis=0)
    rows_pair = pair_rows(row_parts)
    hidden_pair = fold(hidden_all, shared_hidden_all)
    grads_pair = pair_rows(grad_parts)

    def expert_sum(left, pair):
        e_pair, s_pair = pair
        terms = [mm_tn(left, e_pair[e]).astype(bf16) for e in range(e_pair.shape[0])]
        terms.append(mm_tn(left, s_pair).astype(bf16))
        wide = jnp.concatenate(terms, axis=1)
        m = n // 2
        summed = line_scatter(wide.reshape(m, features // m, -1), z, n)
        summed = summed.reshape(2, features // n, -1)
        ours = lax.dynamic_index_in_dim(summed, x, 0, keepdims=False)
        other = lax.dynamic_index_in_dim(summed, 1 - x, 0, keepdims=False)
        got = swap(other.astype(bf16), "ctx", 1).astype(f32)
        first, second = jnp.where(x == 0, ours, got), jnp.where(x == 0, got, ours)
        width = e_pair.shape[2]
        shared = s_pair.shape[1]
        experts = [
            value[:, e * width : (e + 1) * width]
            for value in (first, second)
            for e in range(e_pair.shape[0])
        ]
        shared_columns_sum = jnp.concatenate([first[:, -shared:], second[:, -shared:]], axis=1)
        fine = features // n // groups

        def fine_rows(i):
            return lax.dynamic_slice_in_dim(
                shared_columns_sum.astype(bf16), (w ^ i) * fine, fine, 0
            )

        shared_rows = jnp.concatenate(perm4(exchange_wa(fine_rows), w), axis=1).astype(f32)
        return jnp.stack(experts), shared_rows

    grad_expert_down, grad_shared_down = expert_sum(grads_pair, hidden_pair)
    gate_pair = fold(
        jnp.concatenate([back[0][2], back[1][2]], axis=1),
        jnp.concatenate([back[0][4], back[1][4]], axis=0),
    )
    grad_expert_gate, grad_shared_gate = expert_sum(rows_pair, gate_pair)
    up_pair = fold(
        jnp.concatenate([back[0][3], back[1][3]], axis=1),
        jnp.concatenate([back[0][5], back[1][5]], axis=0),
    )
    grad_expert_up, grad_shared_up = expert_sum(rows_pair, up_pair)

    def fine_columns(value, index):
        blocks = value.reshape(value.shape[0], n, groups, features // n // groups)
        return lax.dynamic_index_in_dim(blocks, index, 2, keepdims=False).reshape(
            value.shape[0], slab
        )

    attn_in = (input_rows * factor_a * gain_a).astype(bf16)
    attn_in_fine = jnp.concatenate(exchange_wa(lambda i: fine_columns(attn_in, w ^ i)))
    attn_out_parts = jnp.concatenate(gather_wa(attn_out))
    gz_fine = jnp.concatenate(exchange_wa(lambda i: fine_columns(gz, w ^ i)))
    grad_output = dense_scatter(mm_tn(gz_fine, attn_out_parts), c, n)

    gz_parts = perm4([columns(gz, s) for s in range(4)], w)
    d_attn_rows = mm(gz_parts[0], output_parts[0])
    for i in range(1, 4):
        d_attn_rows = d_attn_rows + mm(gz_parts[i], output_parts[i])
    d_attn = heads(d_attn_rows.astype(bf16), GROUP)
    delta = jnp.transpose(jnp.sum(d_attn.astype(f32) * attn, axis=-1), (1, 2, 0))[..., None]
    d_q, d_kv_terms = attention_backward(
        q, kv_all, pos, qpos, length, kept_attn, d_attn, delta
    )
    d_q_low = d_q.reshape(rows, -1).astype(bf16)
    far_d_q = swap(d_q_low, "wa", 2)
    d_kv_low = scatter_keys(d_kv_terms, n).astype(bf16)
    far_d_kv = swap(d_kv_low, "wa", 2)

    both_d_q = jnp.concatenate([d_q_low, far_d_q])
    both_d_kv = jnp.concatenate([d_kv_low, far_d_kv])
    all_d_q = jnp.concatenate([d_q_low, swap(d_q_low, "wa", 1), far_d_q, swap(far_d_q, "wa", 1)])
    all_d_kv = jnp.concatenate(
        [d_kv_low, swap(d_kv_low, "wa", 1), far_d_kv, swap(far_d_kv, "wa", 1)]
    )
    grad_query = dense_scatter(mm_tn(attn_in_fine, all_d_q), c, n)

    back_own = mm_nt(both_d_q, query_weight) + mm_nt(both_d_kv, weights_kv)
    back_near = mm_nt(both_d_q, near_q) + mm_nt(both_d_kv, near_kv)
    returned = swap(
        jnp.concatenate([back_own[rows:], back_near[rows:]], axis=1).astype(bf16), "wa", 2
    ).astype(f32)
    grad_attn_in = jnp.concatenate(
        perm4([back_own[:rows], back_near[:rows], returned[:, :slab], returned[:, slab:]], w),
        axis=1,
    )
    grad_norm_a, grad_gain_a = norm_backward(input_rows, factor_a, gain_a, grad_attn_in)
    grad_tokens = grad_resid + grad_norm_a

    smalls_grad = jnp.concatenate(
        [grad_router_t, grad_gain_a[None], grad_gain_b[None]], axis=0
    )
    small_parts = exchange_wa(lambda i: fine_columns(smalls_grad, w ^ i))
    small_sum = (small_parts[0] + small_parts[1] + small_parts[2] + small_parts[3]).T
    kv_and_small = jnp.concatenate([mm_tn(attn_in_fine, all_d_kv), small_sum], axis=1)
    summed = dense_scatter(kv_and_small, c, n)
    width = KEY_VALUE_HEADS * HEAD_SIZE
    grad_key, grad_value = summed[:, :width], summed[:, width : 2 * width]
    grad_router = summed[:, 2 * width : 2 * width + experts_all]
    grad_attn_gain = summed[:, 2 * width + experts_all]
    grad_moe_gain = summed[:, 2 * width + experts_all + 1]

    bit = 1
    while bit < groups:
        loss_sum = loss_sum + swap(loss_sum, "wa", bit)
        bit *= 2
    bit = 1
    while bit < n:
        loss_sum = loss_sum + swap(loss_sum, "ctx", bit)
        bit *= 2
    loss = loss_sum[0] / (2.0 * features * count)

    return (
        block_out[None],
        grad_tokens[None],
        grad_query,
        grad_key,
        grad_value,
        grad_output,
        grad_attn_gain,
        grad_moe_gain,
        grad_router,
        grad_shared_gate,
        grad_shared_up,
        grad_shared_down,
        grad_expert_gate,
        grad_expert_up,
        grad_expert_down,
        loss,
    )


def solution(mesh):
    return jax.shard_map(
        per_device,
        mesh=mesh,
        in_specs=(
            P("wa", "ctx", None),
            P("wa", "ctx", None),
            P(),
            P("wa", "ctx", None),
            P("wa", None),
            P("wa", None),
            P("wa", None),
            P("wa", None),
            P("wa"),
            P("wa"),
            P("wa", None),
            P("wa", None),
            P("wa", None),
            P("wa", None),
            P("wa", None, None),
            P("wa", None, None),
            P("wa", None, None),
        ),
        out_specs=(
            P("wa", "ctx", None),
            P("wa", "ctx", None),
            P(("ctx", "wa"), None),
            P(("ctx", "wa"), None),
            P(("ctx", "wa"), None),
            P(("ctx", "wa"), None),
            P(("ctx", "wa")),
            P(("ctx", "wa")),
            P(("ctx", "wa"), None),
            P(("ctx", "wa"), None),
            P(("ctx", "wa"), None),
            P(("ctx", "wa"), None),
            P("wa", "ctx", None),
            P("wa", "ctx", None),
            P("wa", "ctx", None),
            P(),
        ),
        check_vma=False,
    )
```

```python
import jax
import jax.numpy as jnp
from jax import lax
from jax.experimental import pallas as pl
from jax.experimental.pallas import tpu as pltpu
from jax.sharding import PartitionSpec as P

QUERY_HEADS = 12
KEY_VALUE_HEADS = 4
HEAD_SIZE = 128
TOP = 6
GROUP = QUERY_HEADS // KEY_VALUE_HEADS

epsilon = 1e-06
masked = -1e30
bf16 = jnp.bfloat16
f32 = jnp.float32


def dot(a, b, dims):
    return lax.dot_general(a, b, ((dims[0], dims[1]), ((), ())), preferred_element_type=f32)


def mm(a, b):
    return dot(a, b, ((1,), (0,)))


def mm_nt(a, b):
    return dot(a, b, ((1,), (1,)))


def mm_tn(a, b):
    return dot(a, b, ((0,), (0,)))


def swap(value, axis, bit):
    size = lax.axis_size(axis)
    return lax.ppermute(value, axis, [(i, i ^ bit) for i in range(size)])


def perm4(parts, w):
    core, upper = w % 2 == 1, w // 2 == 1
    a, b, c, d = parts
    a, b, c, d = (
        jnp.where(core, b, a),
        jnp.where(core, a, b),
        jnp.where(core, d, c),
        jnp.where(core, c, d),
    )
    return [
        jnp.where(upper, c, a),
        jnp.where(upper, d, b),
        jnp.where(upper, a, c),
        jnp.where(upper, b, d),
    ]


def gather_wa(value):
    near = swap(value, "wa", 1)
    far = swap(value, "wa", 2)
    return [value, near, far, swap(far, "wa", 1)]


def silu_parts(rows):
    sigma = jax.nn.sigmoid(rows)
    return rows * sigma, sigma * (1.0 + rows * (1.0 - sigma))


def rms_factor(rows):
    return lax.rsqrt(jnp.mean(rows * rows, axis=-1, keepdims=True) + epsilon)


def norm_backward(rows, factor, gain, upstream):
    weighted = upstream * gain
    inner = jnp.mean(weighted * rows, axis=-1, keepdims=True)
    grad = factor * weighted - rows * (factor * factor * factor * inner)
    return grad, jnp.sum(upstream * rows * factor, axis=0)


def gather_keys(kv, c, n):
    rows = kv.shape[0]
    if n > 8:
        return lax.all_gather(kv, "ctx", axis=0, tiled=True), jnp.arange(n * rows)
    levels = [kv]
    for s in range(1, n // 2):
        levels.append(lax.ppermute(kv, "ctx", [(i, i + 2 * s) for i in range(n - 2 * s)]))
    blocks, pos = [], []
    for s, level in enumerate(levels):
        blocks += [level, swap(level, "ctx", 1)]
        start = (c - 2 * s) * rows
        pos += [start + jnp.arange(rows), (c - 2 * s + 1 - 2 * (c % 2)) * rows + jnp.arange(rows)]
    return jnp.concatenate(blocks), jnp.concatenate(pos)


def scatter_keys(grads, n):
    rows = grads.shape[0] // n
    if n > 8:
        return lax.psum_scatter(grads, "ctx", scatter_dimension=0, tiled=True).astype(f32)
    blocks = grads.reshape(n, rows, -1)
    total = None
    for s in reversed(range(n // 2)):
        level = blocks[2 * s].astype(f32) + swap(blocks[2 * s + 1], "ctx", 1).astype(f32)
        if s:
            level = lax.ppermute(
                level.astype(bf16), "ctx", [(i + 2 * s, i) for i in range(n - 2 * s)]
            ).astype(f32)
        total = level if total is None else total + level
    return total


def heads(rows, groups):
    return rows.reshape(rows.shape[0], KEY_VALUE_HEADS, groups, HEAD_SIZE)


def attention_scores(q, k, pos, qpos, length):
    scale = HEAD_SIZE**-0.5
    scores = jnp.einsum("tkgd,nkd->kgtn", q, k, preferred_element_type=f32) * scale
    allowed = (pos[None, :] >= 0) & (pos[None, :] <= qpos[:, None]) & (pos[None, :] < length)
    return scores, allowed


def chunked(kv, pos):
    size = 1024
    if kv.shape[0] <= size:
        return None
    return kv.reshape(-1, size, kv.shape[1]), pos.reshape(-1, size)


def attention_forward(q, kv, pos, qpos, length):
    rows = q.shape[0]
    pieces = chunked(kv, pos)
    width = KEY_VALUE_HEADS * HEAD_SIZE
    if pieces is None:
        k, v = heads(kv[:, :width], 1)[:, :, 0], heads(kv[:, width:], 1)[:, :, 0]
        scores, allowed = attention_scores(q, k, pos, qpos, length)
        scores = jnp.where(allowed, scores, masked)
        top = jnp.max(scores, axis=-1, keepdims=True)
        weights = jnp.exp(scores - top)
        probs = (weights / jnp.sum(weights, axis=-1, keepdims=True)).astype(bf16)
        attn = jnp.einsum("kgtn,nkd->tkgd", probs, v, preferred_element_type=f32)
        return attn, probs

    def step(carry, piece):
        top, total, accum = carry
        kv_now, pos_now = piece
        k, v = heads(kv_now[:, :width], 1)[:, :, 0], heads(kv_now[:, width:], 1)[:, :, 0]
        scores, allowed = attention_scores(q, k, pos_now, qpos, length)
        scores = jnp.where(allowed, scores, masked)
        new_top = jnp.maximum(top, jnp.max(scores, axis=-1, keepdims=True))
        weights = jnp.where(allowed, jnp.exp(scores - new_top), 0.0)
        shrink = jnp.exp(top - new_top)
        total = total * shrink + jnp.sum(weights, axis=-1, keepdims=True)
        update = jnp.einsum("kgtn,nkd->kgtd", weights.astype(bf16), v, preferred_element_type=f32)
        return (new_top, total, accum * shrink + update), None

    shape = (KEY_VALUE_HEADS, GROUP, rows)
    start = (
        jnp.full(shape + (1,), masked, f32),
        jnp.zeros(shape + (1,), f32),
        jnp.zeros(shape + (HEAD_SIZE,), f32),
    )
    (top, total, accum), _ = lax.scan(step, start, pieces)
    return jnp.transpose(accum / total, (2, 0, 1, 3)), top + jnp.log(total)


def attention_backward(q, kv, pos, qpos, length, kept, d_attn, delta):
    scale = HEAD_SIZE**-0.5
    width = KEY_VALUE_HEADS * HEAD_SIZE

    def terms(probs, k, v):
        d_probs = jnp.einsum("tkgd,nkd->kgtn", d_attn, v, preferred_element_type=f32)
        d_scores = (probs.astype(f32) * (d_probs - delta)).astype(bf16)
        d_q = jnp.einsum("kgtn,nkd->tkgd", d_scores, k, preferred_element_type=f32) * scale
        d_k = jnp.einsum("kgtn,tkgd->nkd", d_scores, q, preferred_element_type=f32) * scale
        d_v = jnp.einsum(
            "kgtn,tkgd->nkd", probs.astype(bf16), d_attn, preferred_element_type=f32
        )
        keys = k.shape[0]
        return d_q, jnp.concatenate(
            [d_k.reshape(keys, width), d_v.reshape(keys, width)], axis=1
        ).astype(bf16)

    pieces = chunked(kv, pos)
    if pieces is None:
        k, v = heads(kv[:, :width], 1)[:, :, 0], heads(kv[:, width:], 1)[:, :, 0]
        return terms(kept, k, v)

    def step(d_q, piece):
        kv_now, pos_now = piece
        k, v = heads(kv_now[:, :width], 1)[:, :, 0], heads(kv_now[:, width:], 1)[:, :, 0]
        scores, allowed = attention_scores(q, k, pos_now, qpos, length)
        probs = jnp.where(allowed, jnp.exp(scores - kept), 0.0)
        more, d_kv = terms(probs, k, v)
        return d_q + more, d_kv

    d_q, d_kv = lax.scan(step, jnp.zeros(q.shape, f32), pieces)
    return d_q, d_kv.reshape(kv.shape)


EXTRA = 128
in_vmem = pl.BlockSpec(memory_space=pltpu.VMEM)
in_smem = pl.BlockSpec(memory_space=pltpu.SMEM)
anywhere = pl.BlockSpec(memory_space=pltpu.MemorySpace.HBM)


def hbm(shape, dtype):
    return pltpu.HBM(shape, dtype)


def in_hbm(value):
    return pltpu.with_memory_space_constraint(value, pltpu.HBM)


def start_copy(source, target, sems, index):
    copy = pltpu.make_async_copy(source, target, sems.at[index])
    copy.start()
    return copy


def limits(mib):
    return pltpu.CompilerParams(vmem_limit_bytes=mib << 20)


def split_low(value, lane, shift):
    high = value.astype(bf16).astype(f32)
    rest = pltpu.roll(value - high, shift, 1)
    return jnp.where(lane < shift, high, jnp.where(lane < 2 * shift, rest, 0.0))


def join_low(value, lane, shift):
    total = value + pltpu.roll(value, value.shape[1] - shift, 1)
    return jnp.where(lane < shift, total, 0.0)


def lanes_of(rows):
    return lax.broadcasted_iota(jnp.int32, (rows, EXTRA), 1)


def attention_kernel(info_ref, q_ref, *refs):
    blocks = len(refs) - 4
    kv_refs, (attn_ref, probs_out, probs_ref, sems) = refs[:blocks], refs[blocks:]
    sent = []
    rows = q_ref.shape[0]
    width = KEY_VALUE_HEADS * HEAD_SIZE
    qpos = info_ref[0] * rows + lax.broadcasted_iota(jnp.int32, (rows, rows), 0)
    biases = []
    for b in range(blocks):
        kpos = info_ref[2 + b] + lax.broadcasted_iota(jnp.int32, (rows, rows), 1)
        allowed = (kpos >= 0) & (kpos <= qpos) & (kpos < info_ref[1])
        bias = jnp.where(allowed, 0.0, masked)
        biases.append(jnp.concatenate([bias] * GROUP, axis=0))
    for k in range(KEY_VALUE_HEADS):
        first = k * GROUP * HEAD_SIZE
        q = jnp.concatenate(
            [q_ref[:, first + g * HEAD_SIZE : first + (g + 1) * HEAD_SIZE] for g in range(GROUP)],
            axis=0,
        )
        cols = slice(k * HEAD_SIZE, (k + 1) * HEAD_SIZE)
        scores = [
            mm_nt(q, kv_refs[b][:, cols]) * HEAD_SIZE**-0.5 + biases[b] for b in range(blocks)
        ]
        top = scores[0]
        for score in scores[1:]:
            top = jnp.maximum(top, score)
        top = jnp.max(top, axis=1, keepdims=True)
        weights = [jnp.exp(score - top) for score in scores]
        total = weights[0]
        for weight in weights[1:]:
            total = total + weight
        scale = 1.0 / jnp.sum(total, axis=1, keepdims=True)
        attn = None
        for b in range(blocks):
            probs = (weights[b] * scale).astype(bf16)
            probs_ref[k, b] = probs
            term = mm(probs, kv_refs[b][:, width + k * HEAD_SIZE : width + (k + 1) * HEAD_SIZE])
            attn = term if attn is None else attn + term
        sent.append(start_copy(probs_ref.at[k], probs_out.at[k], sems, k))
        for g in range(GROUP):
            attn_ref[:, first + g * HEAD_SIZE : first + (g + 1) * HEAD_SIZE] = attn[
                g * rows : (g + 1) * rows
            ]
    for copy in sent:
        copy.wait()


def attention_call(info, q, kv_blocks):
    rows, blocks = q.shape[0], len(kv_blocks)
    probs = (KEY_VALUE_HEADS, blocks, GROUP * rows, rows)
    return pl.pallas_call(
        attention_kernel,
        out_shape=(jax.ShapeDtypeStruct(q.shape, f32), hbm(probs, bf16)),
        in_specs=[in_smem] + [in_vmem] * (1 + blocks),
        out_specs=(in_vmem, anywhere),
        scratch_shapes=[
            pltpu.VMEM(probs, bf16),
            pltpu.SemaphoreType.DMA((KEY_VALUE_HEADS,)),
        ],
        compiler_params=limits(12),
        name="attention_forward",
    )(info, q, *kv_blocks)


def attention_back_kernel(q_ref, d_ref, attn_ref, probs_ref, *refs):
    blocks = (len(refs) - 1) // 2
    kv_refs, dq_ref, dkv_refs = refs[:blocks], refs[blocks], refs[blocks + 1 :]
    rows = q_ref.shape[0]
    width = KEY_VALUE_HEADS * HEAD_SIZE
    scale = HEAD_SIZE**-0.5

    def stacked(ref, first):
        return jnp.concatenate(
            [ref[:, first + g * HEAD_SIZE : first + (g + 1) * HEAD_SIZE] for g in range(GROUP)],
            axis=0,
        )

    for k in range(KEY_VALUE_HEADS):
        first = k * GROUP * HEAD_SIZE
        q, d_attn = stacked(q_ref, first), stacked(d_ref, first)
        delta = jnp.sum(d_attn.astype(f32) * stacked(attn_ref, first), axis=1, keepdims=True)
        kcols = slice(k * HEAD_SIZE, (k + 1) * HEAD_SIZE)
        vcols = slice(width + k * HEAD_SIZE, width + (k + 1) * HEAD_SIZE)
        d_q = None
        for b in range(blocks):
            key, value = kv_refs[b][:, kcols], kv_refs[b][:, vcols]
            probs = probs_ref[k, b]
            d_probs = mm_nt(d_attn, value)
            d_scores = (probs.astype(f32) * (d_probs - delta)).astype(bf16)
            term = mm(d_scores, key)
            d_q = term if d_q is None else d_q + term
            dkv_refs[b][:, kcols] = (mm_tn(d_scores, q) * scale).astype(bf16)
            dkv_refs[b][:, vcols] = mm_tn(probs, d_attn).astype(bf16)
        d_q = (d_q * scale).astype(bf16)
        for g in range(GROUP):
            dq_ref[:, first + g * HEAD_SIZE : first + (g + 1) * HEAD_SIZE] = d_q[
                g * rows : (g + 1) * rows
            ]


def attention_back_call(q, d_attn, attn, probs, kv_blocks):
    blocks = len(kv_blocks)
    kv_shape = jax.ShapeDtypeStruct(kv_blocks[0].shape, bf16)
    done = pl.pallas_call(
        attention_back_kernel,
        out_shape=(jax.ShapeDtypeStruct(q.shape, bf16),) + (kv_shape,) * blocks,
        in_specs=[in_vmem] * (4 + blocks),
        out_specs=(in_vmem,) * (1 + blocks),
        compiler_params=limits(12),
        name="attention_backward",
    )(q, d_attn, attn, probs, *kv_blocks)
    return done[0], list(done[1:])


def out_halves(info_ref, size):
    x = info_ref[1]
    return (
        pl.ds(pl.multiple_of(x * size, 128), size),
        pl.ds(pl.multiple_of((1 - x) * size, 128), size),
    )


def branch_kernel(
    info_ref, attn_ref, o0, o1, o2, o3, o4, o5, tok_ref, gain_ref, router_ref, routes_ref,
    resid_ref, ext_ref, gates_ref,
):
    rows, features = tok_ref.shape
    slab = o0.shape[0]
    here, other = out_halves(info_ref, o2.shape[1])
    attn = attn_ref[...]
    for i in range(4):
        if i < 2:
            term = mm_nt(attn, (o0, o1)[i][...])
        else:
            term = mm_nt(attn_ref[:, here], (o2, o3)[i - 2][...])
            term = term + mm_nt(attn_ref[:, other], (o4, o5)[i - 2][...])
        at = pl.ds(pl.multiple_of((info_ref[0] ^ i) * slab, 128), slab)
        resid_ref[:, at] = tok_ref[:, at].astype(f32) + term
    resid = resid_ref[...]
    moe_in = (resid * rms_factor(resid) * gain_ref[...]).astype(bf16)
    logits = mm_nt(moe_in, router_ref[...])
    lane = lanes_of(rows)
    chosen = lane == routes_ref[:, 0:1]
    for t in range(1, routes_ref.shape[1]):
        chosen = chosen | (lane == routes_ref[:, t : t + 1])
    logits = jnp.where(chosen, logits, masked)
    raised = jnp.where(chosen, jnp.exp(logits - jnp.max(logits, axis=1, keepdims=True)), 0.0)
    gates = raised / jnp.sum(raised, axis=1, keepdims=True)
    gates_ref[...] = gates
    ext_ref[:, :features] = moe_in
    ext_ref[:, features:] = split_low(gates, lane, 16).astype(bf16)


def branch_call(info, attn, output_parts, own_tokens, gain, router, routes):
    rows, features = own_tokens.shape
    return pl.pallas_call(
        branch_kernel,
        out_shape=(
            jax.ShapeDtypeStruct((rows, features), f32),
            jax.ShapeDtypeStruct((rows, features + EXTRA), bf16),
            jax.ShapeDtypeStruct((rows, EXTRA), f32),
        ),
        in_specs=[in_smem] + [in_vmem] * 11,
        out_specs=(in_vmem,) * 3,
        compiler_params=limits(12),
        name="branch_and_router",
    )(info, attn, *output_parts, own_tokens, gain, router, routes)


def result_kernel(info_ref, scale_ref, resid_ref, own_ref, near_ref, far_ref, teacher_ref,
                  out_ref, grad_ref, ext_ref):
    rows, features = resid_ref.shape
    result = (
        resid_ref[...]
        + own_ref[...]
        + near_ref[...].astype(f32)
        + far_ref[...].astype(f32)
    )
    out_ref[...] = result.astype(bf16)
    first = info_ref[0] + pl.program_id(0) * rows
    qpos = first + lax.broadcasted_iota(jnp.int32, (rows, 1), 0)
    error = jnp.where(qpos < info_ref[1], result - teacher_ref[...], 0.0)
    grad = error * scale_ref[0]
    grad_ref[...] = grad
    ext_ref[:, :features] = grad.astype(bf16)
    lane = lanes_of(rows)
    row_loss = jnp.where(lane == 0, jnp.sum(error * error, axis=1, keepdims=True), 0.0)
    ext_ref[:, features:] = split_low(row_loss, lane, 16).astype(bf16)


def result_call(info, scale, resid, own, near, far, teacher):
    rows, features = resid.shape
    block = rows // 4
    flat = pl.BlockSpec((block, features), lambda i: (i, 0))
    return pl.pallas_call(
        result_kernel,
        grid=(4,),
        out_shape=(
            hbm((rows, features), bf16),
            hbm((rows, features), f32),
            jax.ShapeDtypeStruct((rows, features + EXTRA), bf16),
        ),
        in_specs=[in_smem, in_smem] + [flat] * 5,
        out_specs=(flat, flat, pl.BlockSpec((block, features + EXTRA), lambda i: (i, 0))),
        compiler_params=limits(8),
        name="result_and_error",
    )(info, scale, in_hbm(resid), in_hbm(own), near, far, in_hbm(teacher))


def resid_back_kernel(info_ref, own_ref, near_ref, far_ref, grad_ref, resid_ref, ext_ref, gates_ref,
                      gain_ref, router_ref, o0, o1, o2, o3, o4, o5,
                      out_ref, gz_ref, d_attn_ref, small_ref, sum_ref):
    rows, features = resid_ref.shape
    slab = o0.shape[0]
    lane = lanes_of(rows)
    tail = slice(features, features + EXTRA)
    d_gate = join_low(
        own_ref[:, tail] + near_ref[:, tail].astype(f32) + far_ref[:, tail].astype(f32), lane, 16
    )
    gates = gates_ref[...]
    d_logits = gates * (d_gate - jnp.sum(gates * d_gate, axis=1, keepdims=True))
    d_logits = d_logits.astype(bf16)
    body = slice(0, features)
    upstream = (
        own_ref[:, body]
        + near_ref[:, body].astype(f32)
        + far_ref[:, body].astype(f32)
        + mm(d_logits, router_ref[...])
    )
    resid = resid_ref[...]
    grad_norm, grad_gain = norm_backward(resid, rms_factor(resid), gain_ref[...], upstream)
    experts = small_ref.shape[0] - 8
    small_ref[:experts, :] = mm_tn(d_logits, ext_ref[:, body])[:experts]
    small_ref[experts:, :] = jnp.broadcast_to(grad_gain[None], (8, features))
    grad_resid = grad_ref[...] + grad_norm
    out_ref[...] = grad_resid
    gz_ref[...] = grad_resid.astype(bf16)
    gz = [
        gz_ref[:, pl.ds(pl.multiple_of((info_ref[0] ^ i) * slab, 128), slab)] for i in range(4)
    ]
    sum_ref[...] = mm(gz[0], o0[...]) + mm(gz[1], o1[...])
    here, other = out_halves(info_ref, o2.shape[1])
    sum_ref[:, here] += mm(gz[2], o2[...]) + mm(gz[3], o3[...])
    sum_ref[:, other] += mm(gz[2], o4[...]) + mm(gz[3], o5[...])
    d_attn_ref[...] = sum_ref[...].astype(bf16)


def resid_back_call(info, own, near, far, grad, resid, ext, gates, gain, router, output_parts, experts):
    rows, features = resid.shape
    return pl.pallas_call(
        resid_back_kernel,
        out_shape=(
            jax.ShapeDtypeStruct((rows, features), f32),
            jax.ShapeDtypeStruct((rows, features), bf16),
            jax.ShapeDtypeStruct((rows, output_parts[0].shape[1]), bf16),
            jax.ShapeDtypeStruct((experts + 8, features), f32),
        ),
        in_specs=[in_smem] + [in_vmem] * 15,
        out_specs=(in_vmem,) * 4,
        scratch_shapes=[pltpu.VMEM((rows, output_parts[0].shape[1]), f32)],
        compiler_params=limits(12),
        name="residual_backward",
    )(info, own, near, far, grad, resid, ext, gates, gain, router, *output_parts)


def gate_column(extra, lane, expert):
    here = (lane == expert) | (lane == expert + 16)
    return jnp.sum(jnp.where(here, extra, 0.0), axis=1, keepdims=True)


def store_half(mine, half, cols, value, mine_ref):
    @pl.when(mine == half)
    def _():
        mine_ref[:, cols] = value


def experts_kernel(info_ref, xa_ref, xb_ref, gate_ref, up_ref, down_ref, sg_ref, su_ref, sd_ref,
                   outa_ref, outb_ref, gp_out, upre_out, mine_out,
                   gp_ref, upre_ref, mine_ref, x_ref, acc_ref, sems):
    rows, features = outa_ref.shape
    here, _, width = gate_ref.shape
    x_ref[:rows] = xa_ref[:, :features]
    x_ref[rows:] = xb_ref[:, :features]
    extra = jnp.concatenate([xa_ref[:, features:], xb_ref[:, features:]], axis=0).astype(f32)
    lane = lanes_of(2 * rows)

    def unit(gate_w, up_w):
        gate_pre, up_pre = mm(x_ref[...], gate_w), mm(x_ref[...], up_w)
        return gate_pre, up_pre, gate_pre * jax.nn.sigmoid(gate_pre) * up_pre

    gate_pre, up_pre, hidden = unit(sg_ref[...], su_ref[...])
    hidden = hidden.astype(bf16)
    acc_ref[...] = mm_nt(hidden, sd_ref[...])
    part = hidden.shape[1] // 2
    for half in range(2):
        cols, mine = slice(2 * width, 2 * width + part), slice(half * part, (half + 1) * part)
        gp_ref[half, :, cols] = gate_pre[:, mine].astype(bf16)
        upre_ref[half, :, cols] = up_pre[:, mine].astype(bf16)
        store_half(info_ref[1], half, cols, hidden[:, mine], mine_ref)
    sent = []
    for e in range(here):
        gate = gate_column(extra, lane, info_ref[0] * here + e)
        gate_pre, up_pre, hidden = unit(gate_ref[e], up_ref[e])
        hidden = (hidden * gate).astype(bf16)
        half, at = e // 2, (e % 2) * width
        cols = slice(at, at + width)
        gp_ref[half, :, cols] = gate_pre.astype(bf16)
        upre_ref[half, :, cols] = up_pre.astype(bf16)
        store_half(info_ref[1], half, cols, hidden, mine_ref)
        if e % 2:
            sent.append(start_copy(gp_ref.at[half], gp_out.at[half], sems, 2 * half))
            sent.append(start_copy(upre_ref.at[half], upre_out.at[half], sems, 2 * half + 1))
        if e + 1 == here:
            sent.append(start_copy(mine_ref, mine_out, sems, 4))
        acc_ref[...] += mm_nt(hidden, down_ref[e])
    outa_ref[...] = acc_ref[:rows]
    outb_ref[...] = acc_ref[rows:].astype(bf16)
    for copy in sent:
        copy.wait()


def experts_call(info, xa, xb, weights):
    rows, features = xa.shape[0], xa.shape[1] - EXTRA
    wide = 2 * weights[0].shape[2] + weights[3].shape[1] // 2
    both, half = hbm((2, 2 * rows, wide), bf16), hbm((2 * rows, wide), bf16)
    return pl.pallas_call(
        experts_kernel,
        out_shape=(
            jax.ShapeDtypeStruct((rows, features), f32),
            jax.ShapeDtypeStruct((rows, features), bf16),
            both,
            both,
            half,
        ),
        in_specs=[in_smem] + [in_vmem] * 8,
        out_specs=(in_vmem,) * 2 + (anywhere,) * 3,
        scratch_shapes=[
            pltpu.VMEM(both.shape, bf16),
            pltpu.VMEM(both.shape, bf16),
            pltpu.VMEM(half.shape, bf16),
            pltpu.VMEM((2 * rows, features), bf16),
            pltpu.VMEM((2 * rows, features), f32),
            pltpu.SemaphoreType.DMA((5,)),
        ],
        compiler_params=limits(16),
        name="experts_forward",
    )(info, xa, xb, *weights)


def hidden_back(d_hidden, gate_pre, up_pre, gate):
    gate_pre, up_pre = gate_pre.astype(f32), up_pre.astype(f32)
    act, slope = silu_parts(gate_pre)
    d_gate = None
    if gate is not None:
        d_gate = jnp.sum(d_hidden * act * up_pre, axis=1, keepdims=True)
        d_hidden = d_hidden * gate
    return d_gate, (d_hidden * up_pre * slope).astype(bf16), (d_hidden * act).astype(bf16)


def experts_back_kernel(info_ref, *refs):
    g_in, e_in, (gpa_in, gpb_in, upa_in, upb_in), refs = refs[:4], refs[4:8], refs[8:12], refs[12:]
    (gate_ref, up_ref, down_ref, sg_ref, su_ref, sd_ref), dx_refs, refs = refs[:6], refs[6:10], refs[10:]
    d_out, (gp_ref, upre_ref, dgm_ref, dum_ref, g_ref, acc_ref, sems) = refs[:2], refs[2:]
    rows = g_in[0].shape[0]
    features = g_ref.shape[1]
    here, _, width = gate_ref.shape
    mine = info_ref[1]
    lane = lanes_of(4 * rows)
    first, last = slice(0, 2 * rows), slice(2 * rows, 4 * rows)
    loads = [
        start_copy(source, target, sems, i)
        for i, (source, target) in enumerate(
            [
                (gpa_in, gp_ref.at[:, first]),
                (gpb_in, gp_ref.at[:, last]),
                (upa_in, upre_ref.at[:, first]),
                (upb_in, upre_ref.at[:, last]),
            ]
        )
    ]
    for i, ref in enumerate(g_in):
        g_ref[i * rows : (i + 1) * rows] = ref[:, :features]
    extra = jnp.concatenate([ref[:, features:] for ref in e_in], axis=0).astype(f32)
    d_gates = jnp.zeros((4 * rows, EXTRA), f32)

    def unit(d_hidden, half, cols, gate):
        d_gate, d_gate_pre, d_up_pre = hidden_back(
            d_hidden, gp_ref[half, :, cols], upre_ref[half, :, cols], gate
        )
        store_half(mine, half, cols, d_gate_pre, dgm_ref)
        store_half(mine, half, cols, d_up_pre, dum_ref)
        return d_gate, d_gate_pre, d_up_pre

    d_hidden = mm(g_ref[...], sd_ref[...])
    for copy in loads:
        copy.wait()
    part = d_hidden.shape[1] // 2
    total = None
    for half in range(2):
        at = slice(half * part, (half + 1) * part)
        _, d_gate_pre, d_up_pre = unit(
            d_hidden[:, at], half, slice(2 * width, 2 * width + part), None
        )
        term = mm_nt(d_gate_pre, sg_ref[:, at]) + mm_nt(d_up_pre, su_ref[:, at])
        total = term if total is None else total + term
    acc_ref[...] = total
    sent = []
    for e in range(here):
        expert = info_ref[0] * here + e
        at = (e % 2) * width
        d_gate, d_gate_pre, d_up_pre = unit(
            mm(g_ref[...], down_ref[e]),
            e // 2,
            slice(at, at + width),
            gate_column(extra, lane, expert),
        )
        d_gates = jnp.where(lane == expert, d_gate, d_gates)
        if e + 1 == here:
            sent = [
                start_copy(dgm_ref, d_out[0], sems, 4),
                start_copy(dum_ref, d_out[1], sems, 5),
            ]
        acc_ref[...] += mm_nt(d_gate_pre, gate_ref[e]) + mm_nt(d_up_pre, up_ref[e])
    extra = split_low(d_gates, lane, 16)
    for i, ref in enumerate(dx_refs):
        at = slice(i * rows, (i + 1) * rows)
        ref[:, :features] = acc_ref[at].astype(ref.dtype)
        ref[:, features:] = extra[at].astype(ref.dtype)
    for copy in sent:
        copy.wait()


def experts_back_call(info, grads, exts, kept, weights):
    rows, features = grads[0].shape[0], grads[0].shape[1] - EXTRA
    _, held, wide = kept[0].shape
    return pl.pallas_call(
        experts_back_kernel,
        out_shape=tuple(
            jax.ShapeDtypeStruct(grads[0].shape, bf16 if i % 2 else f32) for i in range(4)
        )
        + (hbm((2 * held, wide), bf16),) * 2,
        in_specs=[in_smem] + [in_vmem] * 8 + [anywhere] * 4 + [in_vmem] * 6,
        out_specs=(in_vmem,) * 4 + (anywhere,) * 2,
        scratch_shapes=[pltpu.VMEM((2, 2 * held, wide), bf16)] * 2
        + [pltpu.VMEM((2 * held, wide), bf16)] * 2
        + [
            pltpu.VMEM((4 * rows, features), bf16),
            pltpu.VMEM((4 * rows, features), f32),
            pltpu.SemaphoreType.DMA((6,)),
        ],
        compiler_params=limits(24),
        name="experts_backward",
    )(info, *grads, *exts, *kept, *weights)


def pair_weights(info_ref, refs, shared_refs):
    x, count = info_ref[1], refs[0].shape[0] // 2
    part = shared_refs[0].shape[1] // 2
    at = pl.ds(pl.multiple_of(x * part, 128), part)
    return [[ref[x * count + j] for ref in refs] for j in range(count)], [
        ref[:, at] for ref in shared_refs
    ]


def pair_kernel(info_ref, x0, x1, x2, x3, gate_ref, up_ref, sg_ref, su_ref,
                gp_out, upre_out, hid_out, gp_ref, upre_ref, hid_ref, x_ref, sems):
    rows, features = x0.shape[0], x_ref.shape[1]
    here, _, width = gate_ref.shape
    for i, ref in enumerate((x0, x1, x2, x3)):
        x_ref[i * rows : (i + 1) * rows] = ref[:, :features]
    extra = jnp.concatenate([ref[:, features:] for ref in (x0, x1, x2, x3)], axis=0).astype(f32)
    lane = lanes_of(4 * rows)
    routed, shared = pair_weights(info_ref, (gate_ref, up_ref), (sg_ref, su_ref))
    for j, (gate_w, up_w) in enumerate(routed + [shared]):
        gate_pre, up_pre = mm(x_ref[...], gate_w), mm(x_ref[...], up_w)
        hidden = gate_pre * jax.nn.sigmoid(gate_pre) * up_pre
        if j < len(routed):
            expert = info_ref[0] * here + info_ref[1] * len(routed) + j
            hidden = hidden * gate_column(extra, lane, expert)
        cols = slice(j * width, j * width + gate_pre.shape[1])
        gp_ref[:, cols] = gate_pre.astype(bf16)
        upre_ref[:, cols] = up_pre.astype(bf16)
        hid_ref[:, cols] = hidden.astype(bf16)
    sent = [
        start_copy(source, target, sems, i)
        for i, (source, target) in enumerate(
            [(hid_ref, hid_out), (gp_ref, gp_out), (upre_ref, upre_out)]
        )
    ]
    for copy in sent:
        copy.wait()


def pair_call(info, exts, weights):
    rows, features = 4 * exts[0].shape[0], exts[0].shape[1] - EXTRA
    e_gate, e_up, _, s_gate, s_up, _ = weights
    wide = (rows, e_gate.shape[0] // 2 * e_gate.shape[2] + s_gate.shape[1] // 2)
    return pl.pallas_call(
        pair_kernel,
        out_shape=(hbm(wide, bf16),) * 3,
        in_specs=[in_smem] + [in_vmem] * 8,
        out_specs=(anywhere,) * 3,
        scratch_shapes=[pltpu.VMEM(wide, bf16)] * 3
        + [pltpu.VMEM((rows, features), bf16), pltpu.SemaphoreType.DMA((3,))],
        compiler_params=limits(16),
        name="pair_forward",
    )(info, *exts, e_gate, e_up, s_gate, s_up)


def pair_back_kernel(info_ref, g0, g1, g2, g3, e0, e1, e2, e3, gp_in, upre_in, down_ref, sd_ref,
                     dg_out, du_out, gp_ref, upre_ref, dg_ref, du_ref, g_ref, sems):
    rows, features = g0.shape[0], g_ref.shape[1]
    here, _, width = down_ref.shape
    loads = [start_copy(gp_in, gp_ref, sems, 0), start_copy(upre_in, upre_ref, sems, 1)]
    for i, ref in enumerate((g0, g1, g2, g3)):
        g_ref[i * rows : (i + 1) * rows] = ref[:, :features]
    extra = jnp.concatenate([ref[:, features:] for ref in (e0, e1, e2, e3)], axis=0).astype(f32)
    lane = lanes_of(4 * rows)
    routed, shared = pair_weights(info_ref, (down_ref,), (sd_ref,))
    for copy in loads:
        copy.wait()
    for j, (weight,) in enumerate(routed + [shared]):
        gate = None
        if j < len(routed):
            gate = gate_column(extra, lane, info_ref[0] * here + info_ref[1] * len(routed) + j)
        cols = slice(j * width, j * width + weight.shape[1])
        _, d_gate_pre, d_up_pre = hidden_back(
            mm(g_ref[...], weight), gp_ref[:, cols], upre_ref[:, cols], gate
        )
        dg_ref[:, cols] = d_gate_pre
        du_ref[:, cols] = d_up_pre
    sent = [start_copy(dg_ref, dg_out, sems, 2), start_copy(du_ref, du_out, sems, 3)]
    for copy in sent:
        copy.wait()


def pair_back_call(info, grads, exts, gate_pre, up_pre, weights):
    rows, features = 4 * exts[0].shape[0], exts[0].shape[1] - EXTRA
    wide = gate_pre.shape
    return pl.pallas_call(
        pair_back_kernel,
        out_shape=(hbm(wide, bf16),) * 2,
        in_specs=[in_smem] + [in_vmem] * 8 + [anywhere] * 2 + [in_vmem] * 2,
        out_specs=(anywhere,) * 2,
        scratch_shapes=[pltpu.VMEM(wide, bf16)] * 4
        + [pltpu.VMEM((rows, features), bf16), pltpu.SemaphoreType.DMA((4,))],
        compiler_params=limits(16),
        name="pair_backward",
    )(info, *grads, *exts, gate_pre, up_pre, weights[2], weights[5])


def weight_grad_kernel(*refs):
    lefts, rights, (out_ref, left_ref, right_ref, tiles_ref, sems) = refs[:8], refs[8:-5], refs[-5:]
    features = left_ref.shape[1]
    at = 0
    for ref in lefts:
        left_ref[at : at + ref.shape[0]] = ref[:, :features]
        at += ref.shape[0]
    at = 0
    for ref in rights[:]:
        right_ref[at : at + ref.shape[0]] = ref[...]
        at += ref.shape[0]
    rows = left_ref.shape[0]
    tile, wide = tiles_ref.shape[1:]
    sent = []
    for group in range(right_ref.shape[0] // rows):
        right = slice(group * rows, (group + 1) * rows)
        for t in range(features // tile):
            cols = slice(t * tile, (t + 1) * tile)
            index = group * (features // tile) + t
            slot = index % tiles_ref.shape[0]
            if len(sent) >= tiles_ref.shape[0]:
                sent[index - tiles_ref.shape[0]].wait()
            tiles_ref[slot] = mm_tn(left_ref[:, cols], right_ref[right]).astype(bf16)
            target = out_ref.at[cols, group * wide : (group + 1) * wide]
            sent.append(start_copy(tiles_ref.at[slot], target, sems, slot))
    for copy in sent[-tiles_ref.shape[0] :]:
        copy.wait()


def weight_grad_call(lefts, rights):
    rows = sum(value.shape[0] for value in lefts)
    features, wide = lefts[0].shape[1] - EXTRA, rights[0].shape[1]
    held = sum(value.shape[0] for value in rights)
    tile = 256
    return pl.pallas_call(
        weight_grad_kernel,
        out_shape=hbm((features, held // rows * wide), bf16),
        in_specs=[in_vmem] * (len(lefts) + len(rights)),
        out_specs=anywhere,
        scratch_shapes=[
            pltpu.VMEM((rows, features), bf16),
            pltpu.VMEM((held, wide), bf16),
            pltpu.VMEM((3, tile, wide), bf16),
            pltpu.SemaphoreType.DMA((3,)),
        ],
        compiler_params=limits(16),
        name="weight_gradients",
    )(*lefts, *rights)


def exchange_wa(pick):
    return [pick(0)] + [swap(pick(i), "wa", i) for i in (1, 2, 3)]


def after(values, *done):
    kept = lax.optimization_barrier((values, done))
    return kept[0]


def key_blocks(kv, n):
    levels = [kv]
    for s in range(1, n // 2):
        levels.append(lax.ppermute(kv, "ctx", [(i, i + 2 * s) for i in range(n - 2 * s)]))
    blocks = []
    for level in levels:
        blocks += [level, swap(level, "ctx", 1)]
    return blocks


def sum_key_blocks(blocks, n):
    total = None
    for s in reversed(range(n // 2)):
        level = blocks[2 * s].astype(f32) + swap(blocks[2 * s + 1], "ctx", 1).astype(f32)
        if s:
            level = lax.ppermute(
                level.astype(bf16), "ctx", [(i + 2 * s, i) for i in range(n - 2 * s)]
            ).astype(f32)
        total = level if total is None else total + level
    return total


def sum_pairs(value, n):
    groups = [[2 * i + x for i in range(n // 2)] for x in range(2)]
    return lax.psum_scatter(
        value, "ctx", scatter_dimension=0, tiled=True, axis_index_groups=groups
    )


def per_device(
    tokens,
    teacher,
    lengths,
    routes,
    query_weight,
    key_projection_matrix,
    value_projection_matrix,
    output_weight,
    attn_gain,
    moe_gain,
    router_weight,
    shared_gate,
    shared_up,
    shared_down,
    expert_gate,
    expert_up,
    expert_down,
):
    w = lax.axis_index("wa")
    c = lax.axis_index("ctx")
    n = lax.axis_size("ctx")
    groups = lax.axis_size("wa")
    x, z, m = c % 2, c // 2, n // 2
    own_tokens = tokens[0]
    rows, features = own_tokens.shape
    slab = features // groups
    experts_all = router_weight.shape[1]
    length = jnp.sum(jnp.where(jnp.arange(lengths.shape[0]) == w, lengths, 0))
    count = jnp.sum(lengths).astype(f32)
    qpos = c * rows + jnp.arange(rows)
    width = KEY_VALUE_HEADS * HEAD_SIZE
    w_info = jnp.stack([w, x]).astype(jnp.int32)

    def columns(value, index):
        return lax.dynamic_slice_in_dim(value, index * slab, slab, 1)

    input_rows = own_tokens.astype(f32)
    factor_a = rms_factor(input_rows)
    far_half = lax.dynamic_slice_in_dim(own_tokens, (1 - w // 2) * 2 * slab, 2 * slab, 1)
    far_tokens = swap(far_half, "wa", 2)
    far_factor = swap(factor_a, "wa", 2)
    small = jnp.concatenate([router_weight.T, attn_gain[None], moe_gain[None]], axis=0)
    near_small = swap(small, "wa", 1)
    near_k = swap(key_projection_matrix, "wa", 1)
    near_v = swap(value_projection_matrix, "wa", 1)
    near_q = swap(query_weight, "wa", 1)

    gain_own = small[-2:-1].astype(f32)
    gain_near = near_small[-2:-1].astype(f32)
    core = w % 2

    def far_columns(index):
        return lax.dynamic_slice_in_dim(far_tokens, index * slab, slab, 1)

    part_own = jnp.concatenate([columns(own_tokens, w), far_columns(core)], axis=0)
    part_near = jnp.concatenate([columns(own_tokens, w ^ 1), far_columns(1 - core)], axis=0)
    both_factor = jnp.concatenate([factor_a, far_factor], axis=0)
    normed_own = (part_own.astype(f32) * both_factor * gain_own).astype(bf16)
    normed_near = (part_near.astype(f32) * both_factor * gain_near).astype(bf16)

    def project(weight_own, weight_near):
        partial = mm(normed_own, weight_own) + mm(normed_near, weight_near)
        return partial[:rows], partial[rows:].astype(bf16)

    k_own, k_far = project(key_projection_matrix, near_k)
    v_own, v_far = project(value_projection_matrix, near_v)
    kv_got = swap(jnp.concatenate([k_far, v_far], axis=1), "wa", 2)
    kv = (jnp.concatenate([k_own, v_own], axis=1) + kv_got.astype(f32)).astype(bf16)
    q_own, q_far = project(query_weight, near_q)
    q_got = swap(after(q_far, kv_got), "wa", 2)
    query_rows = (q_own + q_got.astype(f32)).astype(bf16)

    if n > 8:
        late = [kv_got]
    else:
        kv_all = key_blocks(kv, n)
        late = kv_all[:1] + kv_all[2::2] + [kv_all[1], q_got]

    far_small = swap(after(small, *late), "wa", 2)
    smalls = jnp.concatenate(
        perm4([small, near_small, far_small, swap(far_small, "wa", 1)], w), axis=1
    )
    router_t = jnp.pad(smalls[:experts_all], ((0, EXTRA - experts_all), (0, 0)))
    gain_a, gain_b = smalls[-2:-1].astype(f32), smalls[-1:].astype(f32)
    half_out = output_weight.shape[1] // 2
    own_out_weight = after(output_weight, kv_got)
    far_out = swap(lax.dynamic_slice_in_dim(own_out_weight, x * half_out, half_out, 1), "wa", 2)
    far_other = swap(far_out, "ctx", 1)
    output_parts = [
        output_weight,
        swap(output_weight, "wa", 1),
        far_out,
        swap(far_out, "wa", 1),
        far_other,
        swap(far_other, "wa", 1),
    ]
    shared_width = shared_gate.shape[1] // groups

    def shared_exchange(value):
        def pick(i):
            return lax.dynamic_slice_in_dim(value, (w ^ i) * shared_width, shared_width, 1)

        return exchange_wa(pick)

    shared_parts = [shared_exchange(after(value, kv_got)) for value in (shared_gate, shared_up)]
    query_rows = after(query_rows, *shared_parts, far_out)
    shared_parts.append(shared_exchange(after(shared_down, *late)))
    if n > 8:
        kv_all, pos = gather_keys(kv, c, n)
        q = heads(query_rows, GROUP)
        attn, kept_attn = attention_forward(q, kv_all, pos, qpos, length)
        attn = attn.reshape(rows, -1)
    else:
        first = [c, length]
        for s in range(m):
            first += [(c - 2 * s) * rows, (c - 2 * s + 1 - 2 * x) * rows]
        attn, kept_attn = attention_call(
            jnp.stack(first).astype(jnp.int32), query_rows, kv_all
        )
    attn_out = attn.astype(bf16)
    resid, row_ext, gates = branch_call(
        w_info, attn_out, output_parts, own_tokens, gain_b, router_t, routes[0]
    )

    shared_mine = [jnp.concatenate(perm4(parts, w)) for parts in shared_parts]
    weights = (expert_gate, expert_up, expert_down) + tuple(shared_mine)

    row_parts = [row_ext, swap(row_ext, "wa", 1), swap(row_ext, "wa", 2)]
    rows_own = swap(row_ext, "ctx", 1)
    done = [experts_call(w_info, row_parts[0], row_parts[1], weights)]
    row_parts[2] = after(row_parts[2], done[0][0], rows_own)
    row_parts.append(swap(row_parts[2], "wa", 1))
    rows_far = swap(row_parts[2], "ctx", 1)
    rows_pair = row_parts + [rows_own, swap(rows_own, "wa", 1), rows_far, swap(rows_far, "wa", 1)]
    done.append(experts_call(w_info, row_parts[2], row_parts[3], weights))

    def sum_wa(first_half, second_half):
        near = swap(first_half[1], "wa", 1)
        far = second_half[0] + swap(second_half[1], "wa", 1).astype(f32)
        return first_half[0], near, swap(far.astype(bf16), "wa", 2)

    own_out, near_out, far_out = sum_wa(done[0], done[1])
    gate_pre_pair, up_pre_pair, hidden_pair = pair_call(w_info, rows_pair[4:], weights)
    far_out = after(far_out, rows_far)
    scale = lengths.shape[0] * n * rows / count
    block_out, grad_result, grad_ext = result_call(
        jnp.stack([c * rows, length]).astype(jnp.int32), scale[None], resid, own_out, near_out, far_out, teacher[0]
    )
    grad_parts = [grad_ext, swap(grad_ext, "wa", 1), swap(grad_ext, "wa", 2)]
    pair_own = swap(grad_ext, "ctx", 1)

    grad_parts[2], pair_own = after((grad_parts[2], pair_own), hidden_pair)
    grad_parts.append(swap(grad_parts[2], "wa", 1))
    pair_far = swap(grad_parts[2], "ctx", 1)
    grads_pair = grad_parts + [pair_own, swap(pair_own, "wa", 1), pair_far, swap(pair_far, "wa", 1)]
    down_terms = weight_grad_call(grads_pair, [done[0][4], done[1][4], hidden_pair])

    kept = (done[0][2], done[1][2], done[0][3], done[1][3])
    first_grad = after(grad_parts[0], down_terms)
    back = experts_back_call(w_info, [first_grad] + grad_parts[1:], row_parts, kept, weights)
    own_back, near_back, far_back = sum_wa(back[:2], back[2:4])
    gate_pair, up_pair = pair_back_call(
        w_info, [after(grads_pair[4], back[0])] + grads_pair[5:], rows_pair[4:], gate_pre_pair, up_pre_pair, weights
    )
    pre_terms = weight_grad_call(rows_pair, [back[4], gate_pair, back[5], up_pair])
    far_back = after(far_back, pre_terms)
    grad_resid, gz, d_attn, small_b = resid_back_call(
        w_info, own_back, near_back, far_back, grad_result, resid, row_ext, gates, gain_b,
        router_t, output_parts, experts_all,
    )

    down_sum = sum_pairs(down_terms, n)

    def place(summed):
        fine_rows = features // n
        ours = lax.dynamic_slice_in_dim(summed, x * fine_rows, fine_rows, 0)
        other = lax.dynamic_slice_in_dim(summed, (1 - x) * fine_rows, fine_rows, 0)
        got = swap(other, "ctx", 1)
        first, second = jnp.where(x == 0, ours, got), jnp.where(x == 0, got, ours)
        units = expert_gate.shape[2]
        experts = [
            value[:, e * units : (e + 1) * units].astype(f32)
            for value in (first, second)
            for e in range(expert_gate.shape[0] // 2)
        ]
        used = expert_gate.shape[0] // 2 * units
        shared = jnp.concatenate([first[:, used:], second[:, used:]], axis=1)
        fine = fine_rows // groups

        def part(i):
            return lax.dynamic_slice_in_dim(shared, (w ^ i) * fine, fine, 0)

        shared = jnp.concatenate(perm4(exchange_wa(part), w), axis=1).astype(f32)
        return jnp.stack(experts), shared

    fine = features // n // groups

    def fine_exchange(value):
        blocks = jnp.transpose(value.reshape(-1, n, groups, fine), (2, 0, 1, 3))
        blocks = blocks.reshape(groups, -1, slab)
        return exchange_wa(lambda i: lax.dynamic_index_in_dim(blocks, w ^ i, 0, keepdims=False))

    attn_in = (input_rows * factor_a * gain_a).astype(bf16)
    attn_in_fine = jnp.concatenate(fine_exchange(attn_in))
    attn_out_parts = jnp.concatenate(gather_wa(attn_out))
    gz_fine = jnp.concatenate(fine_exchange(gz))

    def fold_rows(value):
        blocks = value.astype(bf16).reshape(m, 2, fine, value.shape[1])
        mine = lax.dynamic_index_in_dim(blocks, x, 1, keepdims=False)
        got = swap(lax.dynamic_index_in_dim(blocks, 1 - x, 1, keepdims=False), "ctx", 1)
        summed = (mine.astype(f32) + got.astype(f32)).astype(bf16)
        return summed.reshape(m * fine, -1)

    grad_output = fold_rows(mm_tn(gz_fine, attn_out_parts))

    if n > 8:
        d_heads = heads(d_attn, GROUP)
        delta = jnp.sum(d_heads.astype(f32) * heads(attn, GROUP), axis=-1)
        delta = jnp.transpose(delta, (1, 2, 0))[..., None]
        d_q, d_kv = attention_backward(q, kv_all, pos, qpos, length, kept_attn, d_heads, delta)
        d_q = d_q.reshape(rows, -1).astype(bf16)
        d_kv = scatter_keys(d_kv, n).astype(bf16)
    else:
        d_q, d_kv = attention_back_call(query_rows, d_attn, attn, kept_attn, kv_all)
        d_kv = sum_key_blocks(d_kv, n).astype(bf16)
    d_q_parts = gather_wa(d_q)
    pre_sum = sum_pairs(after(pre_terms, down_sum), n)
    gate_sum, up_sum = jnp.split(pre_sum, 2, axis=1)
    grad_query = fold_rows(mm_tn(attn_in_fine, jnp.concatenate(d_q_parts)))
    d_kv = after(d_kv, grad_query, grad_output)
    d_kv_parts = gather_wa(d_kv)

    both_d_q = jnp.concatenate([d_q, d_q_parts[2]])
    both_d_kv = jnp.concatenate([d_kv, d_kv_parts[2]])
    both_d_k, both_d_v = both_d_kv[:, :width], both_d_kv[:, width:]

    def back_through(q_weight, k_weight, v_weight):
        return mm_nt(both_d_q, q_weight) + mm_nt(both_d_k, k_weight) + mm_nt(both_d_v, v_weight)

    back_own = back_through(query_weight, key_projection_matrix, value_projection_matrix)
    back_near = back_through(near_q, near_k, near_v)
    returned = swap(
        jnp.concatenate([back_own[rows:], back_near[rows:]], axis=1).astype(bf16), "wa", 2
    ).astype(f32)
    grad_attn_in = jnp.concatenate(
        perm4([back_own[:rows], back_near[:rows], returned[:, :slab], returned[:, slab:]], w),
        axis=1,
    )
    grad_norm_a, grad_gain_a = norm_backward(input_rows, factor_a, gain_a, grad_attn_in)
    grad_tokens = grad_resid + grad_norm_a

    smalls_grad = jnp.concatenate([small_b[: experts_all + 1], grad_gain_a[None]], axis=0)
    parts = fine_exchange(smalls_grad)
    small_sum = (parts[0] + parts[1] + parts[2] + parts[3]).T
    grad_kv = mm_tn(attn_in_fine, jnp.concatenate(d_kv_parts))
    kv_small = fold_rows(jnp.concatenate([grad_kv, small_sum], axis=1))
    loss_part = jnp.sum(sum(part[:, features:].astype(f32) for part in grads_pair))
    high = lax.optimization_barrier(loss_part.astype(bf16))
    low = (loss_part - high.astype(f32)).astype(bf16)
    place_z = (jnp.arange(m) == z).astype(bf16)
    loss_row = jnp.concatenate([place_z * high, place_z * low])
    loss_columns = jnp.broadcast_to(loss_row, (m * fine, 2 * m))
    ends = [output_weight.shape[1], query_weight.shape[1], 2 * width, experts_all, 1, 1, 2 * m]
    dense_terms = jnp.concatenate([grad_output, grad_query, kv_small, loss_columns], axis=1)
    dense = sum_pairs(after(dense_terms, pre_sum), n).astype(f32)
    pieces, at = [], 0
    for size in ends:
        pieces.append(dense[:, at : at + size])
        at += size
    loss = jnp.sum(pieces[6][0]) / (2.0 * features * count)
    grad_expert_down, grad_shared_down = place(down_sum)
    grad_expert_gate, grad_shared_gate = place(gate_sum)
    grad_expert_up, grad_shared_up = place(up_sum)

    return (
        block_out[None],
        grad_tokens[None],
        pieces[1],
        pieces[2][:, :width],
        pieces[2][:, width:],
        pieces[0],
        pieces[5][:, 0],
        pieces[4][:, 0],
        pieces[3],
        grad_shared_gate,
        grad_shared_up,
        grad_shared_down,
        grad_expert_gate,
        grad_expert_up,
        grad_expert_down,
        loss,
    )


def solution(mesh):
    return jax.shard_map(
        per_device,
        mesh=mesh,
        in_specs=(
            P("wa", "ctx", None),
            P("wa", "ctx", None),
            P(),
            P("wa", "ctx", None),
            P("wa", None),
            P("wa", None),
            P("wa", None),
            P("wa", None),
            P("wa"),
            P("wa"),
            P("wa", None),
            P("wa", None),
            P("wa", None),
            P("wa", None),
            P("wa", None, None),
            P("wa", None, None),
            P("wa", None, None),
        ),
        out_specs=(
            P("wa", "ctx", None),
            P("wa", "ctx", None),
            P(("ctx", "wa"), None),
            P(("ctx", "wa"), None),
            P(("ctx", "wa"), None),
            P(("ctx", "wa"), None),
            P(("ctx", "wa")),
            P(("ctx", "wa")),
            P(("ctx", "wa"), None),
            P(("ctx", "wa"), None),
            P(("ctx", "wa"), None),
            P(("ctx", "wa"), None),
            P("wa", "ctx", None),
            P("wa", "ctx", None),
            P("wa", "ctx", None),
            P(),
        ),
        check_vma=False,
    )
```

```python
import jax
import jax.numpy as jnp
from jax import lax
from jax.experimental import pallas as pl
from jax.experimental.pallas import tpu as pltpu
from jax.sharding import PartitionSpec as P

QUERY_HEADS = 12
KEY_VALUE_HEADS = 4
HEAD_SIZE = 128
TOP = 6
GROUP = QUERY_HEADS // KEY_VALUE_HEADS

epsilon = 1e-06
masked = -1e30
bf16 = jnp.bfloat16
f32 = jnp.float32


def dot(a, b, dims):
    return lax.dot_general(a, b, ((dims[0], dims[1]), ((), ())), preferred_element_type=f32)


def mm(a, b):
    return dot(a, b, ((1,), (0,)))


def mm_nt(a, b):
    return dot(a, b, ((1,), (1,)))


def mm_tn(a, b):
    return dot(a, b, ((0,), (0,)))


def swap(value, axis, bit):
    size = lax.axis_size(axis)
    return lax.ppermute(value, axis, [(i, i ^ bit) for i in range(size)])


def perm4(parts, w):
    core, upper = w % 2 == 1, w // 2 == 1
    a, b, c, d = parts
    a, b, c, d = (
        jnp.where(core, b, a),
        jnp.where(core, a, b),
        jnp.where(core, d, c),
        jnp.where(core, c, d),
    )
    return [
        jnp.where(upper, c, a),
        jnp.where(upper, d, b),
        jnp.where(upper, a, c),
        jnp.where(upper, b, d),
    ]


def gather_wa(value):
    near = swap(value, "wa", 1)
    far = swap(value, "wa", 2)
    return [value, near, far, swap(far, "wa", 1)]


def silu_parts(rows):
    sigma = jax.nn.sigmoid(rows)
    return rows * sigma, sigma * (1.0 + rows * (1.0 - sigma))


def rms_factor(rows):
    return lax.rsqrt(jnp.mean(rows * rows, axis=-1, keepdims=True) + epsilon)


def norm_backward(rows, factor, gain, upstream):
    weighted = upstream * gain
    inner = jnp.mean(weighted * rows, axis=-1, keepdims=True)
    grad = factor * weighted - rows * (factor * factor * factor * inner)
    return grad, jnp.sum(upstream * rows * factor, axis=0)


def gather_keys(kv, c, n):
    rows = kv.shape[0]
    if n > 8:
        return lax.all_gather(kv, "ctx", axis=0, tiled=True), jnp.arange(n * rows)
    levels = [kv]
    for s in range(1, n // 2):
        levels.append(lax.ppermute(kv, "ctx", [(i, i + 2 * s) for i in range(n - 2 * s)]))
    blocks, pos = [], []
    for s, level in enumerate(levels):
        blocks += [level, swap(level, "ctx", 1)]
        start = (c - 2 * s) * rows
        pos += [start + jnp.arange(rows), (c - 2 * s + 1 - 2 * (c % 2)) * rows + jnp.arange(rows)]
    return jnp.concatenate(blocks), jnp.concatenate(pos)


def scatter_keys(grads, n):
    rows = grads.shape[0] // n
    if n > 8:
        return lax.psum_scatter(grads, "ctx", scatter_dimension=0, tiled=True).astype(f32)
    blocks = grads.reshape(n, rows, -1)
    total = None
    for s in reversed(range(n // 2)):
        level = blocks[2 * s].astype(f32) + swap(blocks[2 * s + 1], "ctx", 1).astype(f32)
        if s:
            level = lax.ppermute(
                level.astype(bf16), "ctx", [(i + 2 * s, i) for i in range(n - 2 * s)]
            ).astype(f32)
        total = level if total is None else total + level
    return total


def heads(rows, groups):
    return rows.reshape(rows.shape[0], KEY_VALUE_HEADS, groups, HEAD_SIZE)


def attention_scores(q, k, pos, qpos, length):
    scale = HEAD_SIZE**-0.5
    scores = jnp.einsum("tkgd,nkd->kgtn", q, k, preferred_element_type=f32) * scale
    allowed = (pos[None, :] >= 0) & (pos[None, :] <= qpos[:, None]) & (pos[None, :] < length)
    return scores, allowed


def chunked(kv, pos):
    size = 1024
    if kv.shape[0] <= size:
        return None
    return kv.reshape(-1, size, kv.shape[1]), pos.reshape(-1, size)


def attention_forward(q, kv, pos, qpos, length):
    rows = q.shape[0]
    pieces = chunked(kv, pos)
    width = KEY_VALUE_HEADS * HEAD_SIZE
    if pieces is None:
        k, v = heads(kv[:, :width], 1)[:, :, 0], heads(kv[:, width:], 1)[:, :, 0]
        scores, allowed = attention_scores(q, k, pos, qpos, length)
        scores = jnp.where(allowed, scores, masked)
        top = jnp.max(scores, axis=-1, keepdims=True)
        weights = jnp.exp(scores - top)
        probs = (weights / jnp.sum(weights, axis=-1, keepdims=True)).astype(bf16)
        attn = jnp.einsum("kgtn,nkd->tkgd", probs, v, preferred_element_type=f32)
        return attn, probs

    def step(carry, piece):
        top, total, accum = carry
        kv_now, pos_now = piece
        k, v = heads(kv_now[:, :width], 1)[:, :, 0], heads(kv_now[:, width:], 1)[:, :, 0]
        scores, allowed = attention_scores(q, k, pos_now, qpos, length)
        scores = jnp.where(allowed, scores, masked)
        new_top = jnp.maximum(top, jnp.max(scores, axis=-1, keepdims=True))
        weights = jnp.where(allowed, jnp.exp(scores - new_top), 0.0)
        shrink = jnp.exp(top - new_top)
        total = total * shrink + jnp.sum(weights, axis=-1, keepdims=True)
        update = jnp.einsum("kgtn,nkd->kgtd", weights.astype(bf16), v, preferred_element_type=f32)
        return (new_top, total, accum * shrink + update), None

    shape = (KEY_VALUE_HEADS, GROUP, rows)
    start = (
        jnp.full(shape + (1,), masked, f32),
        jnp.zeros(shape + (1,), f32),
        jnp.zeros(shape + (HEAD_SIZE,), f32),
    )
    (top, total, accum), _ = lax.scan(step, start, pieces)
    return jnp.transpose(accum / total, (2, 0, 1, 3)), top + jnp.log(total)


def attention_backward(q, kv, pos, qpos, length, kept, d_attn, delta):
    scale = HEAD_SIZE**-0.5
    width = KEY_VALUE_HEADS * HEAD_SIZE

    def terms(probs, k, v):
        d_probs = jnp.einsum("tkgd,nkd->kgtn", d_attn, v, preferred_element_type=f32)
        d_scores = (probs.astype(f32) * (d_probs - delta)).astype(bf16)
        d_q = jnp.einsum("kgtn,nkd->tkgd", d_scores, k, preferred_element_type=f32) * scale
        d_k = jnp.einsum("kgtn,tkgd->nkd", d_scores, q, preferred_element_type=f32) * scale
        d_v = jnp.einsum(
            "kgtn,tkgd->nkd", probs.astype(bf16), d_attn, preferred_element_type=f32
        )
        keys = k.shape[0]
        return d_q, jnp.concatenate(
            [d_k.reshape(keys, width), d_v.reshape(keys, width)], axis=1
        ).astype(bf16)

    pieces = chunked(kv, pos)
    if pieces is None:
        k, v = heads(kv[:, :width], 1)[:, :, 0], heads(kv[:, width:], 1)[:, :, 0]
        return terms(kept, k, v)

    def step(d_q, piece):
        kv_now, pos_now = piece
        k, v = heads(kv_now[:, :width], 1)[:, :, 0], heads(kv_now[:, width:], 1)[:, :, 0]
        scores, allowed = attention_scores(q, k, pos_now, qpos, length)
        probs = jnp.where(allowed, jnp.exp(scores - kept), 0.0)
        more, d_kv = terms(probs, k, v)
        return d_q + more, d_kv

    d_q, d_kv = lax.scan(step, jnp.zeros(q.shape, f32), pieces)
    return d_q, d_kv.reshape(kv.shape)


EXTRA = 128
in_vmem = pl.BlockSpec(memory_space=pltpu.VMEM)
in_smem = pl.BlockSpec(memory_space=pltpu.SMEM)
anywhere = pl.BlockSpec(memory_space=pltpu.MemorySpace.HBM)


def hbm(shape, dtype):
    return pltpu.HBM(shape, dtype)


def in_hbm(value):
    return pltpu.with_memory_space_constraint(value, pltpu.HBM)


def start_copy(source, target, sems, index):
    copy = pltpu.make_async_copy(source, target, sems.at[index])
    copy.start()
    return copy


def cost(microseconds):
    return pl.CostEstimate(flops=int(microseconds * 1.15e+09), bytes_accessed=0, transcendentals=0)


def limits(mib):
    return pltpu.CompilerParams(vmem_limit_bytes=mib << 20)


def split_low(value, lane, shift):
    high = value.astype(bf16).astype(f32)
    rest = pltpu.roll(value - high, shift, 1)
    return jnp.where(lane < shift, high, jnp.where(lane < 2 * shift, rest, 0.0))


def join_low(value, lane, shift):
    total = value + pltpu.roll(value, value.shape[1] - shift, 1)
    return jnp.where(lane < shift, total, 0.0)


def lanes_of(rows):
    return lax.broadcasted_iota(jnp.int32, (rows, EXTRA), 1)


def load_rows(sources, rows_ref, extra_ref, sems, first):
    features, copies = rows_ref.shape[1], []
    for i, source in enumerate(sources):
        at = pl.ds(i * source.shape[0], source.shape[0])
        copies.append(
            start_copy(source.at[:, pl.ds(0, features)], rows_ref.at[at], sems, first + 2 * i)
        )
        if extra_ref is not None:
            lanes = pl.ds(features, EXTRA)
            copies.append(
                start_copy(source.at[:, lanes], extra_ref.at[at], sems, first + 2 * i + 1)
            )
    return copies


def wait_all(copies):
    for copy in copies:
        copy.wait()


def attention_kernel(info_ref, q_ref, *refs):
    blocks = len(refs) - 6
    kv_refs, (out_ref, attn_out, probs_out, attn_ref, probs_ref, sems) = refs[:blocks], refs[blocks:]
    sent = []
    rows = q_ref.shape[0]
    width = KEY_VALUE_HEADS * HEAD_SIZE
    qpos = info_ref[0] * rows + lax.broadcasted_iota(jnp.int32, (rows, rows), 0)
    biases = []
    for b in range(blocks):
        kpos = info_ref[2 + b] + lax.broadcasted_iota(jnp.int32, (rows, rows), 1)
        allowed = (kpos >= 0) & (kpos <= qpos) & (kpos < info_ref[1])
        bias = jnp.where(allowed, 0.0, masked)
        biases.append(jnp.concatenate([bias] * GROUP, axis=0))
    for k in range(KEY_VALUE_HEADS):
        first = k * GROUP * HEAD_SIZE
        q = jnp.concatenate(
            [q_ref[:, first + g * HEAD_SIZE : first + (g + 1) * HEAD_SIZE] for g in range(GROUP)],
            axis=0,
        )
        cols = slice(k * HEAD_SIZE, (k + 1) * HEAD_SIZE)
        scores = [
            mm_nt(q, kv_refs[b][:, cols]) * HEAD_SIZE**-0.5 + biases[b] for b in range(blocks)
        ]
        top = scores[0]
        for score in scores[1:]:
            top = jnp.maximum(top, score)
        top = jnp.max(top, axis=1, keepdims=True)
        weights = [jnp.exp(score - top) for score in scores]
        total = weights[0]
        for weight in weights[1:]:
            total = total + weight
        scale = 1.0 / jnp.sum(total, axis=1, keepdims=True)
        attn = None
        for b in range(blocks):
            probs = (weights[b] * scale).astype(bf16)
            probs_ref[k, b] = probs
            term = mm(probs, kv_refs[b][:, width + k * HEAD_SIZE : width + (k + 1) * HEAD_SIZE])
            attn = term if attn is None else attn + term
        sent.append(start_copy(probs_ref.at[k], probs_out.at[k], sems, k))
        for g in range(GROUP):
            at = slice(first + g * HEAD_SIZE, first + (g + 1) * HEAD_SIZE)
            attn_ref[:, at] = attn[g * rows : (g + 1) * rows]
            out_ref[:, at] = attn[g * rows : (g + 1) * rows].astype(bf16)
    sent.append(start_copy(attn_ref, attn_out, sems, KEY_VALUE_HEADS))
    wait_all(sent)


def attention_call(info, q, kv_blocks):
    rows, blocks = q.shape[0], len(kv_blocks)
    probs = (KEY_VALUE_HEADS, blocks, GROUP * rows, rows)
    return pl.pallas_call(
        attention_kernel,
        out_shape=(jax.ShapeDtypeStruct(q.shape, bf16), hbm(q.shape, f32), hbm(probs, bf16)),
        in_specs=[in_smem] + [in_vmem] * (1 + blocks),
        out_specs=(in_vmem, anywhere, anywhere),
        scratch_shapes=[
            pltpu.VMEM(q.shape, f32),
            pltpu.VMEM(probs, bf16),
            pltpu.SemaphoreType.DMA((KEY_VALUE_HEADS + 1,)),
        ],
        compiler_params=limits(12),
        cost_estimate=cost(5),
        name="attention_forward",
    )(info, q, *kv_blocks)


def attention_back_kernel(d_ref, q_in, attn_in, probs_in, *refs):
    blocks = (len(refs) - 6) // 2
    kv_in, refs = refs[:blocks], refs[blocks:]
    dq_ref, refs = refs[0], refs[1:]
    own_refs, pair_refs, refs = refs[: blocks // 2], refs[blocks // 2 : blocks], refs[blocks:]
    q_ref, attn_ref, probs_ref, kv_ref, sems = refs
    rows = q_ref.shape[0]
    width = KEY_VALUE_HEADS * HEAD_SIZE
    scale = HEAD_SIZE**-0.5
    loads = [start_copy(q_in, q_ref, sems, 0), start_copy(attn_in, attn_ref, sems, 1)]
    loads += [start_copy(kv_in[b], kv_ref.at[b], sems, 2 + b) for b in range(blocks)]
    probs_loads = [
        start_copy(probs_in.at[k], probs_ref.at[k], sems, 2 + blocks + k)
        for k in range(KEY_VALUE_HEADS)
    ]
    wait_all(loads)

    def stacked(ref, first):
        return jnp.concatenate(
            [ref[:, first + g * HEAD_SIZE : first + (g + 1) * HEAD_SIZE] for g in range(GROUP)],
            axis=0,
        )

    for k in range(KEY_VALUE_HEADS):
        first = k * GROUP * HEAD_SIZE
        q, d_attn = stacked(q_ref, first), stacked(d_ref, first)
        delta = jnp.sum(d_attn.astype(f32) * stacked(attn_ref, first), axis=1, keepdims=True)
        kcols = slice(k * HEAD_SIZE, (k + 1) * HEAD_SIZE)
        vcols = slice(width + k * HEAD_SIZE, width + (k + 1) * HEAD_SIZE)
        probs_loads[k].wait()
        d_q = None
        for b in range(blocks):
            key, value = kv_ref[b, :, kcols], kv_ref[b, :, vcols]
            probs = probs_ref[k, b]
            d_probs = mm_nt(d_attn, value)
            d_scores = (probs.astype(f32) * (d_probs - delta)).astype(bf16)
            term = mm(d_scores, key)
            d_q = term if d_q is None else d_q + term
            level = b // 2
            target = own_refs[level] if b % 2 == 0 else pair_refs[level]
            target[:, kcols] = (mm_tn(d_scores, q) * scale).astype(bf16)
            target[:, vcols] = mm_tn(probs, d_attn).astype(bf16)
        d_q = (d_q * scale).astype(bf16)
        for g in range(GROUP):
            dq_ref[:, first + g * HEAD_SIZE : first + (g + 1) * HEAD_SIZE] = d_q[
                g * rows : (g + 1) * rows
            ]


def attention_back_call(d_attn, q, attn, probs, kv_blocks):
    blocks = len(kv_blocks)
    kv_shape = kv_blocks[0].shape
    done = pl.pallas_call(
        attention_back_kernel,
        out_shape=(jax.ShapeDtypeStruct(q.shape, bf16),)
        + (jax.ShapeDtypeStruct(kv_shape, bf16),) * blocks,
        in_specs=[in_vmem] + [anywhere] * (3 + blocks),
        out_specs=(in_vmem,) * (1 + blocks),
        scratch_shapes=[
            pltpu.VMEM(q.shape, bf16),
            pltpu.VMEM(q.shape, f32),
            pltpu.VMEM(probs.shape, bf16),
            pltpu.VMEM((blocks,) + kv_shape, bf16),
            pltpu.SemaphoreType.DMA((2 + blocks + KEY_VALUE_HEADS,)),
        ],
        compiler_params=limits(16),
        cost_estimate=cost(10),
        name="attention_backward",
    )(d_attn, in_hbm(q), in_hbm(attn), in_hbm(probs), *[in_hbm(value) for value in kv_blocks])
    return done[0], list(done[1 : 1 + blocks // 2]), list(done[1 + blocks // 2 :])


def out_halves(info_ref, size):
    half = info_ref[2]
    return (
        pl.ds(pl.multiple_of(half * size, 128), size),
        pl.ds(pl.multiple_of((1 - half) * size, 128), size),
    )


def branch_kernel(
    info_ref, attn_ref, o0, o1, o2, o3, tok_ref, gain_ref, router_ref, routes_ref,
    resid_out, ext_ref, gates_ref, resid_ref, sems,
):
    rows, features = tok_ref.shape
    slab = o0.shape[0]
    here, other = out_halves(info_ref, o2.shape[1])
    attn = attn_ref[...]
    for i in range(4):
        if i < 2:
            term = mm_nt(attn, (o0, o1)[i][...])
        else:
            part = (o2, o3)[i - 2]
            term = mm_nt(attn_ref[:, here], part[:slab]) + mm_nt(attn_ref[:, other], part[slab:])
        at = pl.ds(pl.multiple_of((info_ref[0] ^ i) * slab, 128), slab)
        resid_ref[:, at] = tok_ref[:, at].astype(f32) + term
    sent = start_copy(resid_ref, resid_out, sems, 0)
    resid = resid_ref[...]
    moe_in = (resid * rms_factor(resid) * gain_ref[...]).astype(bf16)
    logits = mm_nt(moe_in, router_ref[...])
    lane = lanes_of(rows)
    chosen = lane == routes_ref[:, 0:1]
    for t in range(1, routes_ref.shape[1]):
        chosen = chosen | (lane == routes_ref[:, t : t + 1])
    logits = jnp.where(chosen, logits, masked)
    raised = jnp.where(chosen, jnp.exp(logits - jnp.max(logits, axis=1, keepdims=True)), 0.0)
    gates = raised / jnp.sum(raised, axis=1, keepdims=True)
    gates_ref[...] = gates
    ext_ref[:, :features] = moe_in
    ext_ref[:, features:] = split_low(gates, lane, 16).astype(bf16)
    sent.wait()


def branch_call(info, attn, output_parts, own_tokens, gain, router, routes):
    rows, features = own_tokens.shape
    return pl.pallas_call(
        branch_kernel,
        out_shape=(
            hbm((rows, features), f32),
            jax.ShapeDtypeStruct((rows, features + EXTRA), bf16),
            jax.ShapeDtypeStruct((rows, EXTRA), f32),
        ),
        in_specs=[in_smem] + [in_vmem] * 9,
        out_specs=(anywhere, in_vmem, in_vmem),
        scratch_shapes=[pltpu.VMEM((rows, features), f32), pltpu.SemaphoreType.DMA((1,))],
        compiler_params=limits(12),
        cost_estimate=cost(4.5),
        name="branch_and_router",
    )(info, attn, *output_parts, own_tokens, gain, router, routes)


def result_kernel(info_ref, scale_ref, resid_in, own_in, teacher_in, near_ref, far_ref,
                  out_hbm, grad_hbm, ext_ref,
                  resid_ref, own_ref, teacher_ref, out_ref, grad_ref, sems):
    loads = [
        start_copy(source, target, sems, i)
        for i, (source, target) in enumerate(
            [(resid_in, resid_ref), (own_in, own_ref), (teacher_in, teacher_ref)]
        )
    ]
    rows, features = resid_ref.shape
    wait_all(loads)
    result = (
        resid_ref[...]
        + own_ref[...]
        + near_ref[...].astype(f32)
        + far_ref[...].astype(f32)
    )
    out_ref[...] = result.astype(bf16)
    sent = [start_copy(out_ref, out_hbm, sems, 3)]
    qpos = info_ref[0] * rows + lax.broadcasted_iota(jnp.int32, (rows, 1), 0)
    error = jnp.where(qpos < info_ref[1], result - teacher_ref[...], 0.0)
    grad = error * scale_ref[0]
    grad_ref[...] = grad
    sent.append(start_copy(grad_ref, grad_hbm, sems, 4))
    ext_ref[:, :features] = grad.astype(bf16)
    lane = lanes_of(rows)
    row_loss = jnp.where(lane == 0, jnp.sum(error * error, axis=1, keepdims=True), 0.0)
    ext_ref[:, features:] = split_low(row_loss, lane, 16).astype(bf16)
    wait_all(sent)


def result_call(info, scale, resid, own, near, far, teacher):
    rows, features = resid.shape
    flat = (rows, features)
    return pl.pallas_call(
        result_kernel,
        out_shape=(
            hbm(flat, bf16),
            hbm(flat, f32),
            jax.ShapeDtypeStruct((rows, features + EXTRA), bf16),
        ),
        in_specs=[in_smem] * 2 + [anywhere] * 3 + [in_vmem] * 2,
        out_specs=(anywhere, anywhere, in_vmem),
        scratch_shapes=[pltpu.VMEM(flat, f32)] * 3
        + [pltpu.VMEM(flat, bf16), pltpu.VMEM(flat, f32), pltpu.SemaphoreType.DMA((5,))],
        compiler_params=limits(12),
        cost_estimate=cost(3.5),
        name="result_and_error",
    )(info, scale, in_hbm(resid), in_hbm(own), in_hbm(teacher), near, far)


def resid_back_kernel(info_ref, far_ref, gain_ref, *refs):
    sources, refs = refs[:11], refs[11:]
    (out_hbm, gz_ref, d_attn_ref, small_ref), refs = refs[:4], refs[4:]
    held, (out_ref, sum_ref, sems) = refs[:11], refs[11:]
    loads = [
        start_copy(source, target, sems, i)
        for i, (source, target) in enumerate(zip(sources, held, strict=True))
    ]
    own_ref, near_ref, grad_ref, resid_ref, ext_ref, gates_ref, router_ref, o0, o1, o2, o3 = held
    rows, features = resid_ref.shape
    slab = o0.shape[0]
    lane = lanes_of(rows)
    tail = slice(features, features + EXTRA)
    wait_all(loads[:7])
    d_gate = join_low(
        own_ref[:, tail] + near_ref[:, tail].astype(f32) + far_ref[:, tail].astype(f32), lane, 16
    )
    gates = gates_ref[...]
    d_logits = gates * (d_gate - jnp.sum(gates * d_gate, axis=1, keepdims=True))
    d_logits = d_logits.astype(bf16)
    body = slice(0, features)
    upstream = (
        own_ref[:, body]
        + near_ref[:, body].astype(f32)
        + far_ref[:, body].astype(f32)
        + mm(d_logits, router_ref[...])
    )
    resid = resid_ref[...]
    grad_norm, grad_gain = norm_backward(resid, rms_factor(resid), gain_ref[...], upstream)
    experts = small_ref.shape[0] - 8
    small_ref[:experts, :] = mm_tn(d_logits, ext_ref[:, body])[:experts]
    small_ref[experts:, :] = jnp.broadcast_to(grad_gain[None], (8, features))
    grad_resid = grad_ref[...] + grad_norm
    out_ref[...] = grad_resid
    sent = start_copy(out_ref, out_hbm, sems, len(sources))
    gz_ref[...] = grad_resid.astype(bf16)
    gz = [
        gz_ref[:, pl.ds(pl.multiple_of((info_ref[0] ^ i) * slab, 128), slab)] for i in range(4)
    ]
    wait_all(loads[7:])
    sum_ref[...] = mm(gz[0], o0[...]) + mm(gz[1], o1[...])
    here, other = out_halves(info_ref, o2.shape[1])
    sum_ref[:, here] += mm(gz[2], o2[:slab]) + mm(gz[3], o3[:slab])
    sum_ref[:, other] += mm(gz[2], o2[slab:]) + mm(gz[3], o3[slab:])
    d_attn_ref[...] = sum_ref[...].astype(bf16)
    sent.wait()


def resid_back_call(info, own, near, far, grad, resid, ext, gates, gain, router, output_parts, experts):
    rows, features = resid.shape
    sources = [own, near, grad, resid, ext, gates, router, *output_parts]
    heads_wide = output_parts[0].shape[1]
    return pl.pallas_call(
        resid_back_kernel,
        out_shape=(
            hbm((rows, features), f32),
            jax.ShapeDtypeStruct((rows, features), bf16),
            jax.ShapeDtypeStruct((rows, heads_wide), bf16),
            jax.ShapeDtypeStruct((experts + 8, features), f32),
        ),
        in_specs=[in_smem] + [in_vmem] * 2 + [anywhere] * len(sources),
        out_specs=(anywhere,) + (in_vmem,) * 3,
        scratch_shapes=[pltpu.VMEM(value.shape, value.dtype) for value in sources]
        + [
            pltpu.VMEM((rows, features), f32),
            pltpu.VMEM((rows, heads_wide), f32),
            pltpu.SemaphoreType.DMA((len(sources) + 1,)),
        ],
        compiler_params=limits(20),
        cost_estimate=cost(5),
        name="residual_backward",
    )(info, far, gain, *[in_hbm(value) for value in sources])


def gate_column(extra, lane, expert):
    here = (lane == expert) | (lane == expert + 16)
    return jnp.sum(jnp.where(here, extra, 0.0), axis=1, keepdims=True)


def shared_parts_of(shared_ref):
    width = shared_ref.shape[1] // 3
    return [shared_ref[:, i * width : (i + 1) * width] for i in range(3)]


def experts_kernel(info_ref, xa_ref, xb_ref, gate_ref, up_ref, down_ref, shared_ref,
                   outa_hbm, outb_ref, gp_out, upre_out, hid_out,
                   gp_ref, upre_ref, hid_ref, x_ref, acc_ref, sems):
    rows, features = outb_ref.shape
    here, _, width = gate_ref.shape
    x_ref[:rows] = xa_ref[:, :features]
    x_ref[rows:] = xb_ref[:, :features]
    extra = jnp.concatenate([xa_ref[:, features:], xb_ref[:, features:]], axis=0).astype(f32)
    lane = lanes_of(2 * rows)

    def unit(gate_w, up_w):
        gate_pre, up_pre = mm(x_ref[...], gate_w), mm(x_ref[...], up_w)
        return gate_pre, up_pre, gate_pre * jax.nn.sigmoid(gate_pre) * up_pre

    s_gate, s_up, s_down = shared_parts_of(shared_ref)
    gate_pre, up_pre, hidden = unit(s_gate, s_up)
    hidden = hidden.astype(bf16)
    acc_ref[...] = mm_nt(hidden, s_down)
    part = hidden.shape[1] // 2
    for half in range(2):
        cols, mine = slice(2 * width, 2 * width + part), slice(half * part, (half + 1) * part)
        gp_ref[half, :, cols] = gate_pre[:, mine].astype(bf16)
        upre_ref[half, :, cols] = up_pre[:, mine].astype(bf16)
        hid_ref[info_ref[1] ^ half, :, cols] = hidden[:, mine]
    sent = []
    for e in range(here):
        gate = gate_column(extra, lane, info_ref[0] * here + e)
        gate_pre, up_pre, hidden = unit(gate_ref[e], up_ref[e])
        hidden = (hidden * gate).astype(bf16)
        half, at = e // 2, (e % 2) * width
        cols = slice(at, at + width)
        gp_ref[half, :, cols] = gate_pre.astype(bf16)
        upre_ref[half, :, cols] = up_pre.astype(bf16)
        hid_ref[info_ref[1] ^ half, :, cols] = hidden
        if e % 2:
            sent.append(start_copy(gp_ref.at[half], gp_out.at[half], sems, 2 * half))
            sent.append(start_copy(upre_ref.at[half], upre_out.at[half], sems, 2 * half + 1))
        if e + 1 == here:
            sent.append(start_copy(hid_ref.at[0], hid_out, sems, 4))
        acc_ref[...] += mm_nt(hidden, down_ref[e])
    outb_ref[...] = acc_ref[rows:].astype(bf16)
    sent.append(start_copy(acc_ref.at[pl.ds(0, rows)], outa_hbm, sems, 5))
    wait_all(sent)


def experts_call(info, xa, xb, weights):
    rows, features = xa.shape[0], xa.shape[1] - EXTRA
    wide = 2 * weights[0].shape[2] + weights[3].shape[1] // 6
    both, half = hbm((2, 2 * rows, wide), bf16), hbm((2 * rows, wide), bf16)
    return pl.pallas_call(
        experts_kernel,
        out_shape=(
            hbm((rows, features), f32),
            jax.ShapeDtypeStruct((rows, features), bf16),
            both,
            both,
            half,
        ),
        in_specs=[in_smem] + [in_vmem] * 6,
        out_specs=(anywhere, in_vmem) + (anywhere,) * 3,
        scratch_shapes=[pltpu.VMEM(both.shape, bf16)] * 3
        + [
            pltpu.VMEM((2 * rows, features), bf16),
            pltpu.VMEM((2 * rows, features), f32),
            pltpu.SemaphoreType.DMA((6,)),
        ],
        compiler_params=limits(16),
        cost_estimate=cost(8),
        name="experts_forward",
    )(info, xa, xb, *weights)


def hidden_back(d_hidden, gate_pre, up_pre, gate):
    gate_pre, up_pre = gate_pre.astype(f32), up_pre.astype(f32)
    act, slope = silu_parts(gate_pre)
    d_gate = None
    if gate is not None:
        d_gate = jnp.sum(d_hidden * act * up_pre, axis=1, keepdims=True)
        d_hidden = d_hidden * gate
    return d_gate, (d_hidden * up_pre * slope).astype(bf16), (d_hidden * act).astype(bf16)


def experts_back_kernel(info_ref, *refs):
    (gate_ref, up_ref, down_ref, shared_ref), refs = refs[:4], refs[4:]
    g_in, e_in, (gpa_in, gpb_in, upa_in, upb_in), refs = refs[:4], refs[4:8], refs[8:12], refs[12:]
    (dxa_hbm, dxb_ref, dxc_ref, dxd_ref, dg_out, du_out), refs = refs[:6], refs[6:]
    gp_ref, upre_ref, dg_ref, du_ref, g_ref, extra_ref, dxa_ref, acc_ref, sems = refs
    rows = g_in[0].shape[0]
    features = g_ref.shape[1]
    here, _, width = gate_ref.shape
    x = info_ref[1]
    first, last = pl.ds(0, 2 * rows), pl.ds(2 * rows, 2 * rows)
    loads = load_rows(g_in, g_ref, None, sems, 0)
    late = [
        start_copy(source, target, sems, 8 + i)
        for i, (source, target) in enumerate(
            [
                (gpa_in, gp_ref.at[:, first]),
                (gpb_in, gp_ref.at[:, last]),
                (upa_in, upre_ref.at[:, first]),
                (upb_in, upre_ref.at[:, last]),
            ]
        )
    ]
    for i in range(4):
        at = pl.ds(i * rows, rows)
        source = e_in[i].at[:, pl.ds(features, EXTRA)]
        late.append(start_copy(source, extra_ref.at[at], sems, 12 + i))
    wait_all(loads)
    s_gate, s_up, s_down = shared_parts_of(shared_ref)
    spans = [slice(i * 2 * rows, (i + 1) * 2 * rows) for i in range(2)]
    d_hiddens = [mm(g_ref[span], s_down) for span in spans]
    wait_all(late)
    lane = lanes_of(2 * rows)
    extras = [extra_ref[span].astype(f32) for span in spans]
    d_gates = [jnp.zeros((2 * rows, EXTRA), f32)] * 2
    part = d_hiddens[0].shape[1] // 2
    cols = slice(2 * width, 2 * width + part)
    for i, span in enumerate(spans):
        total = None
        for half in range(2):
            at = slice(half * part, (half + 1) * part)
            _, d_gate_pre, d_up_pre = hidden_back(
                d_hiddens[i][:, at], gp_ref[half, span, cols], upre_ref[half, span, cols], None
            )
            dg_ref[x ^ half, span, cols] = d_gate_pre
            du_ref[x ^ half, span, cols] = d_up_pre
            term = mm_nt(d_gate_pre, s_gate[:, at]) + mm_nt(d_up_pre, s_up[:, at])
            total = term if total is None else total + term
        acc_ref[span] = total
    sent = []
    for e in range(here):
        expert = info_ref[0] * here + e
        half, at = e // 2, (e % 2) * width
        cols = slice(at, at + width)
        for i, span in enumerate(spans):
            d_gate, d_gate_pre, d_up_pre = hidden_back(
                mm(g_ref[span], down_ref[e]),
                gp_ref[half, span, cols],
                upre_ref[half, span, cols],
                gate_column(extras[i], lane, expert),
            )
            dg_ref[x ^ half, span, cols] = d_gate_pre
            du_ref[x ^ half, span, cols] = d_up_pre
            d_gates[i] = jnp.where(lane == expert, d_gate, d_gates[i])
            acc_ref[span] += mm_nt(d_gate_pre, gate_ref[e]) + mm_nt(d_up_pre, up_ref[e])
        if e + 1 == here:
            sent = [
                start_copy(dg_ref.at[0], dg_out, sems, 16),
                start_copy(du_ref.at[0], du_out, sems, 17),
            ]
    for i, ref in enumerate((dxa_ref, dxb_ref, dxc_ref, dxd_ref)):
        at = slice(i * rows, (i + 1) * rows)
        own = slice(i % 2 * rows, (i % 2 + 1) * rows)
        extra = split_low(d_gates[i // 2], lane, 16)[own]
        ref[:, :features] = acc_ref[at].astype(ref.dtype)
        ref[:, features:] = extra.astype(ref.dtype)
    sent.append(start_copy(dxa_ref, dxa_hbm, sems, 18))
    wait_all(sent)


def experts_back_call(info, grads, exts, kept, weights):
    rows, features = grads[0].shape[0], grads[0].shape[1] - EXTRA
    _, held, wide = kept[0].shape
    ext = grads[0].shape
    return pl.pallas_call(
        experts_back_kernel,
        out_shape=(
            hbm(ext, f32),
            jax.ShapeDtypeStruct(ext, bf16),
            jax.ShapeDtypeStruct(ext, f32),
            jax.ShapeDtypeStruct(ext, bf16),
        )
        + (hbm((2 * held, wide), bf16),) * 2,
        in_specs=[in_smem] + [in_vmem] * 4 + [anywhere] * 12,
        out_specs=(anywhere,) + (in_vmem,) * 3 + (anywhere,) * 2,
        scratch_shapes=[pltpu.VMEM((2, 2 * held, wide), bf16)] * 4
        + [
            pltpu.VMEM((4 * rows, features), bf16),
            pltpu.VMEM((4 * rows, EXTRA), bf16),
            pltpu.VMEM(ext, f32),
            pltpu.VMEM((4 * rows, features), f32),
            pltpu.SemaphoreType.DMA((19,)),
        ],
        compiler_params=limits(24),
        cost_estimate=cost(24),
        name="experts_backward",
    )(info, *weights, *[in_hbm(value) for value in (*grads, *exts, *kept)])


def pair_shared(info_ref, shared_ref, which):
    width = shared_ref.shape[1] // 3
    first = which * width + info_ref[1] * (width // 2)
    return shared_ref[:, pl.ds(pl.multiple_of(first, 128), width // 2)]


def pair_kernel(info_ref, gate_ref, up_ref, shared_ref, x0, x1, x2, x3,
                gp_out, upre_out, hid_out, gp_ref, upre_ref, hid_ref, x_ref, extra_ref, sems):
    here, _, width = gate_ref.shape
    count = here // 2
    wait_all(load_rows((x0, x1, x2, x3), x_ref, extra_ref, sems, 3))
    extra = extra_ref[...].astype(f32)
    lane = lanes_of(extra.shape[0])
    for j in range(count + 1):
        if j < count:
            gate_w, up_w = gate_ref[info_ref[1] * count + j], up_ref[info_ref[1] * count + j]
        else:
            gate_w, up_w = (pair_shared(info_ref, shared_ref, i) for i in range(2))
        gate_pre, up_pre = mm(x_ref[...], gate_w), mm(x_ref[...], up_w)
        hidden = gate_pre * jax.nn.sigmoid(gate_pre) * up_pre
        if j < count:
            expert = info_ref[0] * here + info_ref[1] * count + j
            hidden = hidden * gate_column(extra, lane, expert)
        cols = slice(j * width, j * width + gate_pre.shape[1])
        gp_ref[:, cols] = gate_pre.astype(bf16)
        upre_ref[:, cols] = up_pre.astype(bf16)
        hid_ref[:, cols] = hidden.astype(bf16)
    wait_all(
        [
            start_copy(source, target, sems, i)
            for i, (source, target) in enumerate(
                [(hid_ref, hid_out), (gp_ref, gp_out), (upre_ref, upre_out)]
            )
        ]
    )


def pair_call(info, exts, weights):
    rows, features = 4 * exts[0].shape[0], exts[0].shape[1] - EXTRA
    e_gate, e_up, _, shared = weights
    wide = (rows, e_gate.shape[0] // 2 * e_gate.shape[2] + shared.shape[1] // 6)
    return pl.pallas_call(
        pair_kernel,
        out_shape=(hbm(wide, bf16),) * 3,
        in_specs=[in_smem] + [in_vmem] * 3 + [anywhere] * 4,
        out_specs=(anywhere,) * 3,
        scratch_shapes=[pltpu.VMEM(wide, bf16)] * 3
        + [
            pltpu.VMEM((rows, features), bf16),
            pltpu.VMEM((rows, EXTRA), bf16),
            pltpu.SemaphoreType.DMA((11,)),
        ],
        compiler_params=limits(16),
        cost_estimate=cost(8),
        name="pair_forward",
    )(info, e_gate, e_up, shared, *[in_hbm(value) for value in exts])


def pair_back_kernel(info_ref, down_ref, shared_ref, g0, g1, g2, g3, e0, e1, e2, e3, gp_in, upre_in,
                     dg_out, du_out, gp_ref, upre_ref, dg_ref, du_ref, g_ref, extra_ref, sems):
    rows, features = g0.shape[0], g_ref.shape[1]
    here, _, width = down_ref.shape
    count = here // 2
    loads = load_rows((g0, g1, g2, g3), g_ref, None, sems, 4)
    loads += [start_copy(gp_in, gp_ref, sems, 0), start_copy(upre_in, upre_ref, sems, 1)]
    for i, source in enumerate((e0, e1, e2, e3)):
        lanes = source.at[:, pl.ds(features, EXTRA)]
        loads.append(start_copy(lanes, extra_ref.at[pl.ds(i * rows, rows)], sems, 12 + i))
    wait_all(loads)
    extra = extra_ref[...].astype(f32)
    lane = lanes_of(4 * rows)
    for j in range(count + 1):
        gate = None
        if j < count:
            weight = down_ref[info_ref[1] * count + j]
            gate = gate_column(extra, lane, info_ref[0] * here + info_ref[1] * count + j)
        else:
            weight = pair_shared(info_ref, shared_ref, 2)
        cols = slice(j * width, j * width + weight.shape[1])
        _, d_gate_pre, d_up_pre = hidden_back(
            mm(g_ref[...], weight), gp_ref[:, cols], upre_ref[:, cols], gate
        )
        dg_ref[:, cols] = d_gate_pre
        du_ref[:, cols] = d_up_pre
    wait_all([start_copy(dg_ref, dg_out, sems, 2), start_copy(du_ref, du_out, sems, 3)])


def pair_back_call(info, grads, exts, gate_pre, up_pre, weights):
    rows, features = 4 * exts[0].shape[0], exts[0].shape[1] - EXTRA
    wide = gate_pre.shape
    return pl.pallas_call(
        pair_back_kernel,
        out_shape=(hbm(wide, bf16),) * 2,
        in_specs=[in_smem] + [in_vmem] * 2 + [anywhere] * 10,
        out_specs=(anywhere,) * 2,
        scratch_shapes=[pltpu.VMEM(wide, bf16)] * 4
        + [
            pltpu.VMEM((rows, features), bf16),
            pltpu.VMEM((rows, EXTRA), bf16),
            pltpu.SemaphoreType.DMA((16,)),
        ],
        compiler_params=limits(16),
        cost_estimate=cost(7),
        name="pair_backward",
    )(info, weights[2], weights[3], *[in_hbm(value) for value in (*grads, *exts, gate_pre, up_pre)])


def weight_grad_kernel(*refs):
    lefts, rights, (out_ref, left_ref, right_ref, tiles_ref, sems) = refs[:8], refs[8:-5], refs[-5:]
    features = left_ref.shape[1]
    loads, at = load_rows(lefts, left_ref, None, sems, 3), 0
    for i, ref in enumerate(rights):
        target = right_ref.at[pl.ds(at, ref.shape[0])]
        loads.append(start_copy(ref, target, sems, 19 + i))
        at += ref.shape[0]
    wait_all(loads)
    rows = left_ref.shape[0]
    tile, wide = tiles_ref.shape[1:]
    sent = []
    for group in range(right_ref.shape[0] // rows):
        right = slice(group * rows, (group + 1) * rows)
        for t in range(features // tile):
            cols = slice(t * tile, (t + 1) * tile)
            index = group * (features // tile) + t
            slot = index % tiles_ref.shape[0]
            if len(sent) >= tiles_ref.shape[0]:
                sent[index - tiles_ref.shape[0]].wait()
            tiles_ref[slot] = mm_tn(left_ref[:, cols], right_ref[right]).astype(bf16)
            target = out_ref.at[pl.ds(t * tile, tile), pl.ds(group * wide, wide)]
            sent.append(start_copy(tiles_ref.at[slot], target, sems, slot))
    wait_all(sent[-tiles_ref.shape[0] :])


def weight_grad_call(lefts, rights):
    rows = sum(value.shape[0] for value in lefts)
    features, wide = lefts[0].shape[1] - EXTRA, rights[0].shape[1]
    held = sum(value.shape[0] for value in rights)
    operands = [in_hbm(value) for value in (*lefts, *rights)]
    return pl.pallas_call(
        weight_grad_kernel,
        out_shape=hbm((features, held // rows * wide), bf16),
        in_specs=[anywhere] * len(operands),
        out_specs=anywhere,
        scratch_shapes=[
            pltpu.VMEM((rows, features), bf16),
            pltpu.VMEM((held, wide), bf16),
            pltpu.VMEM((3, 256, wide), bf16),
            pltpu.SemaphoreType.DMA((19 + len(rights),)),
        ],
        compiler_params=limits(16),
        cost_estimate=cost(8 * held // rows),
        name="weight_gradients",
    )(*operands)


def exchange_wa(pick):
    return [pick(0)] + [swap(pick(i), "wa", i) for i in (1, 2, 3)]


def after(values, *done):
    kept = lax.optimization_barrier((values, done))
    return kept[0]


def key_blocks(kv, n):
    levels = [kv]
    for s in range(1, n // 2):
        levels.append(lax.ppermute(kv, "ctx", [(i, i + 2 * s) for i in range(n - 2 * s)]))
    blocks = []
    for level in levels:
        blocks += [level, swap(level, "ctx", 1)]
    return blocks


def sum_key_blocks(own, moved, n, beside):
    m, rows = n // 2, own[0].shape[0]
    got = [both[i : i + rows] for both in moved for i in range(0, both.shape[0], rows)]
    total, beside = None, list(beside)
    for s in reversed(range(m)):
        level = own[s].astype(f32) + got[s].astype(f32)
        if s:
            level = lax.ppermute(
                level.astype(bf16), "ctx", [(i + 2 * s, i) for i in range(n - 2 * s)]
            )
            if beside:
                level = after(level, beside.pop(0))
            level = level.astype(f32)
        total = level if total is None else total + level
    return total.astype(bf16)


def sum_pairs(value, n):
    groups = [[2 * i + x for i in range(n // 2)] for x in range(2)]
    return lax.psum_scatter(
        value, "ctx", scatter_dimension=0, tiled=True, axis_index_groups=groups
    )


def per_device(
    tokens,
    teacher,
    lengths,
    routes,
    query_weight,
    key_projection_matrix,
    value_projection_matrix,
    output_weight,
    attn_gain,
    moe_gain,
    router_weight,
    shared_gate,
    shared_up,
    shared_down,
    expert_gate,
    expert_up,
    expert_down,
):
    w = lax.axis_index("wa")
    c = lax.axis_index("ctx")
    n = lax.axis_size("ctx")
    groups = lax.axis_size("wa")
    x, z, m = c % 2, c // 2, n // 2
    own_tokens = tokens[0]
    rows, features = own_tokens.shape
    slab = features // groups
    experts_all = router_weight.shape[1]
    length = jnp.sum(jnp.where(jnp.arange(lengths.shape[0]) == w, lengths, 0))
    count = jnp.sum(lengths).astype(f32)
    qpos = c * rows + jnp.arange(rows)
    width = KEY_VALUE_HEADS * HEAD_SIZE
    z_low = z % 2
    w_info = jnp.stack([w, x, z_low]).astype(jnp.int32)

    def columns(value, index):
        return lax.dynamic_slice_in_dim(value, index * slab, slab, 1)

    input_rows = own_tokens.astype(f32)
    factor_a = rms_factor(input_rows)
    far_half = lax.dynamic_slice_in_dim(own_tokens, (1 - w // 2) * 2 * slab, 2 * slab, 1)
    far_tokens = swap(far_half, "wa", 2)
    far_factor = swap(factor_a, "wa", 2)
    small = jnp.concatenate([router_weight.T, attn_gain[None], moe_gain[None]], axis=0)
    near_small = swap(small, "wa", 1)
    far_small = swap(small, "wa", 2)
    own_weights = (key_projection_matrix, value_projection_matrix, query_weight)
    near_weights = tuple(swap(value, "wa", 1) for value in own_weights)

    gain_own = small[-2:-1].astype(f32)
    gain_near = near_small[-2:-1].astype(f32)
    core = w % 2

    def far_columns(index):
        return lax.dynamic_slice_in_dim(far_tokens, index * slab, slab, 1)

    part_own = jnp.concatenate([columns(own_tokens, w), far_columns(core)], axis=0)
    part_near = jnp.concatenate([columns(own_tokens, w ^ 1), far_columns(1 - core)], axis=0)
    both_factor = jnp.concatenate([factor_a, far_factor], axis=0)
    normed_own = (part_own.astype(f32) * both_factor * gain_own).astype(bf16)
    normed_near = (part_near.astype(f32) * both_factor * gain_near).astype(bf16)

    def project(i):
        return mm(normed_own, own_weights[i]) + mm(normed_near, near_weights[i])

    kv_terms = jnp.concatenate([project(0), project(1)], axis=1)
    kv_got = swap(after(kv_terms[rows:].astype(bf16), far_small), "wa", 2)
    kv = (kv_terms[:rows] + kv_got.astype(f32)).astype(bf16)
    q_terms = project(2)

    half_out = output_weight.shape[1] // 2
    half_weight = lax.dynamic_slice_in_dim(output_weight, z_low * half_out, half_out, 1)
    q_got = swap(after(q_terms[rows:].astype(bf16), kv_got), "wa", 2)
    query_rows = (q_terms[:rows] + q_got.astype(f32)).astype(bf16)
    far_out = swap(after(half_weight, kv_got), "wa", 2)
    if n > 8:
        first_keys, all_keys = [], []
    else:
        kv_all = key_blocks(kv, n)
        first_keys, all_keys = [kv_all[1]] + kv_all[2::2], kv_all[1:]

    shared_width = shared_gate.shape[1] // groups

    shared_weights = after((shared_gate, shared_up, shared_down), kv_got)

    def shared_chunk(i):
        return jnp.concatenate(
            [
                lax.dynamic_slice_in_dim(value, (w ^ i) * shared_width, shared_width, 1)
                for value in shared_weights
            ],
            axis=1,
        )

    shared_far = swap(
        after(jnp.concatenate([shared_chunk(2), shared_chunk(3)]), far_out, q_got, *first_keys), "wa", 2
    )
    far_pair = jnp.concatenate([far_out, swap(far_out, "ctx", 2)])
    output_parts = [
        output_weight,
        swap(output_weight, "wa", 1),
        far_pair,
        swap(after(far_pair, *all_keys), "wa", 1),
    ]
    smalls = jnp.concatenate(
        perm4([small, near_small, far_small, swap(far_small, "wa", 1)], w), axis=1
    )
    router_t = jnp.pad(smalls[:experts_all], ((0, EXTRA - experts_all), (0, 0)))
    gain_a, gain_b = smalls[-2:-1].astype(f32), smalls[-1:].astype(f32)

    if n > 8:
        kv_all, pos = gather_keys(kv, c, n)
        q = heads(query_rows, GROUP)
        attn, kept_attn = attention_forward(q, kv_all, pos, qpos, length)
        attn = attn.reshape(rows, -1)
        attn_out = attn.astype(bf16)
    else:
        first = [c, length]
        for s in range(m):
            first += [(c - 2 * s) * rows, (c - 2 * s + 1 - 2 * x) * rows]
        attn_out, attn, kept_attn = attention_call(
            jnp.stack(first).astype(jnp.int32), query_rows, kv_all
        )
    resid, row_ext, gates = branch_call(
        w_info, attn_out, output_parts, own_tokens, gain_b, router_t, routes[0]
    )
    shared_parts = [
        shared_chunk(0),
        swap(shared_chunk(1), "wa", 1),
        shared_far[:slab],
        swap(after(shared_far[slab:], attn_out), "wa", 1),
    ]
    shared_mine = jnp.concatenate(perm4(shared_parts, w))
    weights = (expert_gate, expert_up, expert_down, shared_mine)

    row_parts = [row_ext, swap(row_ext, "wa", 1), swap(row_ext, "wa", 2)]
    rows_own = swap(row_ext, "ctx", 1)
    done = [experts_call(w_info, row_parts[0], row_parts[1], weights)]
    row_parts[2] = after(row_parts[2], done[0][1], rows_own)
    row_parts.append(swap(row_parts[2], "wa", 1))
    rows_far = swap(row_parts[2], "ctx", 1)
    rows_pair = row_parts + [rows_own, swap(rows_own, "wa", 1), rows_far, swap(rows_far, "wa", 1)]
    done.append(experts_call(w_info, row_parts[2], row_parts[3], weights))

    def sum_wa(own, near, far, far_near):
        far = far + swap(far_near, "wa", 1).astype(f32)
        return own, swap(near, "wa", 1), far.astype(bf16)

    own_out, near_out, far_out = sum_wa(done[0][0], done[0][1], done[1][0], done[1][1])
    far_out = after(swap(far_out, "wa", 2), rows_far)
    gate_pre_pair, up_pre_pair, hidden_pair = pair_call(w_info, rows_pair[4:], weights)
    scale = lengths.shape[0] * n * rows / count
    block_out, grad_result, grad_ext = result_call(
        jnp.stack([c, length]).astype(jnp.int32), scale[None], resid, own_out, near_out, far_out, teacher[0]
    )
    grad_parts = [grad_ext, swap(grad_ext, "wa", 1), swap(grad_ext, "wa", 2)]
    pair_own = swap(grad_ext, "ctx", 1)

    grad_parts[2], pair_own = after((grad_parts[2], pair_own), hidden_pair)
    grad_parts.append(swap(grad_parts[2], "wa", 1))
    pair_far = swap(grad_parts[2], "ctx", 1)
    grads_pair = grad_parts + [pair_own, swap(pair_own, "wa", 1), pair_far, swap(pair_far, "wa", 1)]
    down_terms = weight_grad_call(grads_pair, [done[0][4], done[1][4], hidden_pair])
    down_sum = sum_pairs(down_terms, n)

    kept = (done[0][2], done[1][2], done[0][3], done[1][3])
    first_grad = after(grad_parts[0], down_terms)
    back = experts_back_call(w_info, [first_grad] + grad_parts[1:], row_parts, kept, weights)
    own_back, near_back, far_back = sum_wa(*back[:4])
    grads_pair[4] = after(grads_pair[4], far_back)
    far_back = swap(far_back, "wa", 2)
    gate_pair, up_pair = pair_back_call(
        w_info, grads_pair[4:], rows_pair[4:], gate_pre_pair, up_pre_pair, weights
    )
    gate_pair = after(gate_pair, far_back)
    pre_terms = weight_grad_call(rows_pair, [back[4], gate_pair, back[5], up_pair])
    far_back = after(far_back, pre_terms)
    grad_resid, gz, d_attn, small_b = resid_back_call(
        w_info, own_back, near_back, far_back, grad_result, resid, row_ext, gates, gain_b,
        router_t, output_parts, experts_all,
    )

    fine_rows = features // n

    def whole_rows(summed):
        ours = lax.dynamic_slice_in_dim(summed, x * fine_rows, fine_rows, 0)
        got = swap(lax.dynamic_slice_in_dim(summed, (1 - x) * fine_rows, fine_rows, 0), "ctx", 1)
        return jnp.where(x == 0, ours, got), jnp.where(x == 0, got, ours)

    fine = features // n // groups

    def fine_exchange(value):
        blocks = jnp.transpose(value.reshape(-1, n, groups, fine), (2, 0, 1, 3))
        blocks = blocks.reshape(groups, -1, slab)
        return exchange_wa(lambda i: lax.dynamic_index_in_dim(blocks, w ^ i, 0, keepdims=False))

    attn_in = (input_rows * factor_a * gain_a).astype(bf16)
    attn_in_fine = jnp.concatenate(fine_exchange(attn_in))
    gz_fine = jnp.concatenate(fine_exchange(gz))

    def fold_rows(value):
        blocks = value.astype(bf16).reshape(m, 2, fine, value.shape[1])
        mine = lax.dynamic_index_in_dim(blocks, x, 1, keepdims=False)
        got = swap(lax.dynamic_index_in_dim(blocks, 1 - x, 1, keepdims=False), "ctx", 1)
        summed = (mine.astype(f32) + got.astype(f32)).astype(bf16)
        return summed.reshape(m * fine, -1)


    if n > 8:
        d_heads = heads(d_attn, GROUP)
        delta = jnp.sum(d_heads.astype(f32) * heads(attn, GROUP), axis=-1)
        delta = jnp.transpose(delta, (1, 2, 0))[..., None]
        d_q, d_kv = attention_backward(q, kv_all, pos, qpos, length, kept_attn, d_heads, delta)
        d_q = d_q.reshape(rows, -1).astype(bf16)
        d_kv, moved = scatter_keys(d_kv, n).astype(bf16), []
    else:
        d_q, d_own, d_pair = attention_back_call(d_attn, query_rows, attn, kept_attn, kv_all)
        moved = [swap(jnp.concatenate(d_pair[at : at + 2]), "ctx", 1) for at in range(0, m, 2)]
    attn_parts = gather_wa(after(attn_out, d_q))
    grad_output = fold_rows(mm_tn(gz_fine, jnp.concatenate(attn_parts)))
    d_q_parts = gather_wa(after(d_q, *moved))
    grad_query = fold_rows(mm_tn(attn_in_fine, jnp.concatenate(d_q_parts)))
    down_halves = whole_rows(after(down_sum, d_q))
    if n <= 8:
        d_kv = sum_key_blocks(d_own, moved, n, (grad_output, grad_query, down_halves[0]))
    pre_sum = sum_pairs(after(pre_terms, down_sum, d_q), n)
    d_kv_parts = gather_wa(d_kv)

    both_d_q = jnp.concatenate([d_q, d_q_parts[2]])
    both_d_kv = jnp.concatenate([d_kv, d_kv_parts[2]])

    def back_through(weights):
        both = (both_d_kv[:, :width], both_d_kv[:, width:], both_d_q)
        return sum(mm_nt(value, weight) for value, weight in zip(both, weights, strict=True))

    back_own, back_near = back_through(own_weights), back_through(near_weights)
    returned = swap(
        jnp.concatenate([back_own[rows:], back_near[rows:]], axis=1).astype(bf16), "wa", 2
    ).astype(f32)
    grad_attn_in = jnp.concatenate(
        perm4([back_own[:rows], back_near[:rows], returned[:, :slab], returned[:, slab:]], w),
        axis=1,
    )
    grad_norm_a, grad_gain_a = norm_backward(input_rows, factor_a, gain_a, grad_attn_in)
    grad_tokens = grad_resid + grad_norm_a

    grad_kv = fold_rows(mm_tn(attn_in_fine, jnp.concatenate(d_kv_parts)))
    dense_terms = jnp.concatenate([grad_output, grad_query, grad_kv], axis=1)

    loss_part = jnp.sum(grad_ext[:, features:].astype(f32))
    smalls_grad = jnp.concatenate(
        [small_b[: experts_all + 1], grad_gain_a[None], jnp.full((1, features), loss_part)], axis=0
    )
    parts = fine_exchange(smalls_grad)
    small_sum = (parts[0] + parts[1] + parts[2] + parts[3]).reshape(-1, n, fine)
    small_sum = after(jnp.transpose(small_sum, (1, 0, 2)), dense_terms)
    if m == 4:
        blocks = small_sum.reshape((m, 2) + small_sum.shape[1:])
        got = swap(lax.dynamic_index_in_dim(blocks, 1 - x, 1, keepdims=False), "ctx", 1)
        blocks = lax.dynamic_index_in_dim(blocks, x, 1, keepdims=False) + got
        parts = [lax.dynamic_index_in_dim(blocks, z ^ i, 0, keepdims=False) for i in range(m)]
        small_sum = parts[0] + sum(swap(parts[i], "ctx", 2 * i) for i in range(1, m))
    else:
        small_sum = lax.all_to_all(small_sum, "ctx", split_axis=0, concat_axis=0, tiled=True)
        small_sum = jnp.sum(small_sum, axis=0)
    loss = small_sum[-1, 0] / (2.0 * features * count)
    dense = sum_pairs(after(dense_terms, pre_sum, small_sum), n).astype(f32)
    pieces, at = [], 0
    for size in (output_weight.shape[1], query_weight.shape[1], width, width):
        pieces.append(dense[:, at : at + size])
        at += size

    units = expert_gate.shape[2]
    used = expert_gate.shape[0] // 2 * units

    def experts_of(first, second, at):
        return jnp.stack(
            [
                value[:, at + e * units : at + (e + 1) * units].astype(f32)
                for value in (first, second)
                for e in range(expert_gate.shape[0] // 2)
            ]
        )

    wide = down_sum.shape[1]
    pre_halves = whole_rows(after(pre_sum, dense_terms))
    grad_expert_down = experts_of(*down_halves, 0)
    grad_expert_gate = experts_of(*pre_halves, 0)
    grad_expert_up = experts_of(*pre_halves, wide)
    shared = jnp.concatenate(
        [value[:, used:] for value in down_halves]
        + [value[:, used:wide] for value in pre_halves]
        + [value[:, wide + used :] for value in pre_halves],
        axis=1,
    )

    def shared_rows(i):
        return lax.dynamic_slice_in_dim(shared, (w ^ i) * fine, fine, 0)

    shared = jnp.stack(perm4(exchange_wa(shared_rows), w)).astype(f32)
    shared = shared.reshape(groups, fine, 3, shared_width)
    grad_shared_down, grad_shared_gate, grad_shared_up = (
        jnp.transpose(shared[:, :, i], (1, 0, 2)).reshape(fine, -1) for i in range(3)
    )

    return (
        block_out[None],
        grad_tokens[None],
        pieces[1],
        pieces[2],
        pieces[3],
        pieces[0],
        small_sum[experts_all + 1],
        small_sum[experts_all],
        small_sum[:experts_all].T,
        grad_shared_gate,
        grad_shared_up,
        grad_shared_down,
        grad_expert_gate,
        grad_expert_up,
        grad_expert_down,
        loss,
    )


def solution(mesh):
    return jax.shard_map(
        per_device,
        mesh=mesh,
        in_specs=(
            P("wa", "ctx", None),
            P("wa", "ctx", None),
            P(),
            P("wa", "ctx", None),
            P("wa", None),
            P("wa", None),
            P("wa", None),
            P("wa", None),
            P("wa"),
            P("wa"),
            P("wa", None),
            P("wa", None),
            P("wa", None),
            P("wa", None),
            P("wa", None, None),
            P("wa", None, None),
            P("wa", None, None),
        ),
        out_specs=(
            P("wa", "ctx", None),
            P("wa", "ctx", None),
            P(("ctx", "wa"), None),
            P(("ctx", "wa"), None),
            P(("ctx", "wa"), None),
            P(("ctx", "wa"), None),
            P(("ctx", "wa")),
            P(("ctx", "wa")),
            P(("ctx", "wa"), None),
            P(("ctx", "wa"), None),
            P(("ctx", "wa"), None),
            P(("ctx", "wa"), None),
            P("wa", "ctx", None),
            P("wa", "ctx", None),
            P("wa", "ctx", None),
            P(),
        ),
        check_vma=False,
    )
```

```python
import jax
import jax.numpy as jnp
from jax import lax
from jax.experimental import pallas as pl
from jax.experimental.pallas import tpu as pltpu
from jax.sharding import PartitionSpec as P

QUERY_HEADS = 12
KEY_VALUE_HEADS = 4
HEAD_SIZE = 128
TOP = 6
GROUP = QUERY_HEADS // KEY_VALUE_HEADS

epsilon = 1e-06
masked = -1e30
bf16 = jnp.bfloat16
f32 = jnp.float32


def dot(a, b, dims):
    return lax.dot_general(a, b, ((dims[0], dims[1]), ((), ())), preferred_element_type=f32)


def mm(a, b):
    return dot(a, b, ((1,), (0,)))


def mm_nt(a, b):
    return dot(a, b, ((1,), (1,)))


def mm_tn(a, b):
    return dot(a, b, ((0,), (0,)))


def swap(value, axis, bit):
    size = lax.axis_size(axis)
    return lax.ppermute(value, axis, [(i, i ^ bit) for i in range(size)])


def perm4(parts, w):
    core, upper = w % 2 == 1, w // 2 == 1
    a, b, c, d = parts
    a, b, c, d = (
        jnp.where(core, b, a),
        jnp.where(core, a, b),
        jnp.where(core, d, c),
        jnp.where(core, c, d),
    )
    return [
        jnp.where(upper, c, a),
        jnp.where(upper, d, b),
        jnp.where(upper, a, c),
        jnp.where(upper, b, d),
    ]


def gather_wa(value):
    near = swap(value, "wa", 1)
    far = swap(value, "wa", 2)
    return [value, near, far, swap(far, "wa", 1)]


def silu_parts(rows):
    sigma = jax.nn.sigmoid(rows)
    return rows * sigma, sigma * (1.0 + rows * (1.0 - sigma))


def rms_factor(rows):
    return lax.rsqrt(jnp.mean(rows * rows, axis=-1, keepdims=True) + epsilon)


def norm_backward(rows, factor, gain, upstream):
    weighted = upstream * gain
    inner = jnp.mean(weighted * rows, axis=-1, keepdims=True)
    grad = factor * weighted - rows * (factor * factor * factor * inner)
    return grad, jnp.sum(upstream * rows * factor, axis=0)


def gather_keys(kv, c, n):
    rows = kv.shape[0]
    if n > 8:
        return lax.all_gather(kv, "ctx", axis=0, tiled=True), jnp.arange(n * rows)
    levels = [kv]
    for s in range(1, n // 2):
        levels.append(lax.ppermute(kv, "ctx", [(i, i + 2 * s) for i in range(n - 2 * s)]))
    blocks, pos = [], []
    for s, level in enumerate(levels):
        blocks += [level, swap(level, "ctx", 1)]
        start = (c - 2 * s) * rows
        pos += [start + jnp.arange(rows), (c - 2 * s + 1 - 2 * (c % 2)) * rows + jnp.arange(rows)]
    return jnp.concatenate(blocks), jnp.concatenate(pos)


def scatter_keys(grads, n):
    rows = grads.shape[0] // n
    if n > 8:
        return lax.psum_scatter(grads, "ctx", scatter_dimension=0, tiled=True).astype(f32)
    blocks = grads.reshape(n, rows, -1)
    total = None
    for s in reversed(range(n // 2)):
        level = blocks[2 * s].astype(f32) + swap(blocks[2 * s + 1], "ctx", 1).astype(f32)
        if s:
            level = lax.ppermute(
                level.astype(bf16), "ctx", [(i + 2 * s, i) for i in range(n - 2 * s)]
            ).astype(f32)
        total = level if total is None else total + level
    return total


def heads(rows, groups):
    return rows.reshape(rows.shape[0], KEY_VALUE_HEADS, groups, HEAD_SIZE)


def attention_scores(q, k, pos, qpos, length):
    scale = HEAD_SIZE**-0.5
    scores = jnp.einsum("tkgd,nkd->kgtn", q, k, preferred_element_type=f32) * scale
    allowed = (pos[None, :] >= 0) & (pos[None, :] <= qpos[:, None]) & (pos[None, :] < length)
    return scores, allowed


def chunked(kv, pos):
    size = 1024
    if kv.shape[0] <= size:
        return None
    return kv.reshape(-1, size, kv.shape[1]), pos.reshape(-1, size)


def attention_forward(q, kv, pos, qpos, length):
    rows = q.shape[0]
    pieces = chunked(kv, pos)
    width = KEY_VALUE_HEADS * HEAD_SIZE
    if pieces is None:
        k, v = heads(kv[:, :width], 1)[:, :, 0], heads(kv[:, width:], 1)[:, :, 0]
        scores, allowed = attention_scores(q, k, pos, qpos, length)
        scores = jnp.where(allowed, scores, masked)
        top = jnp.max(scores, axis=-1, keepdims=True)
        weights = jnp.exp(scores - top)
        probs = (weights / jnp.sum(weights, axis=-1, keepdims=True)).astype(bf16)
        attn = jnp.einsum("kgtn,nkd->tkgd", probs, v, preferred_element_type=f32)
        return attn, probs

    def step(carry, piece):
        top, total, accum = carry
        kv_now, pos_now = piece
        k, v = heads(kv_now[:, :width], 1)[:, :, 0], heads(kv_now[:, width:], 1)[:, :, 0]
        scores, allowed = attention_scores(q, k, pos_now, qpos, length)
        scores = jnp.where(allowed, scores, masked)
        new_top = jnp.maximum(top, jnp.max(scores, axis=-1, keepdims=True))
        weights = jnp.where(allowed, jnp.exp(scores - new_top), 0.0)
        shrink = jnp.exp(top - new_top)
        total = total * shrink + jnp.sum(weights, axis=-1, keepdims=True)
        update = jnp.einsum("kgtn,nkd->kgtd", weights.astype(bf16), v, preferred_element_type=f32)
        return (new_top, total, accum * shrink + update), None

    shape = (KEY_VALUE_HEADS, GROUP, rows)
    start = (
        jnp.full(shape + (1,), masked, f32),
        jnp.zeros(shape + (1,), f32),
        jnp.zeros(shape + (HEAD_SIZE,), f32),
    )
    (top, total, accum), _ = lax.scan(step, start, pieces)
    return jnp.transpose(accum / total, (2, 0, 1, 3)), top + jnp.log(total)


def attention_backward(q, kv, pos, qpos, length, kept, d_attn, delta):
    scale = HEAD_SIZE**-0.5
    width = KEY_VALUE_HEADS * HEAD_SIZE

    def terms(probs, k, v):
        d_probs = jnp.einsum("tkgd,nkd->kgtn", d_attn, v, preferred_element_type=f32)
        d_scores = (probs.astype(f32) * (d_probs - delta)).astype(bf16)
        d_q = jnp.einsum("kgtn,nkd->tkgd", d_scores, k, preferred_element_type=f32) * scale
        d_k = jnp.einsum("kgtn,tkgd->nkd", d_scores, q, preferred_element_type=f32) * scale
        d_v = jnp.einsum(
            "kgtn,tkgd->nkd", probs.astype(bf16), d_attn, preferred_element_type=f32
        )
        keys = k.shape[0]
        return d_q, jnp.concatenate(
            [d_k.reshape(keys, width), d_v.reshape(keys, width)], axis=1
        ).astype(bf16)

    pieces = chunked(kv, pos)
    if pieces is None:
        k, v = heads(kv[:, :width], 1)[:, :, 0], heads(kv[:, width:], 1)[:, :, 0]
        return terms(kept, k, v)

    def step(d_q, piece):
        kv_now, pos_now = piece
        k, v = heads(kv_now[:, :width], 1)[:, :, 0], heads(kv_now[:, width:], 1)[:, :, 0]
        scores, allowed = attention_scores(q, k, pos_now, qpos, length)
        probs = jnp.where(allowed, jnp.exp(scores - kept), 0.0)
        more, d_kv = terms(probs, k, v)
        return d_q + more, d_kv

    d_q, d_kv = lax.scan(step, jnp.zeros(q.shape, f32), pieces)
    return d_q, d_kv.reshape(kv.shape)


EXTRA = 128
in_vmem = pl.BlockSpec(memory_space=pltpu.VMEM)
in_smem = pl.BlockSpec(memory_space=pltpu.SMEM)
anywhere = pl.BlockSpec(memory_space=pltpu.MemorySpace.HBM)


def hbm(shape, dtype):
    return pltpu.HBM(shape, dtype)


def in_hbm(value):
    return pltpu.with_memory_space_constraint(value, pltpu.HBM)


def start_copy(source, target, sems, index):
    copy = pltpu.make_async_copy(source, target, sems.at[index])
    copy.start()
    return copy


def cost(microseconds):
    return pl.CostEstimate(flops=int(microseconds * 1.15e+09), bytes_accessed=0, transcendentals=0)


def limits(mib):
    return pltpu.CompilerParams(vmem_limit_bytes=mib << 20)


def split_low(value, lane, shift):
    high = value.astype(bf16).astype(f32)
    rest = pltpu.roll(value - high, shift, 1)
    return jnp.where(lane < shift, high, jnp.where(lane < 2 * shift, rest, 0.0))


def join_low(value, lane, shift):
    total = value + pltpu.roll(value, value.shape[1] - shift, 1)
    return jnp.where(lane < shift, total, 0.0)


def lanes_of(rows):
    return lax.broadcasted_iota(jnp.int32, (rows, EXTRA), 1)


def load_rows(sources, rows_ref, extra_ref, sems, first):
    features, copies = rows_ref.shape[1], []
    for i, source in enumerate(sources):
        at = pl.ds(i * source.shape[0], source.shape[0])
        copies.append(
            start_copy(source.at[:, pl.ds(0, features)], rows_ref.at[at], sems, first + 2 * i)
        )
        if extra_ref is not None:
            lanes = pl.ds(features, EXTRA)
            copies.append(
                start_copy(source.at[:, lanes], extra_ref.at[at], sems, first + 2 * i + 1)
            )
    return copies


def wait_all(copies):
    for copy in copies:
        copy.wait()


def attention_kernel(info_ref, q_ref, *refs):
    blocks = len(refs) - 6
    kv_refs, (out_ref, attn_out, probs_out, attn_ref, probs_ref, sems) = refs[:blocks], refs[blocks:]
    sent = []
    rows = q_ref.shape[0]
    width = KEY_VALUE_HEADS * HEAD_SIZE
    qpos = info_ref[0] * rows + lax.broadcasted_iota(jnp.int32, (rows, rows), 0)
    biases = []
    for b in range(blocks):
        kpos = info_ref[2 + b] + lax.broadcasted_iota(jnp.int32, (rows, rows), 1)
        allowed = (kpos >= 0) & (kpos <= qpos) & (kpos < info_ref[1])
        bias = jnp.where(allowed, 0.0, masked)
        biases.append(jnp.concatenate([bias] * GROUP, axis=0))
    for k in range(KEY_VALUE_HEADS):
        first = k * GROUP * HEAD_SIZE
        q = jnp.concatenate(
            [q_ref[:, first + g * HEAD_SIZE : first + (g + 1) * HEAD_SIZE] for g in range(GROUP)],
            axis=0,
        )
        cols = slice(k * HEAD_SIZE, (k + 1) * HEAD_SIZE)
        scores = [
            mm_nt(q, kv_refs[b][:, cols]) * HEAD_SIZE**-0.5 + biases[b] for b in range(blocks)
        ]
        top = scores[0]
        for score in scores[1:]:
            top = jnp.maximum(top, score)
        top = jnp.max(top, axis=1, keepdims=True)
        weights = [jnp.exp(score - top) for score in scores]
        total = weights[0]
        for weight in weights[1:]:
            total = total + weight
        scale = 1.0 / jnp.sum(total, axis=1, keepdims=True)
        attn = None
        for b in range(blocks):
            probs = (weights[b] * scale).astype(bf16)
            probs_ref[k, b] = probs
            term = mm(probs, kv_refs[b][:, width + k * HEAD_SIZE : width + (k + 1) * HEAD_SIZE])
            attn = term if attn is None else attn + term
        sent.append(start_copy(probs_ref.at[k], probs_out.at[k], sems, k))
        for g in range(GROUP):
            at = slice(first + g * HEAD_SIZE, first + (g + 1) * HEAD_SIZE)
            attn_ref[:, at] = attn[g * rows : (g + 1) * rows]
            out_ref[:, at] = attn[g * rows : (g + 1) * rows].astype(bf16)
    sent.append(start_copy(attn_ref, attn_out, sems, KEY_VALUE_HEADS))
    wait_all(sent)


def attention_call(info, q, kv_blocks):
    rows, blocks = q.shape[0], len(kv_blocks)
    probs = (KEY_VALUE_HEADS, blocks, GROUP * rows, rows)
    return pl.pallas_call(
        attention_kernel,
        out_shape=(jax.ShapeDtypeStruct(q.shape, bf16), hbm(q.shape, f32), hbm(probs, bf16)),
        in_specs=[in_smem] + [in_vmem] * (1 + blocks),
        out_specs=(in_vmem, anywhere, anywhere),
        scratch_shapes=[
            pltpu.VMEM(q.shape, f32),
            pltpu.VMEM(probs, bf16),
            pltpu.SemaphoreType.DMA((KEY_VALUE_HEADS + 1,)),
        ],
        compiler_params=limits(12),
        cost_estimate=cost(5),
        name="attention_forward",
    )(info, q, *kv_blocks)


def attention_back_kernel(d_ref, q_in, attn_in, probs_in, *refs):
    blocks = (len(refs) - 6) // 2
    kv_in, refs = refs[:blocks], refs[blocks:]
    dq_ref, refs = refs[0], refs[1:]
    own_refs, pair_refs, refs = refs[: blocks // 2], refs[blocks // 2 : blocks], refs[blocks:]
    q_ref, attn_ref, probs_ref, kv_ref, sems = refs
    rows = q_ref.shape[0]
    width = KEY_VALUE_HEADS * HEAD_SIZE
    scale = HEAD_SIZE**-0.5
    loads = [start_copy(q_in, q_ref, sems, 0), start_copy(attn_in, attn_ref, sems, 1)]
    loads += [start_copy(kv_in[b], kv_ref.at[b], sems, 2 + b) for b in range(blocks)]
    probs_loads = [
        start_copy(probs_in.at[k], probs_ref.at[k], sems, 2 + blocks + k)
        for k in range(KEY_VALUE_HEADS)
    ]
    wait_all(loads)

    def stacked(ref, first):
        return jnp.concatenate(
            [ref[:, first + g * HEAD_SIZE : first + (g + 1) * HEAD_SIZE] for g in range(GROUP)],
            axis=0,
        )

    for k in range(KEY_VALUE_HEADS):
        first = k * GROUP * HEAD_SIZE
        q, d_attn = stacked(q_ref, first), stacked(d_ref, first)
        delta = jnp.sum(d_attn.astype(f32) * stacked(attn_ref, first), axis=1, keepdims=True)
        kcols = slice(k * HEAD_SIZE, (k + 1) * HEAD_SIZE)
        vcols = slice(width + k * HEAD_SIZE, width + (k + 1) * HEAD_SIZE)
        probs_loads[k].wait()
        d_q = None
        for b in range(blocks):
            key, value = kv_ref[b, :, kcols], kv_ref[b, :, vcols]
            probs = probs_ref[k, b]
            d_probs = mm_nt(d_attn, value)
            d_scores = (probs.astype(f32) * (d_probs - delta)).astype(bf16)
            term = mm(d_scores, key)
            d_q = term if d_q is None else d_q + term
            level = b // 2
            target = own_refs[level] if b % 2 == 0 else pair_refs[level]
            target[:, kcols] = (mm_tn(d_scores, q) * scale).astype(bf16)
            target[:, vcols] = mm_tn(probs, d_attn).astype(bf16)
        d_q = (d_q * scale).astype(bf16)
        for g in range(GROUP):
            dq_ref[:, first + g * HEAD_SIZE : first + (g + 1) * HEAD_SIZE] = d_q[
                g * rows : (g + 1) * rows
            ]


def attention_back_call(d_attn, q, attn, probs, kv_blocks):
    blocks = len(kv_blocks)
    kv_shape = kv_blocks[0].shape
    done = pl.pallas_call(
        attention_back_kernel,
        out_shape=(jax.ShapeDtypeStruct(q.shape, bf16),)
        + (jax.ShapeDtypeStruct(kv_shape, bf16),) * blocks,
        in_specs=[in_vmem] + [anywhere] * (3 + blocks),
        out_specs=(in_vmem,) * (1 + blocks),
        scratch_shapes=[
            pltpu.VMEM(q.shape, bf16),
            pltpu.VMEM(q.shape, f32),
            pltpu.VMEM(probs.shape, bf16),
            pltpu.VMEM((blocks,) + kv_shape, bf16),
            pltpu.SemaphoreType.DMA((2 + blocks + KEY_VALUE_HEADS,)),
        ],
        compiler_params=limits(16),
        cost_estimate=cost(10),
        name="attention_backward",
    )(d_attn, in_hbm(q), in_hbm(attn), in_hbm(probs), *[in_hbm(value) for value in kv_blocks])
    return done[0], list(done[1 : 1 + blocks // 2]), list(done[1 + blocks // 2 :])


def out_halves(info_ref, size):
    half = info_ref[2]
    return (
        pl.ds(pl.multiple_of(half * size, 128), size),
        pl.ds(pl.multiple_of((1 - half) * size, 128), size),
    )


def branch_kernel(
    info_ref, attn_ref, o0, o1, o2, o3, tok_ref, gain_ref, router_ref, routes_ref,
    resid_out, ext_ref, gates_ref, resid_ref, sems,
):
    rows, features = tok_ref.shape
    slab = o0.shape[0]
    here, other = out_halves(info_ref, o2.shape[1])
    attn = attn_ref[...]
    for i in range(4):
        if i < 2:
            term = mm_nt(attn, (o0, o1)[i][...])
        else:
            part = (o2, o3)[i - 2]
            term = mm_nt(attn_ref[:, here], part[:slab]) + mm_nt(attn_ref[:, other], part[slab:])
        at = pl.ds(pl.multiple_of((info_ref[0] ^ i) * slab, 128), slab)
        resid_ref[:, at] = tok_ref[:, at].astype(f32) + term
    sent = start_copy(resid_ref, resid_out, sems, 0)
    resid = resid_ref[...]
    moe_in = (resid * rms_factor(resid) * gain_ref[...]).astype(bf16)
    logits = mm_nt(moe_in, router_ref[...])
    lane = lanes_of(rows)
    chosen = lane == routes_ref[:, 0:1]
    for t in range(1, routes_ref.shape[1]):
        chosen = chosen | (lane == routes_ref[:, t : t + 1])
    logits = jnp.where(chosen, logits, masked)
    raised = jnp.where(chosen, jnp.exp(logits - jnp.max(logits, axis=1, keepdims=True)), 0.0)
    gates = raised / jnp.sum(raised, axis=1, keepdims=True)
    gates_ref[...] = gates
    ext_ref[:, :features] = moe_in
    ext_ref[:, features:] = split_low(gates, lane, 16).astype(bf16)
    sent.wait()


def branch_call(info, attn, output_parts, own_tokens, gain, router, routes):
    rows, features = own_tokens.shape
    return pl.pallas_call(
        branch_kernel,
        out_shape=(
            hbm((rows, features), f32),
            jax.ShapeDtypeStruct((rows, features + EXTRA), bf16),
            jax.ShapeDtypeStruct((rows, EXTRA), f32),
        ),
        in_specs=[in_smem] + [in_vmem] * 9,
        out_specs=(anywhere, in_vmem, in_vmem),
        scratch_shapes=[pltpu.VMEM((rows, features), f32), pltpu.SemaphoreType.DMA((1,))],
        compiler_params=limits(12),
        cost_estimate=cost(4.5),
        name="branch_and_router",
    )(info, attn, *output_parts, own_tokens, gain, router, routes)


def result_kernel(info_ref, scale_ref, resid_in, own_in, teacher_in, near_ref, far_ref,
                  out_hbm, grad_hbm, ext_ref,
                  resid_ref, own_ref, teacher_ref, out_ref, grad_ref, sems):
    loads = [
        start_copy(source, target, sems, i)
        for i, (source, target) in enumerate(
            [(resid_in, resid_ref), (own_in, own_ref), (teacher_in, teacher_ref)]
        )
    ]
    rows, features = resid_ref.shape
    wait_all(loads)
    result = (
        resid_ref[...]
        + own_ref[...]
        + near_ref[...].astype(f32)
        + far_ref[...].astype(f32)
    )
    out_ref[...] = result.astype(bf16)
    sent = [start_copy(out_ref, out_hbm, sems, 3)]
    qpos = info_ref[0] * rows + lax.broadcasted_iota(jnp.int32, (rows, 1), 0)
    error = jnp.where(qpos < info_ref[1], result - teacher_ref[...], 0.0)
    grad = error * scale_ref[0]
    grad_ref[...] = grad
    sent.append(start_copy(grad_ref, grad_hbm, sems, 4))
    ext_ref[:, :features] = grad.astype(bf16)
    lane = lanes_of(rows)
    row_loss = jnp.where(lane == 0, jnp.sum(error * error, axis=1, keepdims=True), 0.0)
    ext_ref[:, features:] = split_low(row_loss, lane, 16).astype(bf16)
    wait_all(sent)


def result_call(info, scale, resid, own, near, far, teacher):
    rows, features = resid.shape
    flat = (rows, features)
    return pl.pallas_call(
        result_kernel,
        out_shape=(
            hbm(flat, bf16),
            hbm(flat, f32),
            jax.ShapeDtypeStruct((rows, features + EXTRA), bf16),
        ),
        in_specs=[in_smem] * 2 + [anywhere] * 3 + [in_vmem] * 2,
        out_specs=(anywhere, anywhere, in_vmem),
        scratch_shapes=[pltpu.VMEM(flat, f32)] * 3
        + [pltpu.VMEM(flat, bf16), pltpu.VMEM(flat, f32), pltpu.SemaphoreType.DMA((5,))],
        compiler_params=limits(12),
        cost_estimate=cost(3.5),
        name="result_and_error",
    )(info, scale, in_hbm(resid), in_hbm(own), in_hbm(teacher), near, far)


def resid_back_kernel(info_ref, far_ref, gain_ref, *refs):
    sources, refs = refs[:11], refs[11:]
    (out_hbm, gz_ref, d_attn_ref, small_ref), refs = refs[:4], refs[4:]
    held, (out_ref, sum_ref, sems) = refs[:11], refs[11:]
    loads = [
        start_copy(source, target, sems, i)
        for i, (source, target) in enumerate(zip(sources, held, strict=True))
    ]
    own_ref, near_ref, grad_ref, resid_ref, ext_ref, gates_ref, router_ref, o0, o1, o2, o3 = held
    rows, features = resid_ref.shape
    slab = o0.shape[0]
    lane = lanes_of(rows)
    tail = slice(features, features + EXTRA)
    wait_all(loads[:7])
    d_gate = join_low(
        own_ref[:, tail] + near_ref[:, tail].astype(f32) + far_ref[:, tail].astype(f32), lane, 16
    )
    gates = gates_ref[...]
    d_logits = gates * (d_gate - jnp.sum(gates * d_gate, axis=1, keepdims=True))
    d_logits = d_logits.astype(bf16)
    body = slice(0, features)
    upstream = (
        own_ref[:, body]
        + near_ref[:, body].astype(f32)
        + far_ref[:, body].astype(f32)
        + mm(d_logits, router_ref[...])
    )
    resid = resid_ref[...]
    grad_norm, grad_gain = norm_backward(resid, rms_factor(resid), gain_ref[...], upstream)
    experts = small_ref.shape[0] - 8
    small_ref[:experts, :] = mm_tn(d_logits, ext_ref[:, body])[:experts]
    small_ref[experts:, :] = jnp.broadcast_to(grad_gain[None], (8, features))
    grad_resid = grad_ref[...] + grad_norm
    out_ref[...] = grad_resid
    sent = start_copy(out_ref, out_hbm, sems, len(sources))
    gz_ref[...] = grad_resid.astype(bf16)
    gz = [
        gz_ref[:, pl.ds(pl.multiple_of((info_ref[0] ^ i) * slab, 128), slab)] for i in range(4)
    ]
    wait_all(loads[7:])
    sum_ref[...] = mm(gz[0], o0[...]) + mm(gz[1], o1[...])
    here, other = out_halves(info_ref, o2.shape[1])
    sum_ref[:, here] += mm(gz[2], o2[:slab]) + mm(gz[3], o3[:slab])
    sum_ref[:, other] += mm(gz[2], o2[slab:]) + mm(gz[3], o3[slab:])
    d_attn_ref[...] = sum_ref[...].astype(bf16)
    sent.wait()


def resid_back_call(info, own, near, far, grad, resid, ext, gates, gain, router, output_parts, experts):
    rows, features = resid.shape
    sources = [own, near, grad, resid, ext, gates, router, *output_parts]
    heads_wide = output_parts[0].shape[1]
    return pl.pallas_call(
        resid_back_kernel,
        out_shape=(
            hbm((rows, features), f32),
            jax.ShapeDtypeStruct((rows, features), bf16),
            jax.ShapeDtypeStruct((rows, heads_wide), bf16),
            jax.ShapeDtypeStruct((experts + 8, features), f32),
        ),
        in_specs=[in_smem] + [in_vmem] * 2 + [anywhere] * len(sources),
        out_specs=(anywhere,) + (in_vmem,) * 3,
        scratch_shapes=[pltpu.VMEM(value.shape, value.dtype) for value in sources]
        + [
            pltpu.VMEM((rows, features), f32),
            pltpu.VMEM((rows, heads_wide), f32),
            pltpu.SemaphoreType.DMA((len(sources) + 1,)),
        ],
        compiler_params=limits(20),
        cost_estimate=cost(5),
        name="residual_backward",
    )(info, far, gain, *[in_hbm(value) for value in sources])


def gate_column(extra, lane, expert):
    here = (lane == expert) | (lane == expert + 16)
    return jnp.sum(jnp.where(here, extra, 0.0), axis=1, keepdims=True)


def shared_parts_of(shared_ref):
    width = shared_ref.shape[1] // 3
    return [shared_ref[:, i * width : (i + 1) * width] for i in range(3)]


def experts_kernel(info_ref, xa_ref, xb_ref, gate_ref, up_ref, down_ref, shared_ref,
                   outa_hbm, outb_ref, gp_out, upre_out, hid_out,
                   gp_ref, upre_ref, hid_ref, x_ref, acc_ref, sems):
    rows, features = outb_ref.shape
    here, _, width = gate_ref.shape
    x_ref[:rows] = xa_ref[:, :features]
    x_ref[rows:] = xb_ref[:, :features]
    extra = jnp.concatenate([xa_ref[:, features:], xb_ref[:, features:]], axis=0).astype(f32)
    lane = lanes_of(2 * rows)

    def unit(gate_w, up_w):
        gate_pre, up_pre = mm(x_ref[...], gate_w), mm(x_ref[...], up_w)
        return gate_pre, up_pre, gate_pre * jax.nn.sigmoid(gate_pre) * up_pre

    s_gate, s_up, s_down = shared_parts_of(shared_ref)
    gate_pre, up_pre, hidden = unit(s_gate, s_up)
    hidden = hidden.astype(bf16)
    acc_ref[...] = mm_nt(hidden, s_down)
    part = hidden.shape[1] // 2
    for half in range(2):
        cols, mine = slice(2 * width, 2 * width + part), slice(half * part, (half + 1) * part)
        gp_ref[half, :, cols] = gate_pre[:, mine].astype(bf16)
        upre_ref[half, :, cols] = up_pre[:, mine].astype(bf16)
        hid_ref[info_ref[1] ^ half, :, cols] = hidden[:, mine]
    sent = []
    for e in range(here):
        gate = gate_column(extra, lane, info_ref[0] * here + e)
        gate_pre, up_pre, hidden = unit(gate_ref[e], up_ref[e])
        hidden = (hidden * gate).astype(bf16)
        half, at = e // 2, (e % 2) * width
        cols = slice(at, at + width)
        gp_ref[half, :, cols] = gate_pre.astype(bf16)
        upre_ref[half, :, cols] = up_pre.astype(bf16)
        hid_ref[info_ref[1] ^ half, :, cols] = hidden
        if e % 2:
            sent.append(start_copy(gp_ref.at[half], gp_out.at[half], sems, 2 * half))
            sent.append(start_copy(upre_ref.at[half], upre_out.at[half], sems, 2 * half + 1))
        if e + 1 == here:
            sent.append(start_copy(hid_ref.at[0], hid_out, sems, 4))
        acc_ref[...] += mm_nt(hidden, down_ref[e])
    outb_ref[...] = acc_ref[rows:].astype(bf16)
    sent.append(start_copy(acc_ref.at[pl.ds(0, rows)], outa_hbm, sems, 5))
    wait_all(sent)


def experts_call(info, xa, xb, weights):
    rows, features = xa.shape[0], xa.shape[1] - EXTRA
    wide = 2 * weights[0].shape[2] + weights[3].shape[1] // 6
    both, half = hbm((2, 2 * rows, wide), bf16), hbm((2 * rows, wide), bf16)
    return pl.pallas_call(
        experts_kernel,
        out_shape=(
            hbm((rows, features), f32),
            jax.ShapeDtypeStruct((rows, features), bf16),
            both,
            both,
            half,
        ),
        in_specs=[in_smem] + [in_vmem] * 6,
        out_specs=(anywhere, in_vmem) + (anywhere,) * 3,
        scratch_shapes=[pltpu.VMEM(both.shape, bf16)] * 3
        + [
            pltpu.VMEM((2 * rows, features), bf16),
            pltpu.VMEM((2 * rows, features), f32),
            pltpu.SemaphoreType.DMA((6,)),
        ],
        compiler_params=limits(16),
        cost_estimate=cost(8),
        name="experts_forward",
    )(info, xa, xb, *weights)


def hidden_back(d_hidden, gate_pre, up_pre, gate):
    gate_pre, up_pre = gate_pre.astype(f32), up_pre.astype(f32)
    act, slope = silu_parts(gate_pre)
    d_gate = None
    if gate is not None:
        d_gate = jnp.sum(d_hidden * act * up_pre, axis=1, keepdims=True)
        d_hidden = d_hidden * gate
    return d_gate, (d_hidden * up_pre * slope).astype(bf16), (d_hidden * act).astype(bf16)


def experts_back_kernel(info_ref, *refs):
    shared_ref, weights_in, refs = refs[0], refs[1:4], refs[4:]
    g_in, e_in, (gpa_in, gpb_in, upa_in, upb_in), refs = refs[:4], refs[4:8], refs[8:12], refs[12:]
    (dxa_hbm, dxb_ref, dxc_ref, dxd_ref, dg_out, du_out), refs = refs[:6], refs[6:]
    held, refs = refs[:3], refs[3:]
    gate_ref, up_ref, down_ref = held
    gp_ref, upre_ref, dg_ref, du_ref, g_ref, extra_ref, dxa_ref, acc_ref, sems = refs
    rows = g_in[0].shape[0]
    features = g_ref.shape[1]
    here, _, width = gate_ref.shape
    x = info_ref[1]
    first, last = pl.ds(0, 2 * rows), pl.ds(2 * rows, 2 * rows)
    loads = load_rows(g_in, g_ref, None, sems, 0)
    weight_loads = [
        [start_copy(weights_in[i].at[e], held[i].at[e], sems, 19 + 3 * e + i) for i in (2, 0, 1)]
        for e in range(1)
    ]
    late = [
        start_copy(source, target, sems, 8 + i)
        for i, (source, target) in enumerate(
            [
                (gpa_in, gp_ref.at[:, first]),
                (gpb_in, gp_ref.at[:, last]),
                (upa_in, upre_ref.at[:, first]),
                (upb_in, upre_ref.at[:, last]),
            ]
        )
    ]
    for i in range(4):
        at = pl.ds(i * rows, rows)
        source = e_in[i].at[:, pl.ds(features, EXTRA)]
        late.append(start_copy(source, extra_ref.at[at], sems, 12 + i))
    weight_loads += [
        [start_copy(weights_in[i].at[e], held[i].at[e], sems, 19 + 3 * e + i) for i in (2, 0, 1)]
        for e in range(1, here)
    ]
    wait_all(loads)
    s_gate, s_up, s_down = shared_parts_of(shared_ref)
    spans = [slice(i * 2 * rows, (i + 1) * 2 * rows) for i in range(2)]
    d_hiddens = [mm(g_ref[span], s_down) for span in spans]
    wait_all(late)
    lane = lanes_of(2 * rows)
    extras = [extra_ref[span].astype(f32) for span in spans]
    d_gates = [jnp.zeros((2 * rows, EXTRA), f32)] * 2
    part = d_hiddens[0].shape[1] // 2
    cols = slice(2 * width, 2 * width + part)
    for i, span in enumerate(spans):
        total = None
        for half in range(2):
            at = slice(half * part, (half + 1) * part)
            _, d_gate_pre, d_up_pre = hidden_back(
                d_hiddens[i][:, at], gp_ref[half, span, cols], upre_ref[half, span, cols], None
            )
            dg_ref[x ^ half, span, cols] = d_gate_pre
            du_ref[x ^ half, span, cols] = d_up_pre
            term = mm_nt(d_gate_pre, s_gate[:, at]) + mm_nt(d_up_pre, s_up[:, at])
            total = term if total is None else total + term
        acc_ref[span] = total
    sent = []
    for e in range(here):
        expert = info_ref[0] * here + e
        half, at = e // 2, (e % 2) * width
        cols = slice(at, at + width)
        wait_all(weight_loads[e])
        for i, span in enumerate(spans):
            d_gate, d_gate_pre, d_up_pre = hidden_back(
                mm(g_ref[span], down_ref[e]),
                gp_ref[half, span, cols],
                upre_ref[half, span, cols],
                gate_column(extras[i], lane, expert),
            )
            dg_ref[x ^ half, span, cols] = d_gate_pre
            du_ref[x ^ half, span, cols] = d_up_pre
            d_gates[i] = jnp.where(lane == expert, d_gate, d_gates[i])
            acc_ref[span] += mm_nt(d_gate_pre, gate_ref[e]) + mm_nt(d_up_pre, up_ref[e])
        if e + 1 == here:
            sent = [
                start_copy(dg_ref.at[0], dg_out, sems, 16),
                start_copy(du_ref.at[0], du_out, sems, 17),
            ]
    for i, ref in enumerate((dxa_ref, dxb_ref, dxc_ref, dxd_ref)):
        at = slice(i * rows, (i + 1) * rows)
        own = slice(i % 2 * rows, (i % 2 + 1) * rows)
        extra = split_low(d_gates[i // 2], lane, 16)[own]
        ref[:, :features] = acc_ref[at].astype(ref.dtype)
        ref[:, features:] = extra.astype(ref.dtype)
    sent.append(start_copy(dxa_ref, dxa_hbm, sems, 18))
    wait_all(sent)


def experts_back_call(info, grads, exts, kept, weights):
    rows, features = grads[0].shape[0], grads[0].shape[1] - EXTRA
    _, held, wide = kept[0].shape
    ext = grads[0].shape
    return pl.pallas_call(
        experts_back_kernel,
        out_shape=(
            hbm(ext, f32),
            jax.ShapeDtypeStruct(ext, bf16),
            jax.ShapeDtypeStruct(ext, f32),
            jax.ShapeDtypeStruct(ext, bf16),
        )
        + (hbm((2 * held, wide), bf16),) * 2,
        in_specs=[in_smem, in_vmem] + [anywhere] * 15,
        out_specs=(anywhere,) + (in_vmem,) * 3 + (anywhere,) * 2,
        scratch_shapes=[pltpu.VMEM(weights[0].shape, bf16)] * 3
        + [pltpu.VMEM((2, 2 * held, wide), bf16)] * 4
        + [
            pltpu.VMEM((4 * rows, features), bf16),
            pltpu.VMEM((4 * rows, EXTRA), bf16),
            pltpu.VMEM(ext, f32),
            pltpu.VMEM((4 * rows, features), f32),
            pltpu.SemaphoreType.DMA((19 + 3 * weights[0].shape[0],)),
        ],
        compiler_params=limits(46),
        cost_estimate=cost(24),
        name="experts_backward",
    )(info, weights[3], *[in_hbm(value) for value in (*weights[:3], *grads, *exts, *kept)])


def pair_shared(info_ref, shared_ref, which):
    width = shared_ref.shape[1] // 3
    first = which * width + info_ref[1] * (width // 2)
    return shared_ref[:, pl.ds(pl.multiple_of(first, 128), width // 2)]


def pair_kernel(info_ref, shared_ref, gate_in, up_in, x0, x1, x2, x3, gp_out, upre_out, hid_out,
                gate_ref, up_ref, gp_ref, upre_ref, hid_ref, x_ref, extra_ref, sems):
    here, _, width = gate_in.shape
    count = here // 2
    loads = load_rows((x0, x1, x2, x3), x_ref, extra_ref, sems, 3)
    weight_loads = [
        [
            start_copy(source.at[info_ref[1] * count + j], target.at[j], sems, 11 + 2 * j + i)
            for i, (source, target) in enumerate([(gate_in, gate_ref), (up_in, up_ref)])
        ]
        for j in range(count)
    ]
    wait_all(loads)
    extra = extra_ref[...].astype(f32)
    lane = lanes_of(extra.shape[0])
    for j in range(count + 1):
        if j < count:
            wait_all(weight_loads[j])
            gate_w, up_w = gate_ref[j], up_ref[j]
        else:
            gate_w, up_w = (pair_shared(info_ref, shared_ref, i) for i in range(2))
        gate_pre, up_pre = mm(x_ref[...], gate_w), mm(x_ref[...], up_w)
        hidden = gate_pre * jax.nn.sigmoid(gate_pre) * up_pre
        if j < count:
            expert = info_ref[0] * here + info_ref[1] * count + j
            hidden = hidden * gate_column(extra, lane, expert)
        cols = slice(j * width, j * width + gate_pre.shape[1])
        gp_ref[:, cols] = gate_pre.astype(bf16)
        upre_ref[:, cols] = up_pre.astype(bf16)
        hid_ref[:, cols] = hidden.astype(bf16)
    wait_all(
        [
            start_copy(source, target, sems, i)
            for i, (source, target) in enumerate(
                [(hid_ref, hid_out), (gp_ref, gp_out), (upre_ref, upre_out)]
            )
        ]
    )


def pair_call(info, exts, weights):
    rows, features = 4 * exts[0].shape[0], exts[0].shape[1] - EXTRA
    e_gate, e_up, _, shared = weights
    wide = (rows, e_gate.shape[0] // 2 * e_gate.shape[2] + shared.shape[1] // 6)
    return pl.pallas_call(
        pair_kernel,
        out_shape=(hbm(wide, bf16),) * 3,
        in_specs=[in_smem, in_vmem] + [anywhere] * 6,
        out_specs=(anywhere,) * 3,
        scratch_shapes=[pltpu.VMEM((e_gate.shape[0] // 2,) + e_gate.shape[1:], bf16)] * 2
        + [pltpu.VMEM(wide, bf16)] * 3
        + [
            pltpu.VMEM((rows, features), bf16),
            pltpu.VMEM((rows, EXTRA), bf16),
            pltpu.SemaphoreType.DMA((11 + e_gate.shape[0],)),
        ],
        compiler_params=limits(24),
        cost_estimate=cost(8),
        name="pair_forward",
    )(info, shared, *[in_hbm(value) for value in (e_gate, e_up, *exts)])


def pair_back_kernel(info_ref, shared_ref, down_in, g0, g1, g2, g3, e0, e1, e2, e3, gp_in, upre_in,
                     dg_out, du_out, down_ref, gp_ref, upre_ref, dg_ref, du_ref, g_ref, extra_ref, sems):
    rows, features = g0.shape[0], g_ref.shape[1]
    here, _, width = down_in.shape
    count = here // 2
    loads = load_rows((g0, g1, g2, g3), g_ref, None, sems, 4)
    weight_loads = [
        start_copy(down_in.at[info_ref[1] * count + j], down_ref.at[j], sems, 16 + j)
        for j in range(count)
    ]
    loads += [start_copy(gp_in, gp_ref, sems, 0), start_copy(upre_in, upre_ref, sems, 1)]
    for i, source in enumerate((e0, e1, e2, e3)):
        lanes = source.at[:, pl.ds(features, EXTRA)]
        loads.append(start_copy(lanes, extra_ref.at[pl.ds(i * rows, rows)], sems, 12 + i))
    wait_all(loads)
    extra = extra_ref[...].astype(f32)
    lane = lanes_of(4 * rows)
    for j in range(count + 1):
        gate = None
        if j < count:
            weight_loads[j].wait()
            weight = down_ref[j]
            gate = gate_column(extra, lane, info_ref[0] * here + info_ref[1] * count + j)
        else:
            weight = pair_shared(info_ref, shared_ref, 2)
        cols = slice(j * width, j * width + weight.shape[1])
        _, d_gate_pre, d_up_pre = hidden_back(
            mm(g_ref[...], weight), gp_ref[:, cols], upre_ref[:, cols], gate
        )
        dg_ref[:, cols] = d_gate_pre
        du_ref[:, cols] = d_up_pre
    wait_all([start_copy(dg_ref, dg_out, sems, 2), start_copy(du_ref, du_out, sems, 3)])


def pair_back_call(info, grads, exts, gate_pre, up_pre, weights):
    rows, features = 4 * exts[0].shape[0], exts[0].shape[1] - EXTRA
    wide = gate_pre.shape
    return pl.pallas_call(
        pair_back_kernel,
        out_shape=(hbm(wide, bf16),) * 2,
        in_specs=[in_smem, in_vmem] + [anywhere] * 11,
        out_specs=(anywhere,) * 2,
        scratch_shapes=[pltpu.VMEM((weights[2].shape[0] // 2,) + weights[2].shape[1:], bf16)]
        + [pltpu.VMEM(wide, bf16)] * 4
        + [
            pltpu.VMEM((rows, features), bf16),
            pltpu.VMEM((rows, EXTRA), bf16),
            pltpu.SemaphoreType.DMA((16 + weights[2].shape[0] // 2,)),
        ],
        compiler_params=limits(20),
        cost_estimate=cost(7),
        name="pair_backward",
    )(
        info,
        weights[3],
        *[in_hbm(value) for value in (weights[2], *grads, *exts, gate_pre, up_pre)],
    )


def weight_grad_kernel(*refs):
    lefts, rights, (out_ref, left_ref, right_ref, tiles_ref, sems) = refs[:8], refs[8:-5], refs[-5:]
    count, rows, tile = left_ref.shape
    slots, _, wide = tiles_ref.shape
    loads, at = [], 0
    for i, ref in enumerate(rights):
        target = right_ref.at[pl.ds(at, ref.shape[0])]
        loads.append(start_copy(ref, target, sems, slots + i))
        at += ref.shape[0]
    columns = []
    for t in range(count):
        at, first = 0, slots + len(rights) + t * len(lefts)
        columns.append([])
        for i, ref in enumerate(lefts):
            source = ref.at[:, pl.ds(t * tile, tile)]
            target = left_ref.at[t, pl.ds(at, ref.shape[0])]
            columns[t].append(start_copy(source, target, sems, first + i))
            at += ref.shape[0]
    wait_all(loads)
    sent = []
    for group in range(right_ref.shape[0] // rows):
        right = slice(group * rows, (group + 1) * rows)
        for t in range(count):
            if group == 0:
                wait_all(columns[t])
            index = group * count + t
            slot = index % slots
            if index >= slots:
                sent[index - slots].wait()
            tiles_ref[slot] = mm_tn(left_ref[t], right_ref[right]).astype(bf16)
            target = out_ref.at[pl.ds(t * tile, tile), pl.ds(group * wide, wide)]
            sent.append(start_copy(tiles_ref.at[slot], target, sems, slot))
    wait_all(sent[-slots:])


def weight_grad_call(lefts, rights):
    rows = sum(value.shape[0] for value in lefts)
    features, wide = lefts[0].shape[1] - EXTRA, rights[0].shape[1]
    held = sum(value.shape[0] for value in rights)
    operands = [in_hbm(value) for value in (*lefts, *rights)]
    return pl.pallas_call(
        weight_grad_kernel,
        out_shape=hbm((features, held // rows * wide), bf16),
        in_specs=[anywhere] * len(operands),
        out_specs=anywhere,
        scratch_shapes=[
            pltpu.VMEM((features // 256, rows, 256), bf16),
            pltpu.VMEM((held, wide), bf16),
            pltpu.VMEM((3, 256, wide), bf16),
            pltpu.SemaphoreType.DMA((3 + len(rights) + features // 256 * len(lefts),)),
        ],
        compiler_params=limits(16),
        cost_estimate=cost(8 * held // rows),
        name="weight_gradients",
    )(*operands)


def exchange_wa(pick):
    return [pick(0)] + [swap(pick(i), "wa", i) for i in (1, 2, 3)]


def after(values, *done):
    kept = lax.optimization_barrier((values, done))
    return kept[0]


def key_blocks(kv, n):
    levels = [kv]
    for s in range(1, n // 2):
        levels.append(lax.ppermute(kv, "ctx", [(i, i + 2 * s) for i in range(n - 2 * s)]))
    blocks = []
    for level in levels:
        blocks += [level, swap(level, "ctx", 1)]
    return blocks


def sum_key_blocks(own, moved, n, beside):
    m, rows = n // 2, own[0].shape[0]
    got = [both[i : i + rows] for both in moved for i in range(0, both.shape[0], rows)]
    total, beside = None, list(beside)
    for s in reversed(range(m)):
        level = own[s].astype(f32) + got[s].astype(f32)
        if s:
            level = lax.ppermute(
                level.astype(bf16), "ctx", [(i + 2 * s, i) for i in range(n - 2 * s)]
            )
            if beside:
                level = after(level, beside.pop(0))
            level = level.astype(f32)
        total = level if total is None else total + level
    return total.astype(bf16)


def sum_pairs(value, n):
    groups = [[2 * i + x for i in range(n // 2)] for x in range(2)]
    return lax.psum_scatter(
        value, "ctx", scatter_dimension=0, tiled=True, axis_index_groups=groups
    )


def per_device(
    tokens,
    teacher,
    lengths,
    routes,
    query_weight,
    key_projection_matrix,
    value_projection_matrix,
    output_weight,
    attn_gain,
    moe_gain,
    router_weight,
    shared_gate,
    shared_up,
    shared_down,
    expert_gate,
    expert_up,
    expert_down,
):
    w = lax.axis_index("wa")
    c = lax.axis_index("ctx")
    n = lax.axis_size("ctx")
    groups = lax.axis_size("wa")
    x, z, m = c % 2, c // 2, n // 2
    own_tokens = tokens[0]
    rows, features = own_tokens.shape
    slab = features // groups
    experts_all = router_weight.shape[1]
    length = jnp.sum(jnp.where(jnp.arange(lengths.shape[0]) == w, lengths, 0))
    count = jnp.sum(lengths).astype(f32)
    qpos = c * rows + jnp.arange(rows)
    width = KEY_VALUE_HEADS * HEAD_SIZE
    z_low = z % 2
    w_info = jnp.stack([w, x, z_low]).astype(jnp.int32)

    def columns(value, index):
        return lax.dynamic_slice_in_dim(value, index * slab, slab, 1)

    input_rows = own_tokens.astype(f32)
    factor_a = rms_factor(input_rows)
    far_half = lax.dynamic_slice_in_dim(own_tokens, (1 - w // 2) * 2 * slab, 2 * slab, 1)
    far_tokens = swap(far_half, "wa", 2)
    far_factor = swap(factor_a, "wa", 2)
    small = jnp.concatenate([router_weight.T, attn_gain[None], moe_gain[None]], axis=0)
    near_small = swap(small, "wa", 1)
    far_small = swap(small, "wa", 2)
    own_weights = (key_projection_matrix, value_projection_matrix, query_weight)
    near_weights = tuple(swap(value, "wa", 1) for value in own_weights)

    gain_own = small[-2:-1].astype(f32)
    gain_near = near_small[-2:-1].astype(f32)
    core = w % 2

    def far_columns(index):
        return lax.dynamic_slice_in_dim(far_tokens, index * slab, slab, 1)

    part_own = jnp.concatenate([columns(own_tokens, w), far_columns(core)], axis=0)
    part_near = jnp.concatenate([columns(own_tokens, w ^ 1), far_columns(1 - core)], axis=0)
    both_factor = jnp.concatenate([factor_a, far_factor], axis=0)
    normed_own = (part_own.astype(f32) * both_factor * gain_own).astype(bf16)
    normed_near = (part_near.astype(f32) * both_factor * gain_near).astype(bf16)

    def project(i):
        return mm(normed_own, own_weights[i]) + mm(normed_near, near_weights[i])

    kv_terms = jnp.concatenate([project(0), project(1)], axis=1)
    kv_got = swap(after(kv_terms[rows:].astype(bf16), far_small), "wa", 2)
    kv = (kv_terms[:rows] + kv_got.astype(f32)).astype(bf16)
    q_terms = project(2)

    half_out = output_weight.shape[1] // 2
    half_weight = lax.dynamic_slice_in_dim(output_weight, z_low * half_out, half_out, 1)
    q_got = swap(after(q_terms[rows:].astype(bf16), kv_got), "wa", 2)
    query_rows = (q_terms[:rows] + q_got.astype(f32)).astype(bf16)
    far_out = swap(after(half_weight, kv_got), "wa", 2)
    if n > 8:
        first_keys, all_keys = [], []
    else:
        kv_all = key_blocks(kv, n)
        first_keys, all_keys = [kv_all[1]] + kv_all[2::2], kv_all[1:]

    shared_width = shared_gate.shape[1] // groups

    shared_weights = after((shared_gate, shared_up, shared_down), kv_got)

    def shared_chunk(i):
        return jnp.concatenate(
            [
                lax.dynamic_slice_in_dim(value, (w ^ i) * shared_width, shared_width, 1)
                for value in shared_weights
            ],
            axis=1,
        )

    shared_far = swap(
        after(jnp.concatenate([shared_chunk(2), shared_chunk(3)]), far_out, q_got, *first_keys), "wa", 2
    )
    far_pair = jnp.concatenate([far_out, swap(far_out, "ctx", 2)])
    output_parts = [
        output_weight,
        swap(output_weight, "wa", 1),
        far_pair,
        swap(after(far_pair, *all_keys), "wa", 1),
    ]
    smalls = jnp.concatenate(
        perm4([small, near_small, far_small, swap(far_small, "wa", 1)], w), axis=1
    )
    router_t = jnp.pad(smalls[:experts_all], ((0, EXTRA - experts_all), (0, 0)))
    gain_a, gain_b = smalls[-2:-1].astype(f32), smalls[-1:].astype(f32)

    if n > 8:
        kv_all, pos = gather_keys(kv, c, n)
        q = heads(query_rows, GROUP)
        attn, kept_attn = attention_forward(q, kv_all, pos, qpos, length)
        attn = attn.reshape(rows, -1)
        attn_out = attn.astype(bf16)
    else:
        first = [c, length]
        for s in range(m):
            first += [(c - 2 * s) * rows, (c - 2 * s + 1 - 2 * x) * rows]
        attn_out, attn, kept_attn = attention_call(
            jnp.stack(first).astype(jnp.int32), query_rows, kv_all
        )
    resid, row_ext, gates = branch_call(
        w_info, attn_out, output_parts, own_tokens, gain_b, router_t, routes[0]
    )
    shared_parts = [
        shared_chunk(0),
        swap(shared_chunk(1), "wa", 1),
        shared_far[:slab],
        swap(after(shared_far[slab:], attn_out), "wa", 1),
    ]
    shared_mine = jnp.concatenate(perm4(shared_parts, w))
    weights = (expert_gate, expert_up, expert_down, shared_mine)

    row_parts = [row_ext, swap(row_ext, "wa", 1), swap(row_ext, "wa", 2)]
    rows_own = swap(row_ext, "ctx", 1)
    done = [experts_call(w_info, row_parts[0], row_parts[1], weights)]
    row_parts[2] = after(row_parts[2], done[0][1], rows_own)
    row_parts.append(swap(row_parts[2], "wa", 1))
    rows_far = swap(row_parts[2], "ctx", 1)
    rows_pair = row_parts + [rows_own, swap(rows_own, "wa", 1), rows_far, swap(rows_far, "wa", 1)]
    done.append(experts_call(w_info, row_parts[2], row_parts[3], weights))

    def sum_wa(own, near, far, far_near):
        far = far + swap(far_near, "wa", 1).astype(f32)
        return own, swap(near, "wa", 1), far.astype(bf16)

    own_out, near_out, far_out = sum_wa(done[0][0], done[0][1], done[1][0], done[1][1])
    far_out = after(swap(far_out, "wa", 2), rows_far)
    gate_pre_pair, up_pre_pair, hidden_pair = pair_call(w_info, rows_pair[4:], weights)
    scale = lengths.shape[0] * n * rows / count
    block_out, grad_result, grad_ext = result_call(
        jnp.stack([c, length]).astype(jnp.int32), scale[None], resid, own_out, near_out, far_out, teacher[0]
    )
    grad_parts = [grad_ext, swap(grad_ext, "wa", 1), swap(grad_ext, "wa", 2)]
    pair_own = swap(grad_ext, "ctx", 1)

    grad_parts[2], pair_own = after((grad_parts[2], pair_own), hidden_pair)
    grad_parts.append(swap(grad_parts[2], "wa", 1))
    pair_far = swap(grad_parts[2], "ctx", 1)
    grads_pair = grad_parts + [pair_own, swap(pair_own, "wa", 1), pair_far, swap(pair_far, "wa", 1)]
    down_terms = weight_grad_call(grads_pair, [done[0][4], done[1][4], hidden_pair])
    down_sum = sum_pairs(down_terms, n)

    kept = (done[0][2], done[1][2], done[0][3], done[1][3])
    first_grad = after(grad_parts[0], down_terms)
    back = experts_back_call(w_info, [first_grad] + grad_parts[1:], row_parts, kept, weights)
    own_back, near_back, far_back = sum_wa(*back[:4])
    grads_pair[4] = after(grads_pair[4], far_back)
    far_back = swap(far_back, "wa", 2)
    gate_pair, up_pair = pair_back_call(
        w_info, grads_pair[4:], rows_pair[4:], gate_pre_pair, up_pre_pair, weights
    )
    gate_pair = after(gate_pair, far_back)
    pre_terms = weight_grad_call(rows_pair, [back[4], gate_pair, back[5], up_pair])
    far_back = after(far_back, pre_terms)
    grad_resid, gz, d_attn, small_b = resid_back_call(
        w_info, own_back, near_back, far_back, grad_result, resid, row_ext, gates, gain_b,
        router_t, output_parts, experts_all,
    )

    fine_rows = features // n

    def whole_rows(summed):
        ours = lax.dynamic_slice_in_dim(summed, x * fine_rows, fine_rows, 0)
        got = swap(lax.dynamic_slice_in_dim(summed, (1 - x) * fine_rows, fine_rows, 0), "ctx", 1)
        return jnp.where(x == 0, ours, got), jnp.where(x == 0, got, ours)

    fine = features // n // groups

    def fine_exchange(value):
        blocks = jnp.transpose(value.reshape(-1, n, groups, fine), (2, 0, 1, 3))
        blocks = blocks.reshape(groups, -1, slab)
        return exchange_wa(lambda i: lax.dynamic_index_in_dim(blocks, w ^ i, 0, keepdims=False))

    attn_in = (input_rows * factor_a * gain_a).astype(bf16)
    attn_in_fine = jnp.concatenate(fine_exchange(attn_in))
    gz_fine = jnp.concatenate(fine_exchange(gz))

    def fold_rows(value):
        blocks = value.astype(bf16).reshape(m, 2, fine, value.shape[1])
        mine = lax.dynamic_index_in_dim(blocks, x, 1, keepdims=False)
        got = swap(lax.dynamic_index_in_dim(blocks, 1 - x, 1, keepdims=False), "ctx", 1)
        summed = (mine.astype(f32) + got.astype(f32)).astype(bf16)
        return summed.reshape(m * fine, -1)


    if n > 8:
        d_heads = heads(d_attn, GROUP)
        delta = jnp.sum(d_heads.astype(f32) * heads(attn, GROUP), axis=-1)
        delta = jnp.transpose(delta, (1, 2, 0))[..., None]
        d_q, d_kv = attention_backward(q, kv_all, pos, qpos, length, kept_attn, d_heads, delta)
        d_q = d_q.reshape(rows, -1).astype(bf16)
        d_kv, moved = scatter_keys(d_kv, n).astype(bf16), []
    else:
        d_q, d_own, d_pair = attention_back_call(d_attn, query_rows, attn, kept_attn, kv_all)
        moved = [swap(jnp.concatenate(d_pair[at : at + 2]), "ctx", 1) for at in range(0, m, 2)]
    attn_parts = gather_wa(after(attn_out, d_q))
    grad_output = fold_rows(mm_tn(gz_fine, jnp.concatenate(attn_parts)))
    d_q_parts = gather_wa(after(d_q, *moved))
    grad_query = fold_rows(mm_tn(attn_in_fine, jnp.concatenate(d_q_parts)))
    down_halves = whole_rows(after(down_sum, d_q))
    if n <= 8:
        d_kv = sum_key_blocks(d_own, moved, n, (grad_output, grad_query, down_halves[0]))
    pre_sum = sum_pairs(after(pre_terms, down_sum, d_q), n)
    d_kv_parts = gather_wa(d_kv)

    both_d_q = jnp.concatenate([d_q, d_q_parts[2]])
    both_d_kv = jnp.concatenate([d_kv, d_kv_parts[2]])

    def back_through(weights):
        both = (both_d_kv[:, :width], both_d_kv[:, width:], both_d_q)
        return sum(mm_nt(value, weight) for value, weight in zip(both, weights, strict=True))

    back_own, back_near = back_through(own_weights), back_through(near_weights)
    returned = swap(
        jnp.concatenate([back_own[rows:], back_near[rows:]], axis=1).astype(bf16), "wa", 2
    ).astype(f32)
    grad_attn_in = jnp.concatenate(
        perm4([back_own[:rows], back_near[:rows], returned[:, :slab], returned[:, slab:]], w),
        axis=1,
    )
    grad_norm_a, grad_gain_a = norm_backward(input_rows, factor_a, gain_a, grad_attn_in)
    grad_tokens = grad_resid + grad_norm_a

    grad_kv = fold_rows(mm_tn(attn_in_fine, jnp.concatenate(d_kv_parts)))
    dense_terms = jnp.concatenate([grad_output, grad_query, grad_kv], axis=1)

    loss_part = jnp.sum(grad_ext[:, features:].astype(f32))
    smalls_grad = jnp.concatenate(
        [small_b[: experts_all + 1], grad_gain_a[None], jnp.full((1, features), loss_part)], axis=0
    )
    parts = fine_exchange(smalls_grad)
    small_sum = (parts[0] + parts[1] + parts[2] + parts[3]).reshape(-1, n, fine)
    small_sum = after(jnp.transpose(small_sum, (1, 0, 2)), dense_terms)
    if m == 4:
        blocks = small_sum.reshape((m, 2) + small_sum.shape[1:])
        got = swap(lax.dynamic_index_in_dim(blocks, 1 - x, 1, keepdims=False), "ctx", 1)
        blocks = lax.dynamic_index_in_dim(blocks, x, 1, keepdims=False) + got
        parts = [lax.dynamic_index_in_dim(blocks, z ^ i, 0, keepdims=False) for i in range(m)]
        small_sum = parts[0] + sum(swap(parts[i], "ctx", 2 * i) for i in range(1, m))
    else:
        small_sum = lax.all_to_all(small_sum, "ctx", split_axis=0, concat_axis=0, tiled=True)
        small_sum = jnp.sum(small_sum, axis=0)
    loss = small_sum[-1, 0] / (2.0 * features * count)
    dense = sum_pairs(after(dense_terms, pre_sum, small_sum), n).astype(f32)
    pieces, at = [], 0
    for size in (output_weight.shape[1], query_weight.shape[1], width, width):
        pieces.append(dense[:, at : at + size])
        at += size

    units = expert_gate.shape[2]
    used = expert_gate.shape[0] // 2 * units

    def experts_of(first, second, at):
        return jnp.stack(
            [
                value[:, at + e * units : at + (e + 1) * units].astype(f32)
                for value in (first, second)
                for e in range(expert_gate.shape[0] // 2)
            ]
        )

    wide = down_sum.shape[1]
    pre_halves = whole_rows(after(pre_sum, dense_terms))
    grad_expert_down = experts_of(*down_halves, 0)
    grad_expert_gate = experts_of(*pre_halves, 0)
    grad_expert_up = experts_of(*pre_halves, wide)
    shared = jnp.concatenate(
        [value[:, used:] for value in down_halves]
        + [value[:, used:wide] for value in pre_halves]
        + [value[:, wide + used :] for value in pre_halves],
        axis=1,
    )

    def shared_rows(i):
        return lax.dynamic_slice_in_dim(shared, (w ^ i) * fine, fine, 0)

    shared = jnp.stack(perm4(exchange_wa(shared_rows), w)).astype(f32)
    shared = shared.reshape(groups, fine, 3, shared_width)
    grad_shared_down, grad_shared_gate, grad_shared_up = (
        jnp.transpose(shared[:, :, i], (1, 0, 2)).reshape(fine, -1) for i in range(3)
    )

    return (
        block_out[None],
        grad_tokens[None],
        pieces[1],
        pieces[2],
        pieces[3],
        pieces[0],
        small_sum[experts_all + 1],
        small_sum[experts_all],
        small_sum[:experts_all].T,
        grad_shared_gate,
        grad_shared_up,
        grad_shared_down,
        grad_expert_gate,
        grad_expert_up,
        grad_expert_down,
        loss,
    )


def solution(mesh):
    return jax.shard_map(
        per_device,
        mesh=mesh,
        in_specs=(
            P("wa", "ctx", None),
            P("wa", "ctx", None),
            P(),
            P("wa", "ctx", None),
            P("wa", None),
            P("wa", None),
            P("wa", None),
            P("wa", None),
            P("wa"),
            P("wa"),
            P("wa", None),
            P("wa", None),
            P("wa", None),
            P("wa", None),
            P("wa", None, None),
            P("wa", None, None),
            P("wa", None, None),
        ),
        out_specs=(
            P("wa", "ctx", None),
            P("wa", "ctx", None),
            P(("ctx", "wa"), None),
            P(("ctx", "wa"), None),
            P(("ctx", "wa"), None),
            P(("ctx", "wa"), None),
            P(("ctx", "wa")),
            P(("ctx", "wa")),
            P(("ctx", "wa"), None),
            P(("ctx", "wa"), None),
            P(("ctx", "wa"), None),
            P(("ctx", "wa"), None),
            P("wa", "ctx", None),
            P("wa", "ctx", None),
            P("wa", "ctx", None),
            P(),
        ),
        check_vma=False,
    )
```
